32 devices in a mesh: chan: 16 (over z, y, x), rad: 2 (over core).
Axes of the slice: x: 2, y: 2, z: 4, core: 2. Of those that a mesh axis runs over, the one named last changes fastest.
Arguments:
- trial_block: float32 [1024, 16, 128], P('chan', None, 'rad')
- ham_blocks: bfloat16 [1024, 8, 128, 128], P('chan', None, 'rad'), may hold values from -0.1875 to 0.1875
- partners: int32 [1024, 8], P('chan'), may hold values from 0 to 1023, as said below
- stored_at: int32 [1024], replicated, may hold values from 0 to 1023, as said below
- precond_diag: float32 [1024, 128], P('chan', 'rad'), may hold values from 1 to 10
Outputs:
- new_block: float32 [1024, 16, 128], P('chan', None, 'rad')
- ritz_values: float32 [16], replicated
The draws below stay inside these ranges and needn't reach their ends.
Inputs may be any that keep to these rules, and one draw needn't show every extreme that they name: `stored_at`: A permutation of the channel numbers. `partners`: among the 512 entries of the rows p with p // 64 = d, for every d, at most 64 have stored_at[partner] // 64 equal to any one value; for every d some value has exactly 64.
All inputs are finite; a program needn't handle non-finite values.
Results may differ from the reference program's by a relative error of at most 0.0051.
Values may be sent and summed in bfloat16 or wider, within the bound.
No kernel may reach another device: no remote copies, remote signals or barrier semaphores. Data moves between devices by JAX's collectives and lax.ppermute only.
A program may use at most 64 MiB of HBM per device.

```python
import math
import jax
import jax.numpy as jnp
from jax import lax

NCH = 1024
NB = 128
K = 16
NCOUP = 8
CH_DEV = 64
CAP = 64
N_CHAN = 16


def stored_perm(key):
    return jax.random.permutation(jax.random.fold_in(key, 11), NCH).astype(jnp.int32)


def draw_stored_at(key, part):
    return stored_perm(key)


def draw_partners(key, part):
    perm = stored_perm(key)
    inverse = jnp.argsort(perm, stable=True).astype(jnp.int32)
    requests = CH_DEV * NCOUP
    slots = N_CHAN * CAP
    slot_owner = jnp.arange(slots, dtype=jnp.int32) // CAP
    popular = jax.random.randint(jax.random.fold_in(key, 16), (N_CHAN,), 0, 4)
    priority = jax.random.randint(jax.random.fold_in(key, 12), (N_CHAN, slots), 0, 2 ** 27)
    priority = priority + (3 - popular[slot_owner])[None, :] * 2 ** 27
    forced = jax.random.randint(jax.random.fold_in(key, 13), (N_CHAN,), 0, N_CHAN)
    priority = jnp.where(slot_owner[None, :] == forced[:, None], -1, priority)
    chosen = jnp.argsort(priority, axis=1, stable=True)[:, :requests].astype(jnp.int32)
    shuffle_keys = jax.random.randint(jax.random.fold_in(key, 14), (N_CHAN, requests), 0, 2 ** 30)
    shuffle = jnp.argsort(shuffle_keys, axis=1, stable=True)
    chosen = jnp.take_along_axis(chosen, shuffle, axis=1)
    owner_dev = chosen // CAP
    local_row = jax.random.randint(jax.random.fold_in(key, 15), (N_CHAN, requests), 0, CH_DEV)
    channel = inverse[owner_dev * CH_DEV + local_row]
    return channel.reshape(NCH, NCOUP).astype(jnp.int32)


def draw_trial_block(key, part):
    position = jnp.arange(NCH, dtype=jnp.float32) / jnp.float32(NCH - 1)
    ramp = (3.0 ** (0.5 * position))[:, None, None]
    columns = jnp.exp(jax.random.uniform(jax.random.fold_in(key, 3), (1, K, 1), jnp.float32, 0.0, math.log(10.0)))
    rough = jnp.exp(jax.random.uniform(jax.random.fold_in(key, 2), (NCH, 1, NB), jnp.float32, 0.0, math.log(3.2)))
    base = jax.random.normal(jax.random.fold_in(key, 1), (NCH, K, NB), jnp.float32)
    return (base * ramp * rough * columns).astype(jnp.float32)


def levels(rng, shape, split, smallest, high):
    def one(axis_at, blocks):
        steps = jax.random.uniform(jax.random.fold_in(jax.random.fold_in(rng, 6), axis_at), (blocks,), jnp.float32, smallest / len(split), high / len(split))
        return jnp.repeat(jnp.exp(steps), shape[axis_at] // blocks).reshape((-1,) + (1,) * (len(shape) - axis_at - 1))

    loudness = one(*split[0])
    for cut in split[1:]:
        loudness = loudness * one(*cut)
    return loudness


def scatter_about(rng, shape, spread, limit, split=(), kind=jnp.bfloat16):
    values = spread * jax.random.normal(rng, shape, jnp.float32)
    if split:
        values = values * levels(rng, shape, split, -0.22, 0.18)
    return jnp.clip(values, -limit, limit).astype(kind)


def setup_inputs(seed: int = 0) -> dict:
    key_list = jax.random.split(jax.random.key(seed), 6)
    return {
        "trial_block": draw_trial_block(jax.random.fold_in(key_list[5], 71), 0),
        "ham_blocks": scatter_about(key_list[1], (NCH, NCOUP, NB, NB), (NCOUP * NB) ** -0.5, 0.1875, ((0, 16), (2, 2))),
        "partners": draw_partners(jax.random.fold_in(key_list[5], 71), 0),
        "stored_at": draw_stored_at(jax.random.fold_in(key_list[5], 71), 0),
        "precond_diag": jnp.clip(jnp.exp(math.log(10.0) - 2.3025851 * jax.random.uniform(key_list[4], (NCH, NB), jnp.float32) ** levels(key_list[4], (NCH, NB), ((0, 16), (1, 2)), -0.2, 0.2)), 1.0, 10.0),
    }


def chol_solve(factor, rhs):
    first = lax.linalg.triangular_solve(factor, rhs, left_side=True, lower=True)
    return lax.linalg.triangular_solve(factor, first, left_side=True, lower=True, transpose_a=True)

def inner_products(left, right):
    return jnp.einsum('pkr,plr->kl', left, right, precision=lax.Precision.HIGHEST)

def reference(trial_block, ham_blocks, partners, stored_at, precond_diag):
    rounded = trial_block.astype(jnp.bfloat16)
    rows_used = stored_at[partners].astype(jnp.int32)
    coupled = rounded[rows_used]
    applied = jnp.einsum('cjks,cjrs->ckr', coupled.astype(jnp.float32), ham_blocks.astype(jnp.float32), precision=lax.Precision.HIGHEST)
    proj_a = inner_products(trial_block, applied)
    proj_b = inner_products(trial_block, trial_block)
    factor = jnp.linalg.cholesky(proj_b)
    coefficients = chol_solve(factor, proj_a)
    ritz_values = jnp.diagonal(coefficients)
    residual = applied - jnp.einsum('pkr,kl->plr', trial_block, coefficients, precision=lax.Precision.HIGHEST)
    correction = residual / precond_diag[:, None, :]
    correlation = inner_products(trial_block, correction)
    mixing = chol_solve(factor, correlation)
    projected = correction - jnp.einsum('pkr,kl->plr', trial_block, mixing, precision=lax.Precision.HIGHEST)
    correlation_gram = inner_products(projected, projected) / jnp.float32(NCH * NB)
    gram_factor = jnp.linalg.cholesky(correlation_gram)
    flat_rows = jnp.transpose(projected, (1, 0, 2)).reshape(K, -1)
    solved = lax.linalg.triangular_solve(gram_factor, flat_rows, left_side=True, lower=True)
    new_block = jnp.transpose(solved.reshape(K, NCH, NB), (1, 0, 2))
    return (new_block, ritz_values)
```

```python
import jax
import jax.numpy as jnp
from jax import lax
from jax.sharding import PartitionSpec as P

HIGHEST = lax.Precision.HIGHEST
SCALE = 2.0 ** -8


def chol_solve(factor, rhs):
    first = lax.linalg.triangular_solve(factor, rhs, left_side=True, lower=True)
    return lax.linalg.triangular_solve(factor, first, left_side=True, lower=True, transpose_a=True)


def exchange_sum(x, axis):
    n = lax.axis_size(axis)
    step = 1
    while step < n:
        x = x + lax.ppermute(x, axis, [(i, i ^ step) for i in range(n)])
        step *= 2
    return x


def body(trial_block, ham_blocks, partners, stored_at, precond_diag):
    n_chan = lax.axis_size("chan")
    n_rad = lax.axis_size("rad")
    ch_dev, vectors, _ = trial_block.shape
    ncoup = partners.shape[1]
    total = n_chan * ch_dev * n_rad * trial_block.shape[2]
    share = ch_dev // n_rad

    rounded = trial_block.astype(jnp.bfloat16)
    own = lax.all_gather(rounded, "rad", axis=2, tiled=True)
    mine = lax.dynamic_slice_in_dim(own, lax.axis_index("rad") * share, share, 0)
    part = lax.all_gather(mine, "chan", axis=0, tiled=True)
    table = lax.all_gather(part, "rad", axis=0, tiled=True)

    stored_rows = jnp.take(stored_at, partners.reshape(-1))
    owner = stored_rows // ch_dev
    local = stored_rows % ch_dev
    where = (local // share) * (n_chan * share) + owner * share + local % share
    coupled = table[where].reshape(ch_dev, ncoup, vectors, table.shape[2])
    applied = lax.dot_general(
        coupled, ham_blocks, (((1, 3), (1, 3)), ((0,), (0,))), preferred_element_type=jnp.float32
    ) * SCALE

    t0 = trial_block
    inv = (1.0 / precond_diag)[:, None, :]
    t1 = t0 * inv
    t2 = t1 * inv
    a2 = applied * inv * inv
    gram_t = jnp.einsum("xpkr,plr->xkl", jnp.stack([t0, t1, t2]), t0, precision=HIGHEST)
    gram_a = jnp.einsum("xpkr,plr->xkl", jnp.stack([t0, t1, t2, a2]), applied, precision=HIGHEST)
    sums = jnp.concatenate([gram_t, gram_a]).reshape(-1, 128)
    sums = exchange_sum(exchange_sum(sums, "rad"), "chan").reshape(7, vectors, vectors)
    b0, b1, b2, s0, s1, s2, aa = (sums[i] for i in range(7))

    def mm(x, y):
        return jnp.matmul(x, y, precision=HIGHEST)

    factor = jnp.linalg.cholesky(b0)
    coef = chol_solve(factor, s0)
    ritz_values = jnp.diagonal(coef) * (1.0 / SCALE)
    mix = chol_solve(factor, s1 - mm(b1, coef))
    cross = mm(s2.T, coef) + mm(s1.T, mix)
    tt = mm(coef.T, mm(b2, coef)) + mm(mix.T, mm(b0, mix))
    tm = mm(coef.T, mm(b1, mix))
    gram = (aa - cross - cross.T + tt + tm + tm.T) / jnp.float32(total)
    gram_factor = jnp.linalg.cholesky(gram)
    ident = jnp.eye(vectors, dtype=jnp.float32)
    linv = lax.linalg.triangular_solve(gram_factor, ident, left_side=True, lower=True)
    wc = mm(linv, coef.T)
    wm = mm(linv, mix.T)
    out = (
        jnp.einsum("lk,pkr->plr", linv, applied, precision=HIGHEST)
        - jnp.einsum("lk,pkr->plr", wc, t0, precision=HIGHEST)
    ) * inv - jnp.einsum("lk,pkr->plr", wm, t0, precision=HIGHEST)
    return (out, ritz_values)


def solution(mesh):
    return jax.shard_map(
        body,
        mesh=mesh,
        in_specs=(
            P("chan", None, "rad"),
            P("chan", None, "rad", None),
            P("chan", None),
            P(),
            P("chan", "rad"),
        ),
        out_specs=(P("chan", None, "rad"), P()),
        check_vma=False,
    )
```

```python
import functools

import jax
import jax.numpy as jnp
from jax import lax
from jax.experimental import pallas as pl
from jax.experimental.pallas import tpu as pltpu
from jax.sharding import PartitionSpec as P

HIGHEST = lax.Precision.HIGHEST
SCALE = 2.0 ** -8
F32 = jnp.float32
BF16 = jnp.bfloat16
NT = (((1,), (1,)), ((), ()))


def swap(x, axis, distance):
    n = lax.axis_size(axis)
    return lax.ppermute(x, axis, [(i, i ^ distance) for i in range(n)])


def exchange_sum(x, axis):
    step = 1
    while step < lax.axis_size(axis):
        x = x + swap(x, axis, step)
        step *= 2
    return x


def trial_kernel(t_ref, d_ref, t0_ref, t1_ref, gram_ref):
    ch, k, r = t_ref.shape
    group = 128 // r
    for i in range(ch // group):
        lanes = pl.ds(i * 128, 128)
        t = jnp.concatenate([t_ref[i * group + g] for g in range(group)], axis=1)
        t0_ref[:, lanes] = t
        t1_ref[:, lanes] = t / d_ref[pl.ds(i, 1), :]
    z = jnp.concatenate([t1_ref[...], t0_ref[...]], axis=0)
    gram_ref[...] = lax.dot_general(z, z, NT, precision=HIGHEST, preferred_element_type=F32)


def apply_kernel(
    n_chan, n_rad, partners_ref, stored_ref, ham_ref, t0_ref, t1_ref, d_ref, *rest
):
    pieces = rest[: 6 * n_rad]
    a1_ref, gram_ref, table, sems = rest[6 * n_rad :]
    step = pl.program_id(0)
    per_step, ncoup, r, _ = ham_ref.shape
    k = t0_ref.shape[0]
    nz, half = table.shape[3:5]
    ch = 2 * half * n_rad
    me_chan, me_rad = lax.axis_index("chan"), lax.axis_index("rad")
    places = ((0, 0), (1, 0), (0, 1), (1, 2), (0, 2), (1, 1))

    @pl.when(step == 0)
    def _():
        copies = []
        for c in range(n_rad):
            for i, (h, d) in enumerate(places):
                piece = pieces[c * 6 + i]
                if piece.shape[0] == nz:
                    copies.append((piece, table.at[c, h, d]))
                else:
                    copies.append((piece.at[pl.ds(0, nz)], table.at[c, h, d]))
                    copies.append((piece.at[pl.ds(nz, nz)], table.at[c, h, 3]))
        copies = [pltpu.make_async_copy(s, d, sems.at[i]) for i, (s, d) in enumerate(copies)]
        for c in copies:
            c.start()
        for c in copies:
            c.wait()

    blocks = []
    for p in range(per_step):
        rows = []
        for j in range(ncoup):
            q = stored_ref[partners_ref[(step * per_step + p) * ncoup + j]]
            owner, local = lax.div(q, ch), lax.rem(q, ch)
            slot = owner ^ me_chan
            core = lax.div(local, 2 * half) ^ me_rad
            h = lax.rem(lax.div(local, half), 2)
            rows.append(table[core, h, slot & 3, lax.div(slot, 4), lax.rem(local, half)])
        lhs = jnp.concatenate(rows, axis=1)
        rhs = jnp.concatenate([ham_ref[p, j] for j in range(ncoup)], axis=1)
        blocks.append(lax.dot_general(lhs, rhs, NT, preferred_element_type=F32))
    a0 = jnp.concatenate(blocks, axis=1) * SCALE
    a1 = a0 / d_ref[...]
    a1_ref[...] = a1
    z = jnp.concatenate([a1, t1_ref[...], t0_ref[...]], axis=0)
    gram = lax.dot_general(
        z, jnp.concatenate([a1, a0], axis=0), NT, precision=HIGHEST, preferred_element_type=F32
    )

    @pl.when(step == 0)
    def _():
        gram_ref[...] = gram

    @pl.when(step > 0)
    def _():
        gram_ref[...] += gram


def mm(x, y, dims=(((1,), (0,)), ((), ()))):
    return lax.dot_general(x, y, dims, precision=HIGHEST, preferred_element_type=F32)


def finish_kernel(total, gt_ref, ga_ref, a1_ref, t1_ref, t0_ref, out_ref, ritz_ref):
    ch, k, r = out_ref.shape
    gt, ga = gt_ref[...], ga_ref[...]
    row = lax.broadcasted_iota(jnp.int32, (k, 4 * k), 0)
    aug = jnp.concatenate([ga[2 * k :, :k], gt[k:, :], ga[2 * k :, k:]], axis=1)
    for i in range(k):
        pivot_row = aug[i : i + 1, :] / aug[i : i + 1, 2 * k + i : 2 * k + i + 1]
        column = aug[:, 2 * k + i : 2 * k + i + 1]
        aug = jnp.where(row == i, pivot_row, aug - column * pivot_row)
    coef = aug[:, 3 * k :]
    mix = aug[:, :k] - mm(aug[:, k : 2 * k], coef)
    eye = lax.broadcasted_iota(jnp.int32, (k, k), 0) == lax.broadcasted_iota(jnp.int32, (k, k), 1)
    ritz_ref[...] = jnp.sum(jnp.where(eye, coef, 0.0), axis=0, keepdims=True) * (1.0 / SCALE)
    w = jnp.concatenate([eye.astype(F32), -coef, -mix], axis=0)
    s2, s1 = ga[k : 2 * k, :k], ga[2 * k :, :k]
    top = jnp.concatenate([ga[:k, :k], s2.T, s1.T], axis=1)
    low = jnp.concatenate([ga[k:, :k], gt], axis=1)
    y = mm(jnp.concatenate([top, low], axis=0), w)
    wide = lax.broadcasted_iota(jnp.int32, (3 * k, 3 * k), 0) == lax.broadcasted_iota(
        jnp.int32, (3 * k, 3 * k), 1
    )
    aug = mm(w, jnp.concatenate([y, wide.astype(F32)], axis=1), (((0,), (0,)), ((), ())))
    for i in range(k):
        pivot_row = aug[i : i + 1, :]
        pivot = pivot_row[:, i : i + 1]
        column = jnp.where(row[:, :1] > i, aug[:, i : i + 1] / pivot, 0.0)
        scaled = pivot_row * (lax.rsqrt(pivot) * (total ** 0.5))
        aug = jnp.where(row == i, scaled, aug - column * pivot_row)
    x = jnp.concatenate([a1_ref[...], t1_ref[...], t0_ref[...]], axis=0)
    new = mm(aug[:, k:], x)
    for p in range(ch):
        out_ref[p] = new[:, p * r : (p + 1) * r]


def body(trial_block, ham_blocks, partners, stored_at, precond_diag):
    n_chan, n_rad = lax.axis_size("chan"), lax.axis_size("rad")
    ch, k, r = trial_block.shape
    ncoup = partners.shape[1]
    lanes = ch * r
    total = float(n_chan * n_rad * lanes)
    share, nz = ch // n_rad, n_chan // 4
    half = share // 2

    rounded = trial_block.astype(BF16)
    own = lax.all_to_all(rounded, "rad", split_axis=0, concat_axis=2, tiled=True)
    column = [own] + [swap(own, "chan", 4 * z) for z in range(1, nz)]
    z1 = jnp.stack([c[:half] for c in column])
    z2 = jnp.stack([c[half:] for c in column])
    x1 = swap(z1, "chan", 1)
    y1 = swap(z2, "chan", 2)
    y2 = swap(jnp.concatenate([z1, x1]), "chan", 2)
    x2 = swap(jnp.concatenate([z2, y1]), "chan", 1)
    mine = [z1, z2, x1, y1, y2, x2]
    pieces = list(mine)
    for c in range(1, n_rad):
        pieces += [swap(m, "rad", c) for m in mine]

    d = precond_diag.reshape(lanes // 128, 128)
    t0, t1, gram_t = pl.pallas_call(
        trial_kernel,
        out_shape=[
            jax.ShapeDtypeStruct((k, lanes), F32),
            jax.ShapeDtypeStruct((k, lanes), F32),
            jax.ShapeDtypeStruct((2 * k, 2 * k), F32),
        ],
        name="trial_gram",
    )(trial_block, d)

    per_step = 8
    block = per_step * r
    columns = pl.BlockSpec((k, block), lambda i, *_: (0, i))
    a1, gram_a = pl.pallas_call(
        functools.partial(apply_kernel, n_chan, n_rad),
        grid_spec=pltpu.PrefetchScalarGridSpec(
            num_scalar_prefetch=2,
            grid=(ch // per_step,),
            in_specs=[
                pl.BlockSpec((per_step, ncoup, r, ham_blocks.shape[3]), lambda i, *_: (i, 0, 0, 0)),
                columns,
                columns,
                pl.BlockSpec((1, block), lambda i, *_: (0, i)),
            ]
            + [pl.BlockSpec(memory_space=pl.ANY)] * len(pieces),
            out_specs=[columns, pl.BlockSpec((3 * k, 2 * k), lambda i, *_: (0, 0))],
            scratch_shapes=[
                pltpu.VMEM((n_rad, 2, 4, nz, half, k, ham_blocks.shape[3]), BF16),
                pltpu.SemaphoreType.DMA((8 * n_rad,)),
            ],
        ),
        out_shape=[
            jax.ShapeDtypeStruct((k, lanes), F32),
            jax.ShapeDtypeStruct((3 * k, 2 * k), F32),
        ],
        compiler_params=pltpu.CompilerParams(vmem_limit_bytes=24 * 1024 * 1024),
        name="apply",
    )(partners.reshape(-1), stored_at, ham_blocks, t0, t1, precond_diag.reshape(1, lanes), *pieces)

    gt = jnp.pad(gram_t, ((0, k), (0, 0)))
    sums = jnp.concatenate([gt, gram_a], axis=1)
    sums = exchange_sum(exchange_sum(sums, "rad"), "chan")
    new_block, ritz = pl.pallas_call(
        functools.partial(finish_kernel, total),
        out_shape=[
            jax.ShapeDtypeStruct((ch, k, r), F32),
            jax.ShapeDtypeStruct((1, k), F32),
        ],
        name="finish",
    )(sums[: 2 * k, : 2 * k], sums[:, 2 * k :], a1, t1, t0)
    return (new_block, ritz.reshape(k))


def solution(mesh):
    return jax.shard_map(
        body,
        mesh=mesh,
        in_specs=(
            P("chan", None, "rad"),
            P("chan", None, "rad", None),
            P("chan", None),
            P(),
            P("chan", "rad"),
        ),
        out_specs=(P("chan", None, "rad"), P()),
        check_vma=False,
    )
```

```python
import functools

import jax
import jax.numpy as jnp
from jax import lax
from jax.experimental import pallas as pl
from jax.experimental.pallas import tpu as pltpu
from jax.sharding import PartitionSpec as P

SCALE = 2.0 ** -8
F32 = jnp.float32
BF16 = jnp.bfloat16
NT = (((1,), (1,)), ((), ()))
TN = (((0,), (0,)), ((), ()))
NN = (((1,), (0,)), ((), ()))
VMEM_LIMIT = 48 * 1024 * 1024
PIECES = 6


def swap(x, axis, distance):
    n = lax.axis_size(axis)
    return lax.ppermute(x, axis, [(i, i ^ distance) for i in range(n)])


def plane_swap(x, order):
    n_chan, n_rad = lax.axis_size("chan"), lax.axis_size("rad")
    pairs = []
    for c in range(n_chan):
        for r in range(n_rad):
            pairs.append((c * n_rad + r, (c ^ order[r % 2]) * n_rad + r))
    return lax.ppermute(x, ("chan", "rad"), pairs)


def z_groups(nz):
    return [[0], [1] + list(range(2, nz, 2)), list(range(3, nz, 2))]


def z_place(z, nz):
    if nz == 4:
        return z
    return jnp.where(z < 2, z, jnp.where((z & 1) == 1, (nz + z - 1) >> 1, 1 + (z >> 1)))


def split3(x):
    hi = x.astype(BF16)
    rest = x - hi.astype(F32)
    mid = rest.astype(BF16)
    return hi, mid, (rest - mid.astype(F32)).astype(BF16)


def dot32(x, y, dims=NN):
    return lax.dot_general(x, y, dims, precision=lax.Precision.HIGHEST, preferred_element_type=F32)


def block_sum(g, rows, cols):
    g = sum(g[i : i + rows] for i in range(0, g.shape[0], rows))
    return sum(g[:, i : i + cols] for i in range(0, g.shape[1], cols))


def trial_kernel(t_ref, d_ref, zhm_ref, zl_ref, dc_ref, gram_ref):
    ch, k, r = t_ref.shape
    group = 128 // r
    for i in range(ch // group):
        lanes = pl.ds(i * 128, 128)
        t = jnp.concatenate([t_ref[i * group + g] for g in range(group)], axis=1)
        d = jnp.concatenate([d_ref[pl.ds(i * group + g, 1), :] for g in range(group)], axis=1)
        dc_ref[:, lanes] = d
        hi, mid, lo = split3(jnp.concatenate([t / d, t], axis=0))
        zhm_ref[:, lanes] = jnp.concatenate([hi, mid], axis=0)
        zl_ref[:, lanes] = lo
    z = jnp.concatenate([zhm_ref[...], zl_ref[...]], axis=0)
    g = block_sum(lax.dot_general(z, z, NT, preferred_element_type=F32), 2 * k, 2 * k)
    gram_ref[...] = jnp.concatenate([g[k:, :], g[:k, :k]], axis=1)


def apply_kernel(
    n_chan, n_rad, groups, partners_ref, stored_ref, ham_hbm, zhm_ref, zl_ref, dc_ref, gt_ref, *rest
):
    pieces = rest[: PIECES * n_rad]
    az_ref, sums_ref, table, ham, table_sems, ham_sems = rest[PIECES * n_rad :]
    ch, ncoup, r, _ = ham.shape
    k = zl_ref.shape[0] // 2
    nz, share = table.shape[2:4]
    per_step = 8
    steps = ch // per_step
    block = per_step * r
    me_chan, me_rad = lax.axis_index("chan"), lax.axis_index("rad")

    first = (0, groups[0], groups[0] + groups[1], nz)
    copies = []
    for c in range(n_rad):
        for i, (g, h) in enumerate(((0, 0), (0, 1), (1, 0), (2, 0), (1, 1), (2, 1))):
            place = table.at[c, pl.ds(2 * h, 2), pl.ds(first[g], groups[g])]
            n = c * PIECES + i
            copies.append(pltpu.make_async_copy(pieces[n], place, table_sems.at[n]))
    for copy in copies:
        copy.start()

    def ham_copy(step):
        rows = pl.ds(step * per_step, per_step)
        return pltpu.make_async_copy(ham_hbm.at[rows], ham.at[rows], ham_sems.at[step])

    for step in range(steps):
        ham_copy(step).start()
    for copy in copies:
        copy.wait()

    def work(step, gram):
        ham_copy(step).wait()
        blocks = []
        for i in range(per_step):
            p = step * per_step + i
            rows = []
            for j in range(ncoup):
                q = stored_ref[partners_ref[j, p]]
                slot = lax.div(q, ch) ^ me_chan
                local = lax.rem(q, ch)
                core = lax.div(local, share)
                near = slot & 3
                part = jnp.where((core & 1) == 1, ((near & 1) << 1) | (near >> 1), near)
                rows.append(table[core ^ me_rad, part, z_place(slot >> 2, nz), lax.rem(local, share)])
            lhs = jnp.concatenate(rows, axis=1)
            rhs = jnp.concatenate([ham[p, j] for j in range(ncoup)], axis=1)
            blocks.append(lax.dot_general(lhs, rhs, NT, preferred_element_type=F32))
        lanes = pl.ds(pl.multiple_of(step * block, block), block)
        a0 = jnp.concatenate(blocks, axis=1) * SCALE
        a1_terms = split3(a0 / dc_ref[:, lanes])
        az_ref[:, lanes] = jnp.concatenate(a1_terms[:2], axis=0)
        right = jnp.concatenate(a1_terms + split3(a0), axis=0)
        left = jnp.concatenate([zhm_ref[:, lanes], zl_ref[:, lanes], right[: 3 * k]], axis=0)
        return gram + lax.dot_general(left, right, NT, preferred_element_type=F32)

    gram = lax.fori_loop(0, steps, work, jnp.zeros((9 * k, 6 * k), F32))
    ta1 = block_sum(gram[: 6 * k, : 3 * k], 2 * k, k)
    ta0 = block_sum(gram[: 6 * k, 3 * k :], 2 * k, k)
    aa = block_sum(gram[6 * k :, : 3 * k], k, k)
    gt = gt_ref[...]
    parts = [ta1[k:], gt[:, : 2 * k], ta0[k:], ta1[:k], gt[:, 2 * k :], aa, jnp.zeros((k, k), F32)]
    sums_ref[...] = jnp.concatenate(parts, axis=1)


def finish_kernel(total, sums_ref, az_ref, zhm_ref, out_ref, ritz_ref):
    ch, k, r = out_ref.shape
    s = jnp.sum(sums_ref[...], axis=0)
    row = lax.broadcasted_iota(jnp.int32, (k, 4 * k), 0)
    b1, b0 = s[:, k : 2 * k], s[:, 2 * k : 3 * k]
    s1, s2 = s[:, :k], s[:, 4 * k : 5 * k]
    b2, aa = s[:, 5 * k : 6 * k], s[:, 6 * k : 7 * k]
    aug = s[:, : 4 * k]
    for i in range(k):
        pivot_row = aug[i : i + 1, :] / aug[i : i + 1, 2 * k + i : 2 * k + i + 1]
        column = aug[:, 2 * k + i : 2 * k + i + 1]
        aug = jnp.where(row == i, pivot_row, aug - column * pivot_row)
    coef = aug[:, 3 * k :]
    mix = aug[:, :k] - dot32(aug[:, k : 2 * k], coef)
    eye = lax.broadcasted_iota(jnp.int32, (k, k), 0) == lax.broadcasted_iota(jnp.int32, (k, k), 1)
    ritz_ref[...] = jnp.sum(jnp.where(eye, coef, 0.0), axis=0, keepdims=True) * (1.0 / SCALE)
    e = jnp.concatenate([coef, mix], axis=0)
    q = jnp.concatenate([s2, s1], axis=0)
    b = jnp.concatenate(
        [jnp.concatenate([b2, b1.T], axis=1), jnp.concatenate([b1, b0], axis=1)], axis=0
    )
    gram = aa - dot32(q, e, TN) - dot32(e, q - dot32(b, e), TN)
    aug = jnp.concatenate([gram, eye.astype(F32), -coef.T, -mix.T], axis=1)
    for i in range(k):
        pivot_row = aug[i : i + 1, :]
        pivot = pivot_row[:, i : i + 1]
        column = jnp.where(row[:, :1] > i, aug[:, i : i + 1] / pivot, 0.0)
        scaled = pivot_row * (lax.rsqrt(pivot) * (total ** 0.5))
        aug = jnp.where(row == i, scaled, aug - column * pivot_row)
    hi, mid, _ = split3(aug[:, k:])
    lhs = jnp.concatenate([hi, hi, mid], axis=1)
    x_hi = jnp.concatenate([az_ref[:k, :], zhm_ref[: 2 * k, :]], axis=0)
    x_mid = jnp.concatenate([az_ref[k:, :], zhm_ref[2 * k :, :]], axis=0)
    new = lax.dot_general(
        lhs, jnp.concatenate([x_hi, x_mid, x_hi], axis=0), NN, preferred_element_type=F32
    )
    for p in range(ch):
        out_ref[p] = new[:, p * r : (p + 1) * r]


def own_share(trial_block):
    n_rad = lax.axis_size("rad")
    ch, k, r = trial_block.shape
    me = lax.axis_index("rad")
    rounded = trial_block.astype(BF16).reshape(n_rad, ch // n_rad, k, r)
    got = []
    for d in range(n_rad):
        part = lax.dynamic_index_in_dim(rounded, me ^ d, 0, keepdims=False)
        got.append(swap(part, "rad", d) if d else part)
    lanes = []
    for c in range(n_rad):
        x = got[0]
        for d in range(1, n_rad):
            x = jnp.where(me ^ d == c, got[d], x)
        lanes.append(x)
    return jnp.concatenate(lanes, axis=2)


def body(trial_block, ham_blocks, partners, stored_at, precond_diag):
    n_chan, n_rad = lax.axis_size("chan"), lax.axis_size("rad")
    ch, k, r = trial_block.shape
    splines = ham_blocks.shape[3]
    lanes = ch * r
    total = float(n_chan * n_rad * lanes)
    share, nz = ch // n_rad, n_chan // 4

    own = own_share(trial_block)
    column = [own] + [None] * (nz - 1)
    for z in range(nz - 2, 0, -2):
        column[z] = swap(own, "chan", 4 * z)
    column[1] = swap(own, "chan", 4)
    near = plane_swap(own[None], (1, 2))
    local = pl.pallas_call(
        trial_kernel,
        out_shape=[
            jax.ShapeDtypeStruct((4 * k, lanes), BF16),
            jax.ShapeDtypeStruct((2 * k, lanes), BF16),
            jax.ShapeDtypeStruct((1, lanes), F32),
            jax.ShapeDtypeStruct((k, 3 * k), F32),
        ],
        name="trial_gram",
    )(trial_block, precond_diag)
    column, near, local = lax.optimization_barrier((column, near, local))
    zhm, zl, dc, gram_t = local

    def second(parts, first):
        half = jnp.stack([parts, first])
        return half, plane_swap(half, (2, 1))

    groups = z_groups(nz)
    half0, far0 = second(own[None], near)
    parts1 = jnp.stack([column[z] for z in groups[1]])
    near1 = plane_swap(parts1, (1, 2))
    for z in groups[2]:
        column[z] = swap(column[z - 1], "chan", 4)
    column, near1, half0, far0 = lax.optimization_barrier((column, near1, half0, far0))
    parts2 = jnp.stack([column[z] for z in groups[2]])
    near2 = plane_swap(parts2, (1, 2))
    half1, far1 = second(parts1, near1)
    others = [[swap(x, "rad", c) for x in (half0, far0, half1)] for c in range(1, n_rad)]
    near2, others = lax.optimization_barrier((near2, others))
    half2, far2 = second(parts2, near2)
    others = [o + [swap(half2, "rad", c + 1)] for c, o in enumerate(others)]
    far1, far2, others = lax.optimization_barrier((far1, far2, others))
    pieces = [half0, far0, half1, half2, far1, far2]
    for c, o in enumerate(others):
        pieces += o + [swap(x, "rad", c + 1) for x in (far1, far2)]
    sizes = [len(g) for g in groups]
    whole = pl.BlockSpec(memory_space=pltpu.VMEM)
    smem = pl.BlockSpec(memory_space=pltpu.SMEM)
    any_ = pl.BlockSpec(memory_space=pl.ANY)
    az, sums = pl.pallas_call(
        functools.partial(apply_kernel, n_chan, n_rad, sizes),
        in_specs=[smem, smem, any_, whole, whole, whole, whole] + [any_] * len(pieces),
        out_shape=[
            jax.ShapeDtypeStruct((2 * k, lanes), BF16),
            jax.ShapeDtypeStruct((k, 8 * k), F32),
        ],
        scratch_shapes=[
            pltpu.VMEM((n_rad, 4, nz, share, k, splines), BF16),
            pltpu.VMEM(ham_blocks.shape, BF16),
            pltpu.SemaphoreType.DMA((len(pieces),)),
            pltpu.SemaphoreType.DMA((ch // 8,)),
        ],
        compiler_params=pltpu.CompilerParams(vmem_limit_bytes=VMEM_LIMIT),
        name="apply",
    )(partners.T, stored_at, ham_blocks, zhm, zl, dc, gram_t, *pieces)

    for c in range(n_rad.bit_length() - 1):
        sums = sums + swap(sums, "rad", 1 << c)
    all_sums = lax.all_to_all(
        jnp.broadcast_to(sums, (n_chan,) + sums.shape), "chan", split_axis=0, concat_axis=0, tiled=True
    )
    new_block, ritz = pl.pallas_call(
        functools.partial(finish_kernel, total),
        out_shape=[
            jax.ShapeDtypeStruct((ch, k, r), F32),
            jax.ShapeDtypeStruct((1, k), F32),
        ],
        name="finish",
    )(all_sums, az, zhm)
    return (new_block, ritz.reshape(k))


def solution(mesh):
    return jax.shard_map(
        body,
        mesh=mesh,
        in_specs=(
            P("chan", None, "rad"),
            P("chan", None, "rad", None),
            P("chan", None),
            P(),
            P("chan", "rad"),
        ),
        out_specs=(P("chan", None, "rad"), P()),
        check_vma=False,
    )
```

```python
import functools

import jax
import jax.numpy as jnp
from jax import lax
from jax.experimental import pallas as pl
from jax.experimental.pallas import tpu as pltpu
from jax.sharding import PartitionSpec as P

SCALE = 2.0 ** -8
F32 = jnp.float32
BF16 = jnp.bfloat16
NT = (((1,), (1,)), ((), ()))
TN = (((0,), (0,)), ((), ()))
NN = (((1,), (0,)), ((), ()))
VMEM_LIMIT = 12 * 1024 * 1024


def swap(x, axis, distance):
    n = lax.axis_size(axis)
    return lax.ppermute(x, axis, [(i, i ^ distance) for i in range(n)])


def plane_swap(x, order):
    n_chan, n_rad = lax.axis_size("chan"), lax.axis_size("rad")
    pairs = []
    for c in range(n_chan):
        for r in range(n_rad):
            pairs.append((c * n_rad + r, (c ^ order[r % 2]) * n_rad + r))
    return lax.ppermute(x, ("chan", "rad"), pairs)


def z_groups(nz):
    return [[0], [1] + list(range(2, nz, 2)), list(range(3, nz, 2))]


def z_place(z, nz):
    if nz == 4:
        return z
    return jnp.where(z < 2, z, jnp.where((z & 1) == 1, (nz + z - 1) >> 1, 1 + (z >> 1)))


def in_vmem(x):
    return pltpu.with_memory_space_constraint(x, pltpu.VMEM)


def in_hbm(x):
    return pltpu.with_memory_space_constraint(x, pltpu.HBM)


def split3(x):
    hi = x.astype(BF16)
    rest = x - hi.astype(F32)
    mid = rest.astype(BF16)
    return hi, mid, (rest - mid.astype(F32)).astype(BF16)


def dot32(x, y, dims=NN):
    return lax.dot_general(x, y, dims, precision=lax.Precision.HIGHEST, preferred_element_type=F32)


def block_sum(g, rows, cols):
    g = sum(g[i : i + rows] for i in range(0, g.shape[0], rows))
    return sum(g[:, i : i + cols] for i in range(0, g.shape[1], cols))


def trial_kernel(t_ref, d_ref, zhm_ref, zl_ref, dc_ref, gram_ref):
    ch, k, r = t_ref.shape
    group = 128 // r
    for i in range(ch // group):
        lanes = pl.ds(i * 128, 128)
        t = jnp.concatenate([t_ref[i * group + g] for g in range(group)], axis=1)
        d = jnp.concatenate([d_ref[pl.ds(i * group + g, 1), :] for g in range(group)], axis=1)
        dc_ref[:, lanes] = d
        hi, mid, lo = split3(jnp.concatenate([t / d, t], axis=0))
        zhm_ref[:, lanes] = jnp.concatenate([hi, mid], axis=0)
        zl_ref[:, lanes] = lo
    z = jnp.concatenate([zhm_ref[...], zl_ref[...]], axis=0)
    g = block_sum(lax.dot_general(z, z, NT, preferred_element_type=F32), 2 * k, 2 * k)
    gram_ref[...] = jnp.concatenate([g[k:, :], g[:k, :k]], axis=1)


def load_kernel(n_chan, n_rad, partners_ref, stored_ref, ham_hbm, ham_ref, rows_ref, sem):
    ncoup, ch = partners_ref.shape
    share, nz = ch // n_rad, n_chan // 4
    copy = pltpu.make_async_copy(ham_hbm, ham_ref, sem)
    copy.start()
    me_chan, me_rad = lax.axis_index("chan"), lax.axis_index("rad")

    def find(p, carry):
        for j in range(ncoup):
            q = stored_ref[partners_ref[j, p]]
            slot = lax.div(q, ch) ^ me_chan
            local = lax.rem(q, ch)
            core = lax.div(local, share)
            near = slot & 3
            part = jnp.where((core & 1) == 1, ((near & 1) << 1) | (near >> 1), near)
            place = ((core ^ me_rad) * 4 + part) * nz + z_place(slot >> 2, nz)
            rows_ref[p * ncoup + j] = place * share + lax.rem(local, share)
        return carry

    lax.fori_loop(0, ch, find, 0)
    copy.wait()


def apply_kernel(rows_ref, ham_ref, table_ref, zhm_ref, zl_ref, dc_ref, gt_ref, az_ref, sums_ref, a0_ref):
    ch, ncoup, r, splines = ham_ref.shape
    k = zl_ref.shape[0] // 2
    group = 256 // r

    def work(g, carry):
        left, right = [], []
        for i in range(group):
            p = g * group + i
            left.append(
                jnp.concatenate([table_ref[rows_ref[p * ncoup + j]] for j in range(ncoup)], axis=1)
            )
            right.append(jnp.concatenate([ham_ref[p, j] for j in range(ncoup)], axis=1))
        product = lax.dot_general(
            jnp.concatenate(left, axis=0),
            jnp.concatenate(right, axis=0),
            NT,
            preferred_element_type=F32,
        )
        own = [product[i * k : (i + 1) * k, i * r : (i + 1) * r] for i in range(group)]
        a0_ref[:, pl.ds(pl.multiple_of(g * 256, 256), 256)] = jnp.concatenate(own, axis=1) * SCALE
        return carry

    lax.fori_loop(0, ch // group, work, 0)

    lanes = ch * r
    block = min(lanes, 1024)

    def gram_block(i, gram):
        at = pl.ds(pl.multiple_of(i * block, block), block)
        a0 = a0_ref[:, at]
        a1_terms = split3(a0 / dc_ref[:, at])
        az_ref[:, at] = jnp.concatenate(a1_terms[:2], axis=0)
        right = jnp.concatenate(a1_terms + split3(a0), axis=0)
        left = jnp.concatenate([zhm_ref[:, at], zl_ref[:, at], right[: 3 * k]], axis=0)
        return gram + lax.dot_general(left, right, NT, preferred_element_type=F32)

    gram = lax.fori_loop(0, lanes // block, gram_block, jnp.zeros((9 * k, 6 * k), F32))
    ta1 = block_sum(gram[: 6 * k, : 3 * k], 2 * k, k)
    ta0 = block_sum(gram[: 6 * k, 3 * k :], 2 * k, k)
    aa = block_sum(gram[6 * k :, : 3 * k], k, k)
    gt = gt_ref[...]
    parts = [ta1[k:], gt[:, : 2 * k], ta0[k:], ta1[:k], gt[:, 2 * k :], aa, jnp.zeros((k, k), F32)]
    sums_ref[...] = jnp.concatenate(parts, axis=1)


def spread(x, i):
    return jnp.broadcast_to(x[:, i : i + 1], (x.shape[0], 128))


def finish_kernel(total, sums_ref, az_ref, zhm_ref, out_ref, ritz_ref):
    ch, k, r = out_ref.shape
    s = sums_ref[...]
    row = lax.broadcasted_iota(jnp.int32, (k, 128), 0)
    cols = [spread(s, 2 * k + i) for i in range(k)]
    x = s
    for i in range(k):
        scale = 1.0 / cols[i][i : i + 1]
        pivot = x[i : i + 1] * scale
        x = jnp.where(row == i, pivot, x - cols[i] * pivot)
        for j in range(i + 1, k):
            part = cols[j][i : i + 1] * scale
            cols[j] = jnp.where(row == i, part, cols[j] - cols[i] * part)
    coef = x[:, 3 * k : 4 * k]
    eye = lax.broadcasted_iota(jnp.int32, (k, k), 0) == lax.broadcasted_iota(jnp.int32, (k, k), 1)
    ritz_ref[...] = jnp.sum(jnp.where(eye, coef, 0.0), axis=0, keepdims=True) * (1.0 / SCALE)
    s1, b1 = s[:, :k], s[:, k : 2 * k]
    s2, b2, aa = s[:, 4 * k : 5 * k], s[:, 5 * k : 6 * k], s[:, 6 * k : 7 * k]
    known = jnp.concatenate([x[:, :k], s1, s2], axis=0)
    known = known - dot32(jnp.concatenate([x[:, k : 2 * k], b1, b2], axis=0), coef)
    mix, corr, weighted = known[:k], known[k : 2 * k], known[2 * k :]
    gram = aa - dot32(
        jnp.concatenate([s2, coef, corr], axis=0), jnp.concatenate([coef, weighted, mix], axis=0), TN
    )
    cols = [spread(gram, i) for i in range(k)]
    pad = jnp.zeros((k, 128 - 3 * k), F32)
    x = jnp.concatenate([eye.astype(F32), -coef.T, -mix.T, pad], axis=1)
    for i in range(k):
        pivot = cols[i][i : i + 1]
        scale = 1.0 / pivot
        below = jnp.where(row > i, cols[i] * scale, 0.0)
        pivot_row = x[i : i + 1]
        x = jnp.where(row == i, pivot_row * (lax.rsqrt(pivot) * (total ** 0.5)), x - below * pivot_row)
        for j in range(i + 1, k):
            cols[j] = cols[j] - below * cols[j][i : i + 1]
    hi, mid, _ = split3(x[:, : 3 * k])
    lhs = jnp.concatenate([hi, hi, mid], axis=1)
    block = min(ch * r, 1024)

    def result(b, carry):
        at = pl.ds(pl.multiple_of(b * block, block), block)
        x_hi = jnp.concatenate([az_ref[:k, at], zhm_ref[: 2 * k, at]], axis=0)
        x_mid = jnp.concatenate([az_ref[k:, at], zhm_ref[2 * k :, at]], axis=0)
        new = lax.dot_general(
            lhs, jnp.concatenate([x_hi, x_mid, x_hi], axis=0), NN, preferred_element_type=F32
        )
        for i in range(block // r):
            out_ref[b * (block // r) + i] = new[:, i * r : (i + 1) * r]
        return carry

    lax.fori_loop(0, ch * r // block, result, 0)


def chip_pairs(pick):
    n_chan, n_rad = lax.axis_size("chan"), lax.axis_size("rad")
    pairs = []
    for c in range(n_chan):
        for r in range(n_rad):
            distance = pick[r % 2]
            if distance:
                pairs.append((c * n_rad + r, (c ^ distance) * n_rad + r))
    return pairs


def sum_everywhere(x):
    n_chan, n_rad = lax.axis_size("chan"), lax.axis_size("rad")
    step = 1
    while step < n_rad:
        x = x + swap(x, "rad", step)
        step *= 2
    even = lax.axis_index("rad") % 2 == 0
    step = 1
    while step < n_chan:
        first = lax.ppermute(x, ("chan", "rad"), chip_pairs((step, 2 * step)))
        other = lax.ppermute(x, ("chan", "rad"), chip_pairs((0, 3 * step)))
        x = first + jnp.where(even, x, other)
        x = x + swap(x, "rad", 1)
        step *= 4
    return x


def own_share(trial_block):
    n_rad = lax.axis_size("rad")
    ch, k, r = trial_block.shape
    me = lax.axis_index("rad")
    rounded = trial_block.astype(BF16).reshape(n_rad, ch // n_rad, k, r)
    got = []
    for d in range(n_rad):
        part = lax.dynamic_index_in_dim(rounded, me ^ d, 0, keepdims=False)
        got.append(swap(part, "rad", d) if d else part)
    lanes = []
    for c in range(n_rad):
        x = got[0]
        for d in range(1, n_rad):
            x = jnp.where(me ^ d == c, got[d], x)
        lanes.append(x)
    return jnp.concatenate(lanes, axis=2)


def body(trial_block, ham_blocks, partners, stored_at, precond_diag):
    n_chan, n_rad = lax.axis_size("chan"), lax.axis_size("rad")
    ch, k, r = trial_block.shape
    ncoup, splines = ham_blocks.shape[1], ham_blocks.shape[3]
    lanes = ch * r
    total = float(n_chan * n_rad * lanes)
    share, nz = ch // n_rad, n_chan // 4

    own = own_share(trial_block)
    column = [own] + [None] * (nz - 1)
    for z in range(nz - 2, 0, -2):
        column[z] = swap(own, "chan", 4 * z)
    column[1] = swap(own, "chan", 4)
    near = plane_swap(own[None], (1, 2))
    local = pl.pallas_call(
        trial_kernel,
        out_shape=[
            pltpu.VMEM((4 * k, lanes), BF16),
            pltpu.VMEM((2 * k, lanes), BF16),
            pltpu.VMEM((1, lanes), F32),
            pltpu.VMEM((k, 3 * k), F32),
        ],
        compiler_params=pltpu.CompilerParams(vmem_limit_bytes=VMEM_LIMIT),
        name="trial_gram",
    )(trial_block, precond_diag)
    column, near, local = lax.optimization_barrier((column, near, local))
    zhm, zl, dc, gram_t = local

    def second(parts, first):
        half = jnp.stack([parts, first])
        return half, plane_swap(half, (2, 1))

    groups = z_groups(nz)
    half0, far0 = second(own[None], near)
    parts1 = jnp.stack([column[z] for z in groups[1]])
    near1 = plane_swap(parts1, (1, 2))
    for z in groups[2]:
        column[z] = swap(column[z - 1], "chan", 4)
    column, near1, half0, far0 = lax.optimization_barrier((column, near1, half0, far0))
    parts2 = jnp.stack([column[z] for z in groups[2]])
    near2 = plane_swap(parts2, (1, 2))
    half1, far1 = second(parts1, near1)
    others = [[swap(x, "rad", c) for x in (half0, far0, half1)] for c in range(1, n_rad)]
    near2, others, partners, stored_at, ham_blocks = lax.optimization_barrier(
        (near2, others, partners.T, stored_at, ham_blocks)
    )
    half2, far2 = second(parts2, near2)
    others = [o + [swap(half2, "rad", c + 1)] for c, o in enumerate(others)]
    smem = pl.BlockSpec(memory_space=pltpu.SMEM)
    any_ = pl.BlockSpec(memory_space=pl.ANY)
    whole = pl.BlockSpec(memory_space=pltpu.VMEM)
    ham, rows = pl.pallas_call(
        functools.partial(load_kernel, n_chan, n_rad),
        in_specs=[smem, smem, any_],
        out_specs=[whole, smem],
        out_shape=[
            pltpu.VMEM(ham_blocks.shape, BF16),
            jax.ShapeDtypeStruct((ch * ncoup,), jnp.int32),
        ],
        scratch_shapes=[pltpu.SemaphoreType.DMA],
        compiler_params=pltpu.CompilerParams(vmem_limit_bytes=VMEM_LIMIT),
        name="load",
    )(in_hbm(partners), in_hbm(stored_at), in_hbm(ham_blocks))
    far1, far2, others, ham, rows = lax.optimization_barrier((far1, far2, others, ham, rows))
    tables = [[half0, far0, half1, half2, far1, far2]]
    for c, o in enumerate(others):
        tables.append(o + [swap(x, "rad", c + 1) for x in (far1, far2)])
    table = jnp.stack(
        [
            jnp.concatenate(
                [jnp.concatenate([t[0], t[2], t[3]], axis=1), jnp.concatenate([t[1], t[4], t[5]], axis=1)]
            )
            for t in tables
        ]
    ).reshape(n_chan * ch, k, splines)

    az, sums = pl.pallas_call(
        apply_kernel,
        in_specs=[smem] + [whole] * 6,
        out_specs=[whole, whole],
        out_shape=[
            pltpu.VMEM((2 * k, lanes), BF16),
            jax.ShapeDtypeStruct((k, 8 * k), F32),
        ],
        scratch_shapes=[pltpu.VMEM((k, lanes), F32)],
        compiler_params=pltpu.CompilerParams(vmem_limit_bytes=VMEM_LIMIT),
        name="apply",
    )(rows, in_vmem(ham), in_vmem(table), in_vmem(zhm), in_vmem(zl), in_vmem(dc), gram_t)

    sums = sum_everywhere(sums)
    new_block, ritz = pl.pallas_call(
        functools.partial(finish_kernel, total),
        out_shape=[
            jax.ShapeDtypeStruct((ch, k, r), F32),
            jax.ShapeDtypeStruct((1, k), F32),
        ],
        compiler_params=pltpu.CompilerParams(vmem_limit_bytes=VMEM_LIMIT),
        name="finish",
    )(sums, in_vmem(az), in_vmem(zhm))
    return (new_block, ritz.reshape(k))


def solution(mesh):
    return jax.shard_map(
        body,
        mesh=mesh,
        in_specs=(
            P("chan", None, "rad"),
            P("chan", None, "rad", None),
            P("chan", None),
            P(),
            P("chan", "rad"),
        ),
        out_specs=(P("chan", None, "rad"), P()),
        check_vma=False,
    )
```

```python
import functools

import jax
import jax.numpy as jnp
from jax import lax
from jax.experimental import pallas as pl
from jax.experimental.pallas import tpu as pltpu
from jax.sharding import PartitionSpec as P

SCALE = 2.0 ** -8
F32 = jnp.float32
BF16 = jnp.bfloat16
NT = (((1,), (1,)), ((), ()))
TN = (((0,), (0,)), ((), ()))
NN = (((1,), (0,)), ((), ()))
VMEM_LIMIT = 4 * 1024 * 1024


def swap(x, axis, distance):
    n = lax.axis_size(axis)
    return lax.ppermute(x, axis, [(i, i ^ distance) for i in range(n)])


def plane_swap(x, order):
    n_chan, n_rad = lax.axis_size("chan"), lax.axis_size("rad")
    pairs = []
    for c in range(n_chan):
        for r in range(n_rad):
            pairs.append((c * n_rad + r, (c ^ order[r % 2]) * n_rad + r))
    return lax.ppermute(x, ("chan", "rad"), pairs)


def z_groups(nz):
    return [[0], [1], list(range(2, nz, 2)), list(range(3, nz, 2))]


def z_place(z, nz):
    if nz == 4:
        return z
    return jnp.where(z < 2, z, jnp.where((z & 1) == 1, (nz + z - 1) >> 1, 1 + (z >> 1)))


def in_vmem(x):
    return pltpu.with_memory_space_constraint(x, pltpu.VMEM)


def in_hbm(x):
    return pltpu.with_memory_space_constraint(x, pltpu.HBM)


def split3(x):
    hi = x.astype(BF16)
    rest = x - hi.astype(F32)
    mid = rest.astype(BF16)
    return hi, mid, (rest - mid.astype(F32)).astype(BF16)


def dot32(x, y, dims=NN):
    return lax.dot_general(x, y, dims, precision=lax.Precision.HIGHEST, preferred_element_type=F32)


def block_sum(g, rows, cols):
    g = sum(g[i : i + rows] for i in range(0, g.shape[0], rows))
    return sum(g[:, i : i + cols] for i in range(0, g.shape[1], cols))


def prepare_kernel(
    n_chan, n_rad, t_ref, d_ref, partners_ref, stored_ref, ham_hbm,
    ham_ref, rows_ref, zhm_ref, zl_ref, dc_ref, gram_ref, sem,
):
    copy = pltpu.make_async_copy(ham_hbm, ham_ref, sem)
    copy.start()
    ch, k, r = t_ref.shape
    group = 128 // r
    for i in range(ch // group):
        lanes = pl.ds(i * 128, 128)
        t = jnp.concatenate([t_ref[i * group + g] for g in range(group)], axis=1)
        d = jnp.concatenate([d_ref[pl.ds(i * group + g, 1), :] for g in range(group)], axis=1)
        dc_ref[:, lanes] = d
        hi, mid, lo = split3(jnp.concatenate([t / d, t], axis=0))
        zhm_ref[:, lanes] = jnp.concatenate([hi, mid], axis=0)
        zl_ref[:, lanes] = lo
    z = jnp.concatenate([zhm_ref[...], zl_ref[...]], axis=0)
    g = block_sum(lax.dot_general(z, z, NT, preferred_element_type=F32), 2 * k, 2 * k)
    gram_ref[...] = jnp.concatenate([g[k:, :], g[:k, :k]], axis=1)

    share, nz = ch // n_rad, n_chan // 4
    q = stored_ref[...]
    slot = lax.div(q, ch) ^ lax.axis_index("chan")
    local = lax.rem(q, ch)
    core = lax.div(local, share)
    near = slot & 3
    part = jnp.where((core & 1) == 1, ((near & 1) << 1) | (near >> 1), near)
    place = ((core ^ lax.axis_index("rad")) * nz + z_place(slot >> 2, nz)) * 4 + part
    place = (place * share + lax.rem(local, share)).astype(F32)
    lane = lax.broadcasted_iota(jnp.int32, (ch, 128), 1)
    columns = []
    for j in range(partners_ref.shape[1]):
        wanted = jnp.broadcast_to(partners_ref[:, j : j + 1], (ch, 128)) - lane
        found = jnp.zeros((ch, 128), F32)
        for c in range(place.shape[0]):
            found = found + jnp.where(wanted == 128 * c, place[c : c + 1], 0.0)
        columns.append(jnp.sum(found, axis=1, keepdims=True))
    rows_ref[...] = jnp.concatenate(columns, axis=1).astype(jnp.int32)
    copy.wait()


def apply_kernel(rows_ref, ham_ref, table_ref, zhm_ref, zl_ref, dc_ref, gt_ref, az_ref, sums_ref, a0_ref):
    ch, ncoup, r, splines = ham_ref.shape
    k = zl_ref.shape[0] // 2
    group = 256 // r

    def work(g, carry):
        left, right = [], []
        for i in range(group):
            p = g * group + i
            left.append(
                jnp.concatenate([table_ref[rows_ref[p, j]] for j in range(ncoup)], axis=1)
            )
            right.append(jnp.concatenate([ham_ref[p, j] for j in range(ncoup)], axis=1))
        product = lax.dot_general(
            jnp.concatenate(left, axis=0),
            jnp.concatenate(right, axis=0),
            NT,
            preferred_element_type=F32,
        )
        own = [product[i * k : (i + 1) * k, i * r : (i + 1) * r] for i in range(group)]
        a0_ref[:, pl.ds(pl.multiple_of(g * 256, 256), 256)] = jnp.concatenate(own, axis=1) * SCALE
        return carry

    lax.fori_loop(0, ch // group, work, 0)

    lanes = ch * r
    block = min(lanes, 1024)

    def gram_block(i, gram):
        at = pl.ds(pl.multiple_of(i * block, block), block)
        a0 = a0_ref[:, at]
        a1_terms = split3(a0 / dc_ref[:, at])
        az_ref[:, at] = jnp.concatenate(a1_terms[:2], axis=0)
        right = jnp.concatenate(a1_terms + split3(a0), axis=0)
        left = jnp.concatenate([zhm_ref[:, at], zl_ref[:, at], right[: 3 * k]], axis=0)
        return gram + lax.dot_general(left, right, NT, preferred_element_type=F32)

    gram = lax.fori_loop(0, lanes // block, gram_block, jnp.zeros((9 * k, 6 * k), F32))
    ta1 = block_sum(gram[: 6 * k, : 3 * k], 2 * k, k)
    ta0 = block_sum(gram[: 6 * k, 3 * k :], 2 * k, k)
    aa = block_sum(gram[6 * k :, : 3 * k], k, k)
    gt = gt_ref[...]
    parts = [ta1[k:], gt[:, : 2 * k], ta0[k:], ta1[:k], gt[:, 2 * k :], aa, jnp.zeros((k, k), F32)]
    sums_ref[...] = jnp.concatenate(parts, axis=1)


def spread(x, i):
    return jnp.broadcast_to(x[:, i : i + 1], (x.shape[0], 128))


def finish_kernel(total, sums_ref, az_ref, zhm_ref, out_ref, ritz_ref):
    ch, k, r = out_ref.shape
    s = sums_ref[...]
    row = lax.broadcasted_iota(jnp.int32, (k, 128), 0)
    cols = [spread(s, 2 * k + i) for i in range(k)]
    x = s
    for i in range(k):
        scale = 1.0 / cols[i][i : i + 1]
        pivot = x[i : i + 1] * scale
        x = jnp.where(row == i, pivot, x - cols[i] * pivot)
        for j in range(i + 1, k):
            part = cols[j][i : i + 1] * scale
            cols[j] = jnp.where(row == i, part, cols[j] - cols[i] * part)
    coef = x[:, 3 * k : 4 * k]
    eye = lax.broadcasted_iota(jnp.int32, (k, k), 0) == lax.broadcasted_iota(jnp.int32, (k, k), 1)
    ritz_ref[...] = jnp.sum(jnp.where(eye, coef, 0.0), axis=0, keepdims=True) * (1.0 / SCALE)
    s1, b1 = s[:, :k], s[:, k : 2 * k]
    s2, b2, aa = s[:, 4 * k : 5 * k], s[:, 5 * k : 6 * k], s[:, 6 * k : 7 * k]
    known = jnp.concatenate([x[:, :k], s1, s2], axis=0)
    known = known - dot32(jnp.concatenate([x[:, k : 2 * k], b1, b2], axis=0), coef)
    mix, corr, weighted = known[:k], known[k : 2 * k], known[2 * k :]
    gram = aa - dot32(
        jnp.concatenate([s2, coef, corr], axis=0), jnp.concatenate([coef, weighted, mix], axis=0), TN
    )
    cols = [spread(gram, i) for i in range(k)]
    pad = jnp.zeros((k, 128 - 3 * k), F32)
    x = jnp.concatenate([eye.astype(F32), -coef.T, -mix.T, pad], axis=1)
    for i in range(k):
        pivot = cols[i][i : i + 1]
        scale = 1.0 / pivot
        below = jnp.where(row > i, cols[i] * scale, 0.0)
        pivot_row = x[i : i + 1]
        x = jnp.where(row == i, pivot_row * (lax.rsqrt(pivot) * (total ** 0.5)), x - below * pivot_row)
        for j in range(i + 1, k):
            cols[j] = cols[j] - below * cols[j][i : i + 1]
    hi, mid, _ = split3(x[:, : 3 * k])
    lhs = jnp.concatenate([hi, hi, mid], axis=1)
    block = min(ch * r, 1024)

    def result(b, carry):
        at = pl.ds(pl.multiple_of(b * block, block), block)
        x_hi = jnp.concatenate([az_ref[:k, at], zhm_ref[: 2 * k, at]], axis=0)
        x_mid = jnp.concatenate([az_ref[k:, at], zhm_ref[2 * k :, at]], axis=0)
        new = lax.dot_general(
            lhs, jnp.concatenate([x_hi, x_mid, x_hi], axis=0), NN, preferred_element_type=F32
        )
        for i in range(block // r):
            out_ref[b * (block // r) + i] = new[:, i * r : (i + 1) * r]
        return carry

    lax.fori_loop(0, ch * r // block, result, 0)


def chip_pairs(pick):
    n_chan, n_rad = lax.axis_size("chan"), lax.axis_size("rad")
    pairs = []
    for c in range(n_chan):
        for r in range(n_rad):
            distance = pick[r % 2]
            if distance:
                pairs.append((c * n_rad + r, (c ^ distance) * n_rad + r))
    return pairs


def sum_everywhere(x):
    n_chan, n_rad = lax.axis_size("chan"), lax.axis_size("rad")
    step = 1
    while step < n_rad:
        x = x + swap(x, "rad", step)
        step *= 2
    even = lax.axis_index("rad") % 2 == 0
    step = 1
    while step < n_chan:
        first = lax.ppermute(x, ("chan", "rad"), chip_pairs((step, 2 * step)))
        other = lax.ppermute(x, ("chan", "rad"), chip_pairs((0, 3 * step)))
        x = first + jnp.where(even, x, other)
        x = x + swap(x, "rad", 1)
        step *= 4
    return x


def own_share(trial_block):
    n_rad = lax.axis_size("rad")
    ch, k, r = trial_block.shape
    me = lax.axis_index("rad")
    rounded = trial_block.astype(BF16).reshape(n_rad, ch // n_rad, k, r)
    got = []
    for d in range(n_rad):
        part = lax.dynamic_index_in_dim(rounded, me ^ d, 0, keepdims=False)
        got.append(swap(part, "rad", d) if d else part)
    lanes = []
    for c in range(n_rad):
        x = got[0]
        for d in range(1, n_rad):
            x = jnp.where(me ^ d == c, got[d], x)
        lanes.append(x)
    return jnp.concatenate(lanes, axis=2)


def body(trial_block, ham_blocks, partners, stored_at, precond_diag):
    n_chan, n_rad = lax.axis_size("chan"), lax.axis_size("rad")
    ch, k, r = trial_block.shape
    ncoup, splines = ham_blocks.shape[1], ham_blocks.shape[3]
    lanes = ch * r
    total = float(n_chan * n_rad * lanes)
    share, nz = ch // n_rad, n_chan // 4

    own = own_share(trial_block)
    barrier = lax.optimization_barrier
    smem = pl.BlockSpec(memory_space=pltpu.SMEM)
    any_ = pl.BlockSpec(memory_space=pl.ANY)
    whole = pl.BlockSpec(memory_space=pltpu.VMEM)

    def near_of(x):
        return plane_swap(x, (1, 2))

    def far_of(x, near):
        half = jnp.stack([x, near], axis=1)
        return half, plane_swap(half, (2, 1))

    def to_cores(x):
        return [swap(x, "rad", c) for c in range(1, n_rad)]

    groups = z_groups(nz)
    z1 = swap(own, "chan", 4)[None]
    z2 = jnp.stack([swap(own, "chan", 4 * z) for z in groups[2]])
    near0 = near_of(own[None])
    near0, z1 = barrier((near0, z1))
    half0, far0 = far_of(own[None], near0)
    near1 = near_of(z1)
    z2, near1 = barrier((z2, near1))
    z3 = swap(z2, "chan", 4)
    near2 = near_of(z2)
    half1, far1 = far_of(z1, near1)
    near2, far0 = barrier((near2, far0))
    half2, far2 = far_of(z2, near2)
    z3, far0 = barrier((z3, far0))
    near3 = near_of(z3)
    c_half0, c_far0, c_half1 = to_cores(half0), to_cores(far0), to_cores(half1)
    inputs = (trial_block, precond_diag, partners, stored_at, ham_blocks)
    inputs, far1 = barrier((inputs, far1))
    trial_block, precond_diag, partners, stored_at, ham_blocks = inputs
    ham, rows, zhm, zl, dc, gram_t = pl.pallas_call(
        functools.partial(prepare_kernel, n_chan, n_rad),
        in_specs=[whole] * 4 + [any_],
        out_specs=[whole] * 6,
        out_shape=[
            pltpu.VMEM(ham_blocks.shape, BF16),
            jax.ShapeDtypeStruct((ch, ncoup), jnp.int32),
            pltpu.VMEM((4 * k, lanes), BF16),
            pltpu.VMEM((2 * k, lanes), BF16),
            pltpu.VMEM((1, lanes), F32),
            pltpu.VMEM((k, 3 * k), F32),
        ],
        scratch_shapes=[pltpu.SemaphoreType.DMA],
        compiler_params=pltpu.CompilerParams(vmem_limit_bytes=VMEM_LIMIT),
        name="prepare",
    )(trial_block, precond_diag, partners, stored_at.reshape(-1, 128), in_hbm(ham_blocks))
    near3, far1, c_half0, c_far0, c_half1 = barrier((near3, far1, c_half0, c_far0, c_half1))
    half3, far3 = far_of(z3, near3)
    c_far1, c_half2, c_half3 = to_cores(far1), to_cores(half2), to_cores(half3)
    c_far2 = to_cores(far2)

    late = jnp.zeros_like(half3)
    table = [half0, far0, half1, far1, half2, far2, half3, late]
    for c in range(n_rad - 1):
        table += [c_half0[c], c_far0[c], c_half1[c], c_far1[c], c_half2[c], c_far2[c], c_half3[c], late]
    table = jnp.concatenate(
        [jnp.concatenate([table[i], table[i + 1]], axis=1) for i in range(0, len(table), 2)]
    )
    table, far3, ham, rows = barrier((table, far3, ham, rows))
    for c, x in enumerate([far3] + to_cores(far3)):
        at = c * nz + nz - len(groups[3])
        table = lax.dynamic_update_slice(table, x, (at, 2, 0, 0, 0))
    table = table.reshape(n_chan * ch, k, splines)

    az, sums = pl.pallas_call(
        apply_kernel,
        in_specs=[smem] + [whole] * 6,
        out_specs=[whole, whole],
        out_shape=[
            pltpu.VMEM((2 * k, lanes), BF16),
            jax.ShapeDtypeStruct((k, 8 * k), F32),
        ],
        scratch_shapes=[pltpu.VMEM((k, lanes), F32)],
        compiler_params=pltpu.CompilerParams(vmem_limit_bytes=VMEM_LIMIT),
        name="apply",
    )(rows, in_vmem(ham), in_vmem(table), in_vmem(zhm), in_vmem(zl), in_vmem(dc), gram_t)

    sums = sum_everywhere(sums)
    new_block, ritz = pl.pallas_call(
        functools.partial(finish_kernel, total),
        out_shape=[
            jax.ShapeDtypeStruct((ch, k, r), F32),
            jax.ShapeDtypeStruct((1, k), F32),
        ],
        compiler_params=pltpu.CompilerParams(vmem_limit_bytes=VMEM_LIMIT),
        name="finish",
    )(sums, in_vmem(az), in_vmem(zhm))
    return (new_block, ritz.reshape(k))


def solution(mesh):
    return jax.shard_map(
        body,
        mesh=mesh,
        in_specs=(
            P("chan", None, "rad"),
            P("chan", None, "rad", None),
            P("chan", None),
            P(),
            P("chan", "rad"),
        ),
        out_specs=(P("chan", None, "rad"), P()),
        check_vma=False,
    )
```

```python
import functools

import jax
import jax.numpy as jnp
from jax import lax
from jax.experimental import pallas as pl
from jax.experimental.pallas import tpu as pltpu
from jax.sharding import PartitionSpec as P

SCALE = 2.0 ** -8
F32 = jnp.float32
BF16 = jnp.bfloat16
NT = (((1,), (1,)), ((), ()))
TN = (((0,), (0,)), ((), ()))
NN = (((1,), (0,)), ((), ()))
VMEM_LIMIT = 4 * 1024 * 1024


def swap(x, axis, distance):
    n = lax.axis_size(axis)
    return lax.ppermute(x, axis, [(i, i ^ distance) for i in range(n)])


def plane_swap(x, order):
    n_chan, n_rad = lax.axis_size("chan"), lax.axis_size("rad")
    pairs = []
    for c in range(n_chan):
        for r in range(n_rad):
            pairs.append((c * n_rad + r, (c ^ order[r % 2]) * n_rad + r))
    return lax.ppermute(x, ("chan", "rad"), pairs)


def table_place(z, part, nz):
    some, odd = nz // 2, nz // 2 - 1
    is_odd = (z & 1 == 1) & (z > 1)
    i = jnp.where(is_odd, (z - 3) >> 1, jnp.where(z == 1, 0, z >> 1))
    start = 2 + 2 * some
    here = jnp.where(is_odd, start + i, 2 + i)
    near = jnp.where(is_odd, start + odd + 2 + i, 2 + some + i)
    far = start + 2 * odd + 2 + (some + odd) * (part & 1) + jnp.where(is_odd, some + i, i)
    own = jnp.where(part < 2, part, start + odd + (part & 1))
    return jnp.where(z == 0, own, jnp.where(part == 0, here, jnp.where(part == 1, near, far)))


def in_vmem(x):
    return pltpu.with_memory_space_constraint(x, pltpu.VMEM)


def in_hbm(x):
    return pltpu.with_memory_space_constraint(x, pltpu.HBM)


def split3(x):
    hi = x.astype(BF16)
    rest = x - hi.astype(F32)
    mid = rest.astype(BF16)
    return hi, mid, (rest - mid.astype(F32)).astype(BF16)


def dot32(x, y, dims=NN):
    return lax.dot_general(x, y, dims, precision=lax.Precision.HIGHEST, preferred_element_type=F32)


def block_sum(g, rows, cols):
    g = sum(g[i : i + rows] for i in range(0, g.shape[0], rows))
    return sum(g[:, i : i + cols] for i in range(0, g.shape[1], cols))


def prepare_kernel(
    n_chan, n_rad, t_ref, d_ref, partners_ref, stored_ref,
    rows_ref, zhm_ref, zl_ref, dc_ref, gram_ref,
):
    ch, k, r = t_ref.shape
    group = 128 // r
    for i in range(ch // group):
        lanes = pl.ds(i * 128, 128)
        t = jnp.concatenate([t_ref[i * group + g] for g in range(group)], axis=1)
        d = jnp.concatenate([d_ref[pl.ds(i * group + g, 1), :] for g in range(group)], axis=1)
        dc_ref[:, lanes] = d
        hi, mid, lo = split3(jnp.concatenate([t / d, t], axis=0))
        zhm_ref[:, lanes] = jnp.concatenate([hi, mid], axis=0)
        zl_ref[:, lanes] = lo
    z = jnp.concatenate([zhm_ref[...], zl_ref[...]], axis=0)
    g = block_sum(lax.dot_general(z, z, NT, preferred_element_type=F32), 2 * k, 2 * k)
    gram_ref[...] = jnp.concatenate([g[k:, :], g[:k, :k]], axis=1)

    share, nz = ch // n_rad, n_chan // 4
    q = stored_ref[...]
    slot = lax.div(q, ch) ^ lax.axis_index("chan")
    local = lax.rem(q, ch)
    core = lax.div(local, share)
    near = slot & 3
    part = jnp.where((core & 1) == 1, ((near & 1) << 1) | (near >> 1), near)
    place = (core ^ lax.axis_index("rad")) * nz * 4 + table_place(slot >> 2, part, nz)
    place = (place * share + lax.rem(local, share)).astype(F32)
    lane = lax.broadcasted_iota(jnp.int32, (ch, 128), 1)
    columns = []
    for j in range(partners_ref.shape[1]):
        wanted = jnp.broadcast_to(partners_ref[:, j : j + 1], (ch, 128)) - lane
        found = jnp.zeros((ch, 128), F32)
        for c in range(place.shape[0]):
            found = found + jnp.where(wanted == 128 * c, place[c : c + 1], 0.0)
        columns.append(jnp.sum(found, axis=1, keepdims=True))
    rows_ref[...] = jnp.concatenate(columns, axis=1).astype(jnp.int32)


def apply_kernel(
    rows_ref, ham_hbm, zhm_ref, zl_ref, dc_ref, gt_ref, *rest
):
    pieces = rest[:-6]
    az_ref, sums_ref, a0_ref, ham_ref, table_ref, sems = rest[-6:]
    ch, ncoup, r, splines = ham_ref.shape
    k = zl_ref.shape[0] // 2
    group = 8

    def load(g):
        at = pl.ds(g * group, group)
        return pltpu.make_async_copy(ham_hbm.at[at], ham_ref.at[at], sems.at[g])

    for g in range(ch // group):
        load(g).start()

    at = 0
    for piece in pieces:
        count, share = piece.shape[:2]

        def place(i, carry, piece=piece, at=at, share=share):
            table_ref[pl.ds(at + i * share, share)] = piece[i]
            return carry

        lax.fori_loop(0, count, place, 0)
        at += count * share

    def work(g, carry):
        load(g).wait()
        products = []
        for i in range(group):
            p = g * group + i
            right = jnp.concatenate([table_ref[rows_ref[p, j]] for j in range(ncoup)], axis=1)
            left = jnp.concatenate([ham_ref[p, j] for j in range(ncoup)], axis=1)
            products.append(lax.dot_general(left, right, NT, preferred_element_type=F32))
        turned = (jnp.concatenate(products, axis=1) * SCALE).T
        own = [turned[i * k : (i + 1) * k] for i in range(group)]
        at = pl.ds(pl.multiple_of(g * group * r, 128), group * r)
        a0_ref[:, at] = jnp.concatenate(own, axis=1)
        return carry

    lax.fori_loop(0, ch // group, work, 0)

    lanes = ch * r
    block = min(lanes, 1024)

    def gram_block(i, gram):
        at = pl.ds(pl.multiple_of(i * block, block), block)
        a0 = a0_ref[:, at]
        a1_terms = split3(a0 / dc_ref[:, at])
        az_ref[:, at] = jnp.concatenate(a1_terms[:2], axis=0)
        right = jnp.concatenate(a1_terms + split3(a0), axis=0)
        left = jnp.concatenate([zhm_ref[:, at], zl_ref[:, at], right[: 3 * k]], axis=0)
        return gram + lax.dot_general(left, right, NT, preferred_element_type=F32)

    gram = lax.fori_loop(0, lanes // block, gram_block, jnp.zeros((9 * k, 6 * k), F32))
    ta1 = block_sum(gram[: 6 * k, : 3 * k], 2 * k, k)
    ta0 = block_sum(gram[: 6 * k, 3 * k :], 2 * k, k)
    aa = block_sum(gram[6 * k :, : 3 * k], k, k)
    gt = gt_ref[...]
    parts = [ta1[k:], gt[:, : 2 * k], ta0[k:], ta1[:k], gt[:, 2 * k :], aa, jnp.zeros((k, k), F32)]
    sums_ref[...] = jnp.concatenate(parts, axis=1)


def spread(x, i):
    return jnp.broadcast_to(x[:, i : i + 1], (x.shape[0], 128))


def finish_kernel(total, sums_ref, az_ref, zhm_ref, out_ref, ritz_ref):
    ch, k, r = out_ref.shape
    s = sums_ref[...]
    row = lax.broadcasted_iota(jnp.int32, (k, 128), 0)
    cols = [spread(s, 2 * k + i) for i in range(k)]
    x = s
    for i in range(k):
        scale = 1.0 / cols[i][i : i + 1]
        pivot = x[i : i + 1] * scale
        x = jnp.where(row == i, pivot, x - cols[i] * pivot)
        for j in range(i + 1, k):
            part = cols[j][i : i + 1] * scale
            cols[j] = jnp.where(row == i, part, cols[j] - cols[i] * part)
    coef = x[:, 3 * k : 4 * k]
    eye = lax.broadcasted_iota(jnp.int32, (k, k), 0) == lax.broadcasted_iota(jnp.int32, (k, k), 1)
    ritz_ref[...] = jnp.sum(jnp.where(eye, coef, 0.0), axis=0, keepdims=True) * (1.0 / SCALE)
    s1, b1 = s[:, :k], s[:, k : 2 * k]
    s2, b2, aa = s[:, 4 * k : 5 * k], s[:, 5 * k : 6 * k], s[:, 6 * k : 7 * k]
    known = jnp.concatenate([x[:, :k], s1, s2], axis=0)
    known = known - dot32(jnp.concatenate([x[:, k : 2 * k], b1, b2], axis=0), coef)
    mix, corr, weighted = known[:k], known[k : 2 * k], known[2 * k :]
    gram = aa - dot32(
        jnp.concatenate([s2, coef, corr], axis=0), jnp.concatenate([coef, weighted, mix], axis=0), TN
    )
    cols = [spread(gram, i) for i in range(k)]
    pad = jnp.zeros((k, 128 - 3 * k), F32)
    x = jnp.concatenate([eye.astype(F32), -coef.T, -mix.T, pad], axis=1)
    for i in range(k):
        pivot = cols[i][i : i + 1]
        scale = 1.0 / pivot
        below = jnp.where(row > i, cols[i] * scale, 0.0)
        pivot_row = x[i : i + 1]
        x = jnp.where(row == i, pivot_row * (lax.rsqrt(pivot) * (total ** 0.5)), x - below * pivot_row)
        for j in range(i + 1, k):
            cols[j] = cols[j] - below * cols[j][i : i + 1]
    hi, mid, _ = split3(x[:, : 3 * k])
    lhs = jnp.concatenate([hi, hi, mid], axis=1)
    block = min(ch * r, 1024)

    def result(b, carry):
        at = pl.ds(pl.multiple_of(b * block, block), block)
        x_hi = jnp.concatenate([az_ref[:k, at], zhm_ref[: 2 * k, at]], axis=0)
        x_mid = jnp.concatenate([az_ref[k:, at], zhm_ref[2 * k :, at]], axis=0)
        new = lax.dot_general(
            lhs, jnp.concatenate([x_hi, x_mid, x_hi], axis=0), NN, preferred_element_type=F32
        )
        for i in range(block // r):
            out_ref[b * (block // r) + i] = new[:, i * r : (i + 1) * r]
        return carry

    lax.fori_loop(0, ch * r // block, result, 0)


def sum_everywhere(x):
    n_chan, n_rad = lax.axis_size("chan"), lax.axis_size("rad")
    step = 1
    while step < n_rad:
        x = x + swap(x, "rad", step)
        step *= 2
    step = 1
    while step < n_chan:
        starts = [c for c in range(n_chan) if (c // step) % 4 == 0]
        groups = [[c + i * step for i in range(4)] for c in starts]
        x = lax.psum(x, "chan", axis_index_groups=groups)
        step *= 4
    return x


def own_share(trial_block):
    n_rad = lax.axis_size("rad")
    ch, k, r = trial_block.shape
    me = lax.axis_index("rad")
    rounded = trial_block.astype(BF16).reshape(n_rad, ch // n_rad, k, r)
    got = []
    for d in range(n_rad):
        part = lax.dynamic_index_in_dim(rounded, me ^ d, 0, keepdims=False)
        got.append(swap(part, "rad", d) if d else part)
    lanes = []
    for c in range(n_rad):
        x = got[0]
        for d in range(1, n_rad):
            x = jnp.where(me ^ d == c, got[d], x)
        lanes.append(x)
    return jnp.concatenate(lanes, axis=2)


def body(trial_block, ham_blocks, partners, stored_at, precond_diag):
    n_chan, n_rad = lax.axis_size("chan"), lax.axis_size("rad")
    ch, k, r = trial_block.shape
    ncoup, splines = ham_blocks.shape[1], ham_blocks.shape[3]
    lanes = ch * r
    total = float(n_chan * n_rad * lanes)
    share, nz = ch // n_rad, n_chan // 4

    own = own_share(trial_block)
    barrier = lax.optimization_barrier
    smem = pl.BlockSpec(memory_space=pltpu.SMEM)
    any_ = pl.BlockSpec(memory_space=pl.ANY)
    whole = pl.BlockSpec(memory_space=pltpu.VMEM)

    def near_of(x):
        return plane_swap(x, (1, 2))

    def far_of(x, near):
        return plane_swap(jnp.concatenate([x, near]), (2, 1))

    def in_cores(x):
        return [x] + [swap(x, "rad", c) for c in range(1, n_rad)]

    own = own[None]
    z_even = jnp.concatenate([swap(own, "chan", 4 * z) for z in range(2, nz, 2)])
    z1 = swap(own, "chan", 4)
    near0 = near_of(own)
    z_even, z1, near0 = barrier((z_even, z1, near0))
    z_odd = swap(z_even, "chan", 4)
    some = jnp.concatenate([z1, z_even])
    near1 = near_of(some)
    far0 = far_of(own, near0)
    z_odd, near1 = barrier((z_odd, near1))
    near2 = near_of(z_odd)
    early = in_cores(jnp.concatenate([own, near0, some, near1, z_odd]))
    near2, far0, early = barrier((near2, far0, early))
    far1 = far_of(jnp.concatenate([some, z_odd]), jnp.concatenate([near1, near2]))
    far0 = in_cores(far0)

    inputs = (trial_block, precond_diag, partners, stored_at)
    inputs, near2 = barrier((inputs, near2))
    trial_block, precond_diag, partners, stored_at = inputs
    rows, zhm, zl, dc, gram_t = pl.pallas_call(
        functools.partial(prepare_kernel, n_chan, n_rad),
        in_specs=[whole] * 4,
        out_specs=[whole] * 5,
        out_shape=[
            jax.ShapeDtypeStruct((ch, ncoup), jnp.int32),
            pltpu.VMEM((4 * k, lanes), BF16),
            pltpu.VMEM((2 * k, lanes), BF16),
            pltpu.VMEM((1, lanes), F32),
            pltpu.VMEM((k, 3 * k), F32),
        ],
        compiler_params=pltpu.CompilerParams(vmem_limit_bytes=VMEM_LIMIT),
        name="prepare",
    )(trial_block, precond_diag, partners, stored_at.reshape(-1, 128))

    far0, far1, rows = barrier((far0, far1, rows))
    last = in_cores(jnp.concatenate([near2, far1]))
    pieces = [in_vmem(x) for trio in zip(early, far0, last) for x in trio]

    az, sums = pl.pallas_call(
        apply_kernel,
        in_specs=[smem, any_] + [whole] * (4 + len(pieces)),
        out_specs=[whole, whole],
        out_shape=[
            pltpu.VMEM((2 * k, lanes), BF16),
            jax.ShapeDtypeStruct((k, 8 * k), F32),
        ],
        scratch_shapes=[
            pltpu.VMEM((k, lanes), F32),
            pltpu.VMEM(ham_blocks.shape, BF16),
            pltpu.VMEM((n_chan * ch, k, splines), BF16),
            pltpu.SemaphoreType.DMA((ch // 8,)),
        ],
        compiler_params=pltpu.CompilerParams(vmem_limit_bytes=VMEM_LIMIT + 12 * 1024 * 1024),
        name="apply",
    )(rows, in_hbm(ham_blocks), in_vmem(zhm), in_vmem(zl), in_vmem(dc), gram_t, *pieces)

    sums = sum_everywhere(sums)
    new_block, ritz = pl.pallas_call(
        functools.partial(finish_kernel, total),
        out_shape=[
            jax.ShapeDtypeStruct((ch, k, r), F32),
            jax.ShapeDtypeStruct((1, k), F32),
        ],
        compiler_params=pltpu.CompilerParams(vmem_limit_bytes=VMEM_LIMIT),
        name="finish",
    )(sums, in_vmem(az), in_vmem(zhm))
    return (new_block, ritz.reshape(k))


def solution(mesh):
    return jax.shard_map(
        body,
        mesh=mesh,
        in_specs=(
            P("chan", None, "rad"),
            P("chan", None, "rad", None),
            P("chan", None),
            P(),
            P("chan", "rad"),
        ),
        out_specs=(P("chan", None, "rad"), P()),
        check_vma=False,
    )
```

```python
import functools

import jax
import jax.numpy as jnp
from jax import lax
from jax.experimental import pallas as pl
from jax.experimental.pallas import tpu as pltpu
from jax.sharding import PartitionSpec as P

SCALE = 2.0 ** -8
F32 = jnp.float32
BF16 = jnp.bfloat16
NT = (((1,), (1,)), ((), ()))
TN = (((0,), (0,)), ((), ()))
NN = (((1,), (0,)), ((), ()))
VMEM_LIMIT = 4 * 1024 * 1024


def swap(x, axis, distance):
    n = lax.axis_size(axis)
    return lax.ppermute(x, axis, [(i, i ^ distance) for i in range(n)])


def plane_swap(x, order):
    n_chan, n_rad = lax.axis_size("chan"), lax.axis_size("rad")
    pairs = []
    for c in range(n_chan):
        for r in range(n_rad):
            pairs.append((c * n_rad + r, (c ^ order[r % 2]) * n_rad + r))
    return lax.ppermute(x, ("chan", "rad"), pairs)


def in_vmem(x):
    return pltpu.with_memory_space_constraint(x, pltpu.VMEM)


def in_hbm(x):
    return pltpu.with_memory_space_constraint(x, pltpu.HBM)


def split3(x):
    hi = x.astype(BF16)
    rest = x - hi.astype(F32)
    mid = rest.astype(BF16)
    return hi, mid, (rest - mid.astype(F32)).astype(BF16)


def dot32(x, y, dims=NN):
    return lax.dot_general(x, y, dims, precision=lax.Precision.HIGHEST, preferred_element_type=F32)


def block_sum(g, rows, cols):
    g = sum(g[i : i + rows] for i in range(0, g.shape[0], rows))
    return sum(g[:, i : i + cols] for i in range(0, g.shape[1], cols))


def prepare_kernel(
    n_chan, n_rad, t_ref, d_ref, partners_ref, stored_ref, ham_hbm,
    ham_ref, rows_ref, zhm_ref, zl_ref, dc_ref, gram_ref, sem,
):
    copy = pltpu.make_async_copy(ham_hbm, ham_ref, sem)
    copy.start()
    ch, k, r = t_ref.shape
    group = 128 // r
    for i in range(ch // group):
        lanes = pl.ds(i * 128, 128)
        t = jnp.concatenate([t_ref[i * group + g] for g in range(group)], axis=1)
        d = jnp.concatenate([d_ref[pl.ds(i * group + g, 1), :] for g in range(group)], axis=1)
        dc_ref[:, lanes] = d
        hi, mid, lo = split3(jnp.concatenate([t / d, t], axis=0))
        zhm_ref[:, lanes] = jnp.concatenate([hi, mid], axis=0)
        zl_ref[:, lanes] = lo
    z = jnp.concatenate([zhm_ref[...], zl_ref[...]], axis=0)
    g = block_sum(lax.dot_general(z, z, NT, preferred_element_type=F32), 2 * k, 2 * k)
    gram_ref[...] = jnp.concatenate([g[k:, :], g[:k, :k]], axis=1)

    share, nz = ch // n_rad, n_chan // 4
    q = stored_ref[...]
    owner, local = lax.div(q, ch), lax.rem(q, ch)
    core = lax.div(local, share)
    apart = (owner ^ lax.axis_index("chan")) & 3
    part = jnp.where((core & 1) == 1, ((apart & 1) << 1) | (apart >> 1), apart)
    place = ((core ^ lax.axis_index("rad")) * 4 + part) * nz + (owner >> 2)
    place = (place * share + lax.rem(local, share)).astype(F32)
    lane = lax.broadcasted_iota(jnp.int32, (ch, 128), 1)
    columns = []
    for j in range(partners_ref.shape[1]):
        wanted = jnp.broadcast_to(partners_ref[:, j : j + 1], (ch, 128)) - lane
        found = jnp.zeros((ch, 128), F32)
        for c in range(place.shape[0]):
            found = found + jnp.where(wanted == 128 * c, place[c : c + 1], 0.0)
        columns.append(jnp.sum(found, axis=1, keepdims=True))
    rows_ref[...] = jnp.concatenate(columns, axis=1).astype(jnp.int32)
    copy.wait()


def apply_kernel(rows_ref, ham_ref, table_ref, zhm_ref, zl_ref, dc_ref, gt_ref, az_ref, sums_ref, a0_ref):
    ch, ncoup, r, splines = ham_ref.shape
    k = zl_ref.shape[0] // 2
    group = 256 // r

    def work(g, carry):
        left, right = [], []
        for i in range(group):
            p = g * group + i
            left.append(
                jnp.concatenate([table_ref[rows_ref[p, j]] for j in range(ncoup)], axis=1)
            )
            right.append(jnp.concatenate([ham_ref[p, j] for j in range(ncoup)], axis=1))
        product = lax.dot_general(
            jnp.concatenate(left, axis=0),
            jnp.concatenate(right, axis=0),
            NT,
            preferred_element_type=F32,
        )
        own = [product[i * k : (i + 1) * k, i * r : (i + 1) * r] for i in range(group)]
        a0_ref[:, pl.ds(pl.multiple_of(g * 256, 256), 256)] = jnp.concatenate(own, axis=1) * SCALE
        return carry

    lax.fori_loop(0, ch // group, work, 0, unroll=min(2, ch // group))

    lanes = ch * r
    block = min(lanes, 1024)

    def gram_block(i, gram):
        at = pl.ds(pl.multiple_of(i * block, block), block)
        a0 = a0_ref[:, at]
        a1_terms = split3(a0 / dc_ref[:, at])
        az_ref[:, at] = jnp.concatenate(a1_terms[:2], axis=0)
        right = jnp.concatenate(a1_terms + split3(a0), axis=0)
        left = jnp.concatenate([zhm_ref[:, at], zl_ref[:, at], right[: 3 * k]], axis=0)
        return gram + lax.dot_general(left, right, NT, preferred_element_type=F32)

    gram = lax.fori_loop(0, lanes // block, gram_block, jnp.zeros((9 * k, 6 * k), F32))
    ta1 = block_sum(gram[: 6 * k, : 3 * k], 2 * k, k)
    ta0 = block_sum(gram[: 6 * k, 3 * k :], 2 * k, k)
    aa = block_sum(gram[6 * k :, : 3 * k], k, k)
    gt = gt_ref[...]
    parts = [ta1[k:], gt[:, : 2 * k], ta0[k:], ta1[:k], gt[:, 2 * k :], aa, jnp.zeros((k, k), F32)]
    sums_ref[...] = jnp.concatenate(parts, axis=1)


def spread(x, i):
    return jnp.broadcast_to(x[:, i : i + 1], (x.shape[0], 128))


def finish_kernel(total, sums_ref, az_ref, zhm_ref, out_ref, ritz_ref):
    ch, k, r = out_ref.shape
    s = sums_ref[...]
    row = lax.broadcasted_iota(jnp.int32, (k, 128), 0)
    cols = [spread(s, 2 * k + i) for i in range(k)]
    x = s
    for i in range(k):
        scale = 1.0 / cols[i][i : i + 1]
        pivot = x[i : i + 1] * scale
        x = jnp.where(row == i, pivot, x - cols[i] * pivot)
        for j in range(i + 1, k):
            part = cols[j][i : i + 1] * scale
            cols[j] = jnp.where(row == i, part, cols[j] - cols[i] * part)
    coef = x[:, 3 * k : 4 * k]
    eye = lax.broadcasted_iota(jnp.int32, (k, k), 0) == lax.broadcasted_iota(jnp.int32, (k, k), 1)
    ritz_ref[...] = jnp.sum(jnp.where(eye, coef, 0.0), axis=0, keepdims=True) * (1.0 / SCALE)
    s1, b1 = s[:, :k], s[:, k : 2 * k]
    s2, b2, aa = s[:, 4 * k : 5 * k], s[:, 5 * k : 6 * k], s[:, 6 * k : 7 * k]
    known = jnp.concatenate([x[:, :k], s1, s2], axis=0)
    known = known - dot32(jnp.concatenate([x[:, k : 2 * k], b1, b2], axis=0), coef)
    mix, corr, weighted = known[:k], known[k : 2 * k], known[2 * k :]
    gram = aa - dot32(
        jnp.concatenate([s2, coef, corr], axis=0), jnp.concatenate([coef, weighted, mix], axis=0), TN
    )
    cols = [spread(gram, i) for i in range(k)]
    pad = jnp.zeros((k, 128 - 3 * k), F32)
    x = jnp.concatenate([eye.astype(F32), -coef.T, -mix.T, pad], axis=1)
    for i in range(k):
        pivot = cols[i][i : i + 1]
        scale = 1.0 / pivot
        below = jnp.where(row > i, cols[i] * scale, 0.0)
        pivot_row = x[i : i + 1]
        x = jnp.where(row == i, pivot_row * (lax.rsqrt(pivot) * (total ** 0.5)), x - below * pivot_row)
        for j in range(i + 1, k):
            cols[j] = cols[j] - below * cols[j][i : i + 1]
    hi, mid, _ = split3(x[:, : 3 * k])
    lhs = jnp.concatenate([hi, hi, mid], axis=1)
    block = min(ch * r, 1024)

    def result(b, carry):
        at = pl.ds(pl.multiple_of(b * block, block), block)
        x_hi = jnp.concatenate([az_ref[:k, at], zhm_ref[: 2 * k, at]], axis=0)
        x_mid = jnp.concatenate([az_ref[k:, at], zhm_ref[2 * k :, at]], axis=0)
        new = lax.dot_general(
            lhs, jnp.concatenate([x_hi, x_mid, x_hi], axis=0), NN, preferred_element_type=F32
        )
        for i in range(block // r):
            out_ref[b * (block // r) + i] = new[:, i * r : (i + 1) * r]
        return carry

    lax.fori_loop(0, ch * r // block, result, 0)


def sum_everywhere(x):
    n_chan, n_rad = lax.axis_size("chan"), lax.axis_size("rad")
    step = 1
    while step < n_rad:
        x = x + swap(x, "rad", step)
        step *= 2
    half = n_chan // 2
    parts = []
    for t in range(half):
        pairs = []
        for c in range(n_chan):
            for r in range(n_rad):
                distance = t + half * (r % 2)
                if distance:
                    pairs.append((c * n_rad + r, (c ^ distance) * n_rad + r))
        parts.append(lax.ppermute(x, ("chan", "rad"), pairs))
    parts[0] = jnp.where(lax.axis_index("rad") % 2 == 0, x, parts[0])
    while len(parts) > 1:
        parts = [parts[i] + parts[i + 1] for i in range(0, len(parts), 2)]
    return parts[0] + swap(parts[0], "rad", 1)


def own_share(trial_block):
    n_rad = lax.axis_size("rad")
    ch, k, r = trial_block.shape
    me = lax.axis_index("rad")
    rounded = trial_block.astype(BF16).reshape(n_rad, ch // n_rad, k, r)
    got = []
    for d in range(n_rad):
        part = lax.dynamic_index_in_dim(rounded, me ^ d, 0, keepdims=False)
        got.append(swap(part, "rad", d) if d else part)
    lanes = []
    for c in range(n_rad):
        x = got[0]
        for d in range(1, n_rad):
            x = jnp.where(me ^ d == c, got[d], x)
        lanes.append(x)
    return jnp.concatenate(lanes, axis=2)


def body(trial_block, ham_blocks, partners, stored_at, precond_diag):
    n_chan, n_rad = lax.axis_size("chan"), lax.axis_size("rad")
    ch, k, r = trial_block.shape
    ncoup, splines = ham_blocks.shape[1], ham_blocks.shape[3]
    lanes = ch * r
    total = float(n_chan * n_rad * lanes)
    share, nz = ch // n_rad, n_chan // 4

    barrier = lax.optimization_barrier
    smem = pl.BlockSpec(memory_space=pltpu.SMEM)
    any_ = pl.BlockSpec(memory_space=pl.ANY)
    whole = pl.BlockSpec(memory_space=pltpu.VMEM)

    def in_cores(x):
        return [x] + [swap(x, "rad", c) for c in range(1, n_rad)]

    own = own_share(trial_block)
    column = lax.all_to_all(
        jnp.broadcast_to(own, (nz,) + own.shape),
        "chan",
        split_axis=0,
        concat_axis=0,
        axis_index_groups=[[i + 4 * z for z in range(nz)] for i in range(4)],
        tiled=True,
    )
    near = plane_swap(column, (1, 2))
    far = plane_swap(column, (2, 1))
    columns = in_cores(column)
    inputs = (trial_block, precond_diag, partners, stored_at, ham_blocks)
    inputs, _ = barrier((inputs, column))
    trial_block, precond_diag, partners, stored_at, ham_blocks = inputs
    ham, rows, zhm, zl, dc, gram_t = pl.pallas_call(
        functools.partial(prepare_kernel, n_chan, n_rad),
        in_specs=[whole] * 4 + [any_],
        out_specs=[whole] * 6,
        out_shape=[
            pltpu.VMEM(ham_blocks.shape, BF16),
            jax.ShapeDtypeStruct((ch, ncoup), jnp.int32),
            pltpu.VMEM((4 * k, lanes), BF16),
            pltpu.VMEM((2 * k, lanes), BF16),
            pltpu.VMEM((1, lanes), F32),
            pltpu.VMEM((k, 3 * k), F32),
        ],
        scratch_shapes=[pltpu.SemaphoreType.DMA],
        compiler_params=pltpu.CompilerParams(vmem_limit_bytes=VMEM_LIMIT),
        name="prepare",
    )(trial_block, precond_diag, partners, stored_at.reshape(-1, 128), in_hbm(ham_blocks))
    near, far, columns, rows = barrier((near, far, columns, rows))
    both = plane_swap(near, (2, 1))
    nears, fars = in_cores(near), in_cores(far)
    both, nears, fars = barrier((both, nears, fars))
    boths = in_cores(both)
    table = jnp.concatenate([x for four in zip(columns, nears, fars, boths) for x in four])
    table = table.reshape(n_chan * ch, k, splines)

    az, sums = pl.pallas_call(
        apply_kernel,
        in_specs=[smem] + [whole] * 6,
        out_specs=[whole, whole],
        out_shape=[
            pltpu.VMEM((2 * k, lanes), BF16),
            jax.ShapeDtypeStruct((k, 8 * k), F32),
        ],
        scratch_shapes=[pltpu.VMEM((k, lanes), F32)],
        compiler_params=pltpu.CompilerParams(vmem_limit_bytes=VMEM_LIMIT),
        name="apply",
    )(rows, in_vmem(ham), in_vmem(table), in_vmem(zhm), in_vmem(zl), in_vmem(dc), gram_t)

    sums = sum_everywhere(sums)
    new_block, ritz = pl.pallas_call(
        functools.partial(finish_kernel, total),
        out_shape=[
            jax.ShapeDtypeStruct((ch, k, r), F32),
            jax.ShapeDtypeStruct((1, k), F32),
        ],
        compiler_params=pltpu.CompilerParams(vmem_limit_bytes=VMEM_LIMIT),
        name="finish",
    )(sums, in_vmem(az), in_vmem(zhm))
    return (new_block, ritz.reshape(k))


def solution(mesh):
    return jax.shard_map(
        body,
        mesh=mesh,
        in_specs=(
            P("chan", None, "rad"),
            P("chan", None, "rad", None),
            P("chan", None),
            P(),
            P("chan", "rad"),
        ),
        out_specs=(P("chan", None, "rad"), P()),
        check_vma=False,
    )
```

```python
import functools

import jax
import jax.numpy as jnp
from jax import lax
from jax.experimental import pallas as pl
from jax.experimental.pallas import tpu as pltpu
from jax.sharding import PartitionSpec as P

SCALE = 2.0 ** -8
F32 = jnp.float32
BF16 = jnp.bfloat16
NT = (((1,), (1,)), ((), ()))
TN = (((0,), (0,)), ((), ()))
NN = (((1,), (0,)), ((), ()))
VMEM_LIMIT = 4 * 1024 * 1024


def swap(x, axis, distance):
    n = lax.axis_size(axis)
    return lax.ppermute(x, axis, [(i, i ^ distance) for i in range(n)])


def plane_swap(x, order):
    n_chan, n_rad = lax.axis_size("chan"), lax.axis_size("rad")
    pairs = []
    for c in range(n_chan):
        for r in range(n_rad):
            pairs.append((c * n_rad + r, (c ^ order[r % 2]) * n_rad + r))
    return lax.ppermute(x, ("chan", "rad"), pairs)


def table_piece(z, part, nz):
    z = z if nz == 4 else jnp.where(z < 2, z, jnp.where((z & 1) == 1, (nz + z - 1) >> 1, 1 + (z >> 1)))
    near = jnp.where(z == 0, nz, nz + 2 + z)
    far = (part & 1) + jnp.where(z == 0, nz + 1, 2 * nz + 1 + z + (part & 1) * (nz - 2))
    return jnp.where(part == 0, z, jnp.where(part == 1, near, far))


def in_vmem(x):
    return pltpu.with_memory_space_constraint(x, pltpu.VMEM)


def in_hbm(x):
    return pltpu.with_memory_space_constraint(x, pltpu.HBM)


def split3(x):
    hi = x.astype(BF16)
    rest = x - hi.astype(F32)
    mid = rest.astype(BF16)
    return hi, mid, (rest - mid.astype(F32)).astype(BF16)


def dot32(x, y, dims=NN):
    return lax.dot_general(x, y, dims, precision=lax.Precision.HIGHEST, preferred_element_type=F32)


def block_sum(g, rows, cols):
    g = sum(g[i : i + rows] for i in range(0, g.shape[0], rows))
    return sum(g[:, i : i + cols] for i in range(0, g.shape[1], cols))


def prepare_kernel(
    n_chan, n_rad, t_ref, d_ref, partners_ref, stored_ref, ham_hbm,
    ham_ref, rows_ref, zhm_ref, zl_ref, dc_ref, gram_ref, sem,
):
    copy = pltpu.make_async_copy(ham_hbm, ham_ref, sem)
    copy.start()
    ch, k, r = t_ref.shape
    group = 128 // r
    for i in range(ch // group):
        lanes = pl.ds(i * 128, 128)
        t = jnp.concatenate([t_ref[i * group + g] for g in range(group)], axis=1)
        d = jnp.concatenate([d_ref[pl.ds(i * group + g, 1), :] for g in range(group)], axis=1)
        dc_ref[:, lanes] = d
        hi, mid, lo = split3(jnp.concatenate([t / d, t], axis=0))
        zhm_ref[:, lanes] = jnp.concatenate([hi, mid], axis=0)
        zl_ref[:, lanes] = lo
    z = jnp.concatenate([zhm_ref[...], zl_ref[...]], axis=0)
    g = block_sum(lax.dot_general(z, z, NT, preferred_element_type=F32), 2 * k, 2 * k)
    gram_ref[...] = jnp.concatenate([g[k:, :], g[:k, :k]], axis=1)

    share, nz = ch // n_rad, n_chan // 4
    q = stored_ref[...]
    owner, local = lax.div(q, ch), lax.rem(q, ch)
    core = lax.div(local, share)
    apart = (owner ^ lax.axis_index("chan")) & 3
    part = jnp.where((core & 1) == 1, ((apart & 1) << 1) | (apart >> 1), apart)
    piece = table_piece((owner ^ lax.axis_index("chan")) >> 2, part, nz)
    place = (core ^ lax.axis_index("rad")) * 4 * nz + piece
    place = (place * share + lax.rem(local, share)).astype(F32)
    lane = lax.broadcasted_iota(jnp.int32, (ch, 128), 1)
    columns = []
    for j in range(partners_ref.shape[1]):
        wanted = jnp.broadcast_to(partners_ref[:, j : j + 1], (ch, 128)) - lane
        found = jnp.zeros((ch, 128), F32)
        for c in range(place.shape[0]):
            found = found + jnp.where(wanted == 128 * c, place[c : c + 1], 0.0)
        columns.append(jnp.sum(found, axis=1, keepdims=True))
    rows_ref[...] = jnp.concatenate(columns, axis=1).astype(jnp.int32)
    copy.wait()


def apply_kernel(rows_ref, ham_ref, table_ref, zhm_ref, zl_ref, dc_ref, gt_ref, az_ref, sums_ref, a0_ref):
    ch, ncoup, r, splines = ham_ref.shape
    k = zl_ref.shape[0] // 2
    group = 256 // r

    def work(g, carry):
        left, right = [], []
        for i in range(group):
            p = g * group + i
            left.append(
                jnp.concatenate([table_ref[rows_ref[p, j]] for j in range(ncoup)], axis=1)
            )
            right.append(jnp.concatenate([ham_ref[p, j] for j in range(ncoup)], axis=1))
        product = lax.dot_general(
            jnp.concatenate(left, axis=0),
            jnp.concatenate(right, axis=0),
            NT,
            preferred_element_type=F32,
        )
        own = [product[i * k : (i + 1) * k, i * r : (i + 1) * r] for i in range(group)]
        a0_ref[:, pl.ds(pl.multiple_of(g * 256, 256), 256)] = jnp.concatenate(own, axis=1) * SCALE
        return carry

    lax.fori_loop(0, ch // group, work, 0, unroll=min(2, ch // group))

    lanes = ch * r
    block = min(lanes, 1024)

    def gram_block(i, gram):
        at = pl.ds(pl.multiple_of(i * block, block), block)
        a0 = a0_ref[:, at]
        a1_terms = split3(a0 / dc_ref[:, at])
        az_ref[:, at] = jnp.concatenate(a1_terms[:2], axis=0)
        right = jnp.concatenate(a1_terms + split3(a0), axis=0)
        left = jnp.concatenate([zhm_ref[:, at], zl_ref[:, at], right[: 3 * k]], axis=0)
        return gram + lax.dot_general(left, right, NT, preferred_element_type=F32)

    gram = lax.fori_loop(0, lanes // block, gram_block, jnp.zeros((9 * k, 6 * k), F32))
    ta1 = block_sum(gram[: 6 * k, : 3 * k], 2 * k, k)
    ta0 = block_sum(gram[: 6 * k, 3 * k :], 2 * k, k)
    aa = block_sum(gram[6 * k :, : 3 * k], k, k)
    gt = gt_ref[...]
    parts = [ta1[k:], gt[:, : 2 * k], ta0[k:], ta1[:k], gt[:, 2 * k :], aa, jnp.zeros((k, k), F32)]
    sums_ref[...] = jnp.concatenate(parts, axis=1)


def spread(x, i):
    return jnp.broadcast_to(x[:, i : i + 1], (x.shape[0], 128))


def finish_kernel(total, sums_ref, az_ref, zhm_ref, out_ref, ritz_ref):
    ch, k, r = out_ref.shape
    s = jnp.sum(sums_ref[...], axis=0)
    row = lax.broadcasted_iota(jnp.int32, (k, 128), 0)
    cols = [spread(s, 2 * k + i) for i in range(k)]
    x = s
    for i in range(k):
        scale = 1.0 / cols[i][i : i + 1]
        pivot = x[i : i + 1] * scale
        x = jnp.where(row == i, pivot, x - cols[i] * pivot)
        for j in range(i + 1, k):
            part = cols[j][i : i + 1] * scale
            cols[j] = jnp.where(row == i, part, cols[j] - cols[i] * part)
    coef = x[:, 3 * k : 4 * k]
    eye = lax.broadcasted_iota(jnp.int32, (k, k), 0) == lax.broadcasted_iota(jnp.int32, (k, k), 1)
    ritz_ref[...] = jnp.sum(jnp.where(eye, coef, 0.0), axis=0, keepdims=True) * (1.0 / SCALE)
    s1, b1 = s[:, :k], s[:, k : 2 * k]
    s2, b2, aa = s[:, 4 * k : 5 * k], s[:, 5 * k : 6 * k], s[:, 6 * k : 7 * k]
    known = jnp.concatenate([x[:, :k], s1, s2], axis=0)
    known = known - dot32(jnp.concatenate([x[:, k : 2 * k], b1, b2], axis=0), coef)
    mix, corr, weighted = known[:k], known[k : 2 * k], known[2 * k :]
    gram = aa - dot32(
        jnp.concatenate([s2, coef, corr], axis=0), jnp.concatenate([coef, weighted, mix], axis=0), TN
    )
    cols = [spread(gram, i) for i in range(k)]
    pad = jnp.zeros((k, 128 - 3 * k), F32)
    x = jnp.concatenate([eye.astype(F32), -coef.T, -mix.T, pad], axis=1)
    for i in range(k):
        pivot = cols[i][i : i + 1]
        scale = 1.0 / pivot
        below = jnp.where(row > i, cols[i] * scale, 0.0)
        pivot_row = x[i : i + 1]
        x = jnp.where(row == i, pivot_row * (lax.rsqrt(pivot) * (total ** 0.5)), x - below * pivot_row)
        for j in range(i + 1, k):
            cols[j] = cols[j] - below * cols[j][i : i + 1]
    hi, mid, _ = split3(x[:, : 3 * k])
    lhs = jnp.concatenate([hi, hi, mid], axis=1)
    block = min(ch * r, 1024)

    def result(b, carry):
        at = pl.ds(pl.multiple_of(b * block, block), block)
        x_hi = jnp.concatenate([az_ref[:k, at], zhm_ref[: 2 * k, at]], axis=0)
        x_mid = jnp.concatenate([az_ref[k:, at], zhm_ref[2 * k :, at]], axis=0)
        new = lax.dot_general(
            lhs, jnp.concatenate([x_hi, x_mid, x_hi], axis=0), NN, preferred_element_type=F32
        )
        for i in range(block // r):
            out_ref[b * (block // r) + i] = new[:, i * r : (i + 1) * r]
        return carry

    lax.fori_loop(0, ch * r // block, result, 0)


def gather_sums(x):
    n_chan, n_rad = lax.axis_size("chan"), lax.axis_size("rad")
    step = 1
    while step < n_rad:
        x = x + swap(x, "rad", step)
        step *= 2
    every = jnp.broadcast_to(x, (n_chan,) + x.shape)
    return lax.all_to_all(every, "chan", split_axis=0, concat_axis=0, tiled=True)


def own_share(trial_block):
    n_rad = lax.axis_size("rad")
    ch, k, r = trial_block.shape
    me = lax.axis_index("rad")
    rounded = trial_block.astype(BF16).reshape(n_rad, ch // n_rad, k, r)
    got = []
    for d in range(n_rad):
        part = lax.dynamic_index_in_dim(rounded, me ^ d, 0, keepdims=False)
        got.append(swap(part, "rad", d) if d else part)
    lanes = []
    for c in range(n_rad):
        x = got[0]
        for d in range(1, n_rad):
            x = jnp.where(me ^ d == c, got[d], x)
        lanes.append(x)
    return jnp.concatenate(lanes, axis=2)


def body(trial_block, ham_blocks, partners, stored_at, precond_diag):
    n_chan, n_rad = lax.axis_size("chan"), lax.axis_size("rad")
    ch, k, r = trial_block.shape
    ncoup, splines = ham_blocks.shape[1], ham_blocks.shape[3]
    lanes = ch * r
    total = float(n_chan * n_rad * lanes)
    share, nz = ch // n_rad, n_chan // 4

    barrier = lax.optimization_barrier
    smem = pl.BlockSpec(memory_space=pltpu.SMEM)
    any_ = pl.BlockSpec(memory_space=pl.ANY)
    whole = pl.BlockSpec(memory_space=pltpu.VMEM)

    def near_of(x):
        return plane_swap(x, (1, 2))

    def far_of(x, near):
        return plane_swap(jnp.concatenate([x, near]), (2, 1))

    def in_cores(x):
        return [x] + [swap(x, "rad", c) for c in range(1, n_rad)]

    own = own_share(trial_block)[None]
    z_even = jnp.concatenate([swap(own, "chan", 4 * z) for z in range(2, nz, 2)])
    z1 = swap(own, "chan", 4)
    near0 = near_of(own)
    z_even, z1, near0 = barrier((z_even, z1, near0))
    some = jnp.concatenate([z1, z_even])
    near1 = near_of(some)
    far0 = far_of(own, near0)
    z_odd = swap(z_even, "chan", 4)
    z_odd, near1, far0 = barrier((z_odd, near1, far0))
    near2 = near_of(z_odd)
    here = jnp.concatenate([some, z_odd])
    early1 = jnp.concatenate([own, here, near0])
    near2, near1, far0, here, early1 = barrier((near2, near1, far0, here, early1))
    near = jnp.concatenate([near1, near2])
    far = far_of(here, near)
    early1, early2 = in_cores(early1), in_cores(jnp.concatenate([far0, near]))

    inputs = (trial_block, precond_diag, partners, stored_at, ham_blocks)
    inputs, _ = barrier((inputs, near2))
    trial_block, precond_diag, partners, stored_at, ham_blocks = inputs
    ham, rows, zhm, zl, dc, gram_t = pl.pallas_call(
        functools.partial(prepare_kernel, n_chan, n_rad),
        in_specs=[whole] * 4 + [any_],
        out_specs=[whole] * 6,
        out_shape=[
            pltpu.VMEM(ham_blocks.shape, BF16),
            jax.ShapeDtypeStruct((ch, ncoup), jnp.int32),
            pltpu.VMEM((4 * k, lanes), BF16),
            pltpu.VMEM((2 * k, lanes), BF16),
            pltpu.VMEM((1, lanes), F32),
            pltpu.VMEM((k, 3 * k), F32),
        ],
        scratch_shapes=[pltpu.SemaphoreType.DMA],
        compiler_params=pltpu.CompilerParams(vmem_limit_bytes=VMEM_LIMIT),
        name="prepare",
    )(trial_block, precond_diag, partners, stored_at.reshape(-1, 128), in_hbm(ham_blocks))
    far, early1, early2, rows = barrier((far, early1, early2, rows))
    table = jnp.concatenate([x for three in zip(early1, early2, in_cores(far)) for x in three])
    table = table.reshape(n_chan * ch, k, splines)

    az, sums = pl.pallas_call(
        apply_kernel,
        in_specs=[smem] + [whole] * 6,
        out_specs=[whole, whole],
        out_shape=[
            pltpu.VMEM((2 * k, lanes), BF16),
            jax.ShapeDtypeStruct((k, 8 * k), F32),
        ],
        scratch_shapes=[pltpu.VMEM((k, lanes), F32)],
        compiler_params=pltpu.CompilerParams(vmem_limit_bytes=VMEM_LIMIT),
        name="apply",
    )(rows, in_vmem(ham), in_vmem(table), in_vmem(zhm), in_vmem(zl), in_vmem(dc), gram_t)

    sums = gather_sums(sums)
    new_block, ritz = pl.pallas_call(
        functools.partial(finish_kernel, total),
        out_shape=[
            jax.ShapeDtypeStruct((ch, k, r), F32),
            jax.ShapeDtypeStruct((1, k), F32),
        ],
        compiler_params=pltpu.CompilerParams(vmem_limit_bytes=VMEM_LIMIT),
        name="finish",
    )(sums, in_vmem(az), in_vmem(zhm))
    return (new_block, ritz.reshape(k))


def solution(mesh):
    return jax.shard_map(
        body,
        mesh=mesh,
        in_specs=(
            P("chan", None, "rad"),
            P("chan", None, "rad", None),
            P("chan", None),
            P(),
            P("chan", "rad"),
        ),
        out_specs=(P("chan", None, "rad"), P()),
        check_vma=False,
    )
```

```python
import functools

import jax
import jax.numpy as jnp
from jax import lax
from jax.experimental import pallas as pl
from jax.experimental.pallas import tpu as pltpu
from jax.sharding import PartitionSpec as P

SCALE = 2.0 ** -8
F32 = jnp.float32
BF16 = jnp.bfloat16
NT = (((1,), (1,)), ((), ()))
TN = (((0,), (0,)), ((), ()))
NN = (((1,), (0,)), ((), ()))
VMEM_LIMIT = 4 * 1024 * 1024


def swap(x, axis, distance):
    n = lax.axis_size(axis)
    return lax.ppermute(x, axis, [(i, i ^ distance) for i in range(n)])


def plane_swap(x, order):
    n_chan, n_rad = lax.axis_size("chan"), lax.axis_size("rad")
    pairs = []
    for c in range(n_chan):
        for r in range(n_rad):
            pairs.append((c * n_rad + r, (c ^ order[r % 2]) * n_rad + r))
    return lax.ppermute(x, ("chan", "rad"), pairs)


def table_piece(z, part, nz):
    z = z if nz == 4 else jnp.where(z < 2, z, jnp.where((z & 1) == 1, (nz + z - 1) >> 1, 1 + (z >> 1)))
    near = jnp.where(z == 0, nz, nz + 2 + z)
    far = (part & 1) + jnp.where(z == 0, nz + 1, 2 * nz + 1 + z + (part & 1) * (nz - 2))
    return jnp.where(part == 0, z, jnp.where(part == 1, near, far))


def in_vmem(x):
    return pltpu.with_memory_space_constraint(x, pltpu.VMEM)


def in_hbm(x):
    return pltpu.with_memory_space_constraint(x, pltpu.HBM)


def split3(x):
    hi = x.astype(BF16)
    rest = x - hi.astype(F32)
    mid = rest.astype(BF16)
    return hi, mid, (rest - mid.astype(F32)).astype(BF16)


def dot32(x, y, dims=NN):
    return lax.dot_general(x, y, dims, precision=lax.Precision.HIGHEST, preferred_element_type=F32)


def block_sum(g, rows, cols):
    g = sum(g[i : i + rows] for i in range(0, g.shape[0], rows))
    return sum(g[:, i : i + cols] for i in range(0, g.shape[1], cols))


def prepare_kernel(
    n_chan, n_rad, t_ref, d_ref, partners_ref, stored_ref, ham_hbm,
    ham_ref, rows_ref, zhm_ref, zl_ref, dc_ref, gram_ref, sem,
):
    copy = pltpu.make_async_copy(ham_hbm, ham_ref, sem)
    copy.start()
    ch, k, r = t_ref.shape
    group = 128 // r
    for i in range(ch // group):
        lanes = pl.ds(i * 128, 128)
        t = jnp.concatenate([t_ref[i * group + g] for g in range(group)], axis=1)
        d = jnp.concatenate([d_ref[pl.ds(i * group + g, 1), :] for g in range(group)], axis=1)
        dc_ref[:, lanes] = d
        hi, mid, lo = split3(jnp.concatenate([t / d, t], axis=0))
        zhm_ref[:, lanes] = jnp.concatenate([hi, mid], axis=0)
        zl_ref[:, lanes] = lo
    z = jnp.concatenate([zhm_ref[...], zl_ref[...]], axis=0)
    g = block_sum(lax.dot_general(z, z, NT, preferred_element_type=F32), 2 * k, 2 * k)
    gram_ref[...] = jnp.concatenate([g[k:, :], g[:k, :k]], axis=1)

    share, nz = ch // n_rad, n_chan // 4
    q = stored_ref[...]
    owner, local = lax.div(q, ch), lax.rem(q, ch)
    core = lax.div(local, share)
    apart = (owner ^ lax.axis_index("chan")) & 3
    part = jnp.where((core & 1) == 1, ((apart & 1) << 1) | (apart >> 1), apart)
    piece = table_piece((owner ^ lax.axis_index("chan")) >> 2, part, nz)
    place = (core ^ lax.axis_index("rad")) * 4 * nz + piece
    place = (place * share + lax.rem(local, share)).astype(F32)
    lane = lax.broadcasted_iota(jnp.int32, (ch, 128), 1)
    columns = []
    for j in range(partners_ref.shape[1]):
        wanted = jnp.broadcast_to(partners_ref[:, j : j + 1], (ch, 128)) - lane
        found = jnp.zeros((ch, 128), F32)
        for c in range(place.shape[0]):
            found = found + jnp.where(wanted == 128 * c, place[c : c + 1], 0.0)
        columns.append(jnp.sum(found, axis=1, keepdims=True))
    rows_ref[...] = jnp.concatenate(columns, axis=1).astype(jnp.int32)
    copy.wait()


def assemble_kernel(*refs):
    pieces, table_ref, sems = refs[:-2], refs[-2], refs[-1]
    cores = len(pieces) // 2
    copies = []
    for i, piece in enumerate(pieces):
        at = (i // 2) * (table_ref.shape[0] // cores) + (i % 2) * pieces[0].shape[0]
        copies.append(
            pltpu.make_async_copy(piece, table_ref.at[pl.ds(at, piece.shape[0])], sems.at[i])
        )
        copies[-1].start()
    for copy in copies:
        copy.wait()


def terms_kernel(a0_ref, dc_ref, az_ref):
    lanes = a0_ref.shape[1]
    block = min(lanes, 1024)

    def terms(i, carry):
        at = pl.ds(pl.multiple_of(i * block, block), block)
        az_ref[:, at] = jnp.concatenate(split3(a0_ref[:, at] / dc_ref[:, at])[:2], axis=0)
        return carry

    lax.fori_loop(0, lanes // block, terms, 0)


def apply_kernel(rows_ref, ham_ref, _, zhm_ref, zl_ref, dc_ref, gt_ref, *rest):
    last, (a0_ref, sums_ref, table_ref) = rest[:-3], rest[-3:]
    share = table_ref.shape[1]
    for c, piece in enumerate(last):
        start = (c + 1) * (table_ref.shape[0] // len(last)) - piece.shape[0]

        def put(i, carry, piece=piece, start=start):
            table_ref[start + i] = piece[i]
            return carry

        lax.fori_loop(0, piece.shape[0], put, 0)
    ch, ncoup, r, splines = ham_ref.shape
    k = zl_ref.shape[0] // 2
    group = 256 // r

    def row_of(n):
        return table_ref[lax.div(n, share), lax.rem(n, share)]

    def work(g, carry):
        left, right = [], []
        for i in range(group):
            p = g * group + i
            left.append(
                jnp.concatenate([row_of(rows_ref[p, j]) for j in range(ncoup)], axis=1)
            )
            right.append(jnp.concatenate([ham_ref[p, j] for j in range(ncoup)], axis=1))
        product = lax.dot_general(
            jnp.concatenate(left, axis=0),
            jnp.concatenate(right, axis=0),
            NT,
            preferred_element_type=F32,
        )
        own = [product[i * k : (i + 1) * k, i * r : (i + 1) * r] for i in range(group)]
        a0_ref[:, pl.ds(pl.multiple_of(g * 256, 256), 256)] = jnp.concatenate(own, axis=1) * SCALE
        return carry

    lax.fori_loop(0, ch // group, work, 0, unroll=min(2, ch // group))

    lanes = ch * r
    block = min(lanes, 1024)

    def gram_block(i, gram):
        at = pl.ds(pl.multiple_of(i * block, block), block)
        a0 = a0_ref[:, at]
        a1_terms = split3(a0 / dc_ref[:, at])
        right = jnp.concatenate(a1_terms + split3(a0), axis=0)
        left = jnp.concatenate([zhm_ref[:, at], zl_ref[:, at], right[: 3 * k]], axis=0)
        return gram + lax.dot_general(left, right, NT, preferred_element_type=F32)

    gram = lax.fori_loop(0, lanes // block, gram_block, jnp.zeros((9 * k, 6 * k), F32))
    ta1 = block_sum(gram[: 6 * k, : 3 * k], 2 * k, k)
    ta0 = block_sum(gram[: 6 * k, 3 * k :], 2 * k, k)
    aa = block_sum(gram[6 * k :, : 3 * k], k, k)
    gt = gt_ref[...]
    parts = [ta1[k:], gt[:, : 2 * k], ta0[k:], ta1[:k], gt[:, 2 * k :], aa, jnp.zeros((k, k), F32)]
    sums_ref[...] = jnp.concatenate(parts, axis=1)


def spread(x, i):
    return jnp.broadcast_to(x[:, i : i + 1], (x.shape[0], 128))


def finish_kernel(total, sums_ref, az_ref, zhm_ref, out_ref, ritz_ref):
    ch, k, r = out_ref.shape
    s = jnp.sum(sums_ref[...], axis=0)
    row = lax.broadcasted_iota(jnp.int32, (k, 128), 0)
    cols = [spread(s, 2 * k + i) for i in range(k)]
    x = s
    for i in range(k):
        scale = 1.0 / cols[i][i : i + 1]
        pivot = x[i : i + 1] * scale
        x = jnp.where(row == i, pivot, x - cols[i] * pivot)
        for j in range(i + 1, k):
            part = cols[j][i : i + 1] * scale
            cols[j] = jnp.where(row == i, part, cols[j] - cols[i] * part)
    coef = x[:, 3 * k : 4 * k]
    eye = lax.broadcasted_iota(jnp.int32, (k, k), 0) == lax.broadcasted_iota(jnp.int32, (k, k), 1)
    ritz_ref[...] = jnp.sum(jnp.where(eye, coef, 0.0), axis=0, keepdims=True) * (1.0 / SCALE)
    s1, b1 = s[:, :k], s[:, k : 2 * k]
    s2, b2, aa = s[:, 4 * k : 5 * k], s[:, 5 * k : 6 * k], s[:, 6 * k : 7 * k]
    known = jnp.concatenate([x[:, :k], s1, s2], axis=0)
    known = known - dot32(jnp.concatenate([x[:, k : 2 * k], b1, b2], axis=0), coef)
    mix, corr, weighted = known[:k], known[k : 2 * k], known[2 * k :]
    gram = aa - dot32(
        jnp.concatenate([s2, coef, corr], axis=0), jnp.concatenate([coef, weighted, mix], axis=0), TN
    )
    cols = [spread(gram, i) for i in range(k)]
    pad = jnp.zeros((k, 128 - 3 * k), F32)
    x = jnp.concatenate([eye.astype(F32), -coef.T, -mix.T, pad], axis=1)
    for i in range(k):
        pivot = cols[i][i : i + 1]
        scale = 1.0 / pivot
        below = jnp.where(row > i, cols[i] * scale, 0.0)
        pivot_row = x[i : i + 1]
        x = jnp.where(row == i, pivot_row * (lax.rsqrt(pivot) * (total ** 0.5)), x - below * pivot_row)
        for j in range(i + 1, k):
            cols[j] = cols[j] - below * cols[j][i : i + 1]
    hi, mid, _ = split3(x[:, : 3 * k])
    lhs = jnp.concatenate([hi, hi, mid], axis=1)
    block = min(ch * r, 1024)

    def result(b, carry):
        at = pl.ds(pl.multiple_of(b * block, block), block)
        x_hi = jnp.concatenate([az_ref[:k, at], zhm_ref[: 2 * k, at]], axis=0)
        x_mid = jnp.concatenate([az_ref[k:, at], zhm_ref[2 * k :, at]], axis=0)
        new = lax.dot_general(
            lhs, jnp.concatenate([x_hi, x_mid, x_hi], axis=0), NN, preferred_element_type=F32
        )
        for i in range(block // r):
            out_ref[b * (block // r) + i] = new[:, i * r : (i + 1) * r]
        return carry

    lax.fori_loop(0, ch * r // block, result, 0)


def gather_sums(x):
    n_chan, n_rad = lax.axis_size("chan"), lax.axis_size("rad")
    step = 1
    while step < n_rad:
        x = x + swap(x, "rad", step)
        step *= 2
    every = jnp.broadcast_to(x, (n_chan,) + x.shape)
    return lax.all_to_all(every, "chan", split_axis=0, concat_axis=0, tiled=True)


def own_share(trial_block):
    n_rad = lax.axis_size("rad")
    ch, k, r = trial_block.shape
    me = lax.axis_index("rad")
    rounded = trial_block.astype(BF16).reshape(n_rad, ch // n_rad, k, r)
    got = []
    for d in range(n_rad):
        part = lax.dynamic_index_in_dim(rounded, me ^ d, 0, keepdims=False)
        got.append(swap(part, "rad", d) if d else part)
    lanes = []
    for c in range(n_rad):
        x = got[0]
        for d in range(1, n_rad):
            x = jnp.where(me ^ d == c, got[d], x)
        lanes.append(x)
    return jnp.concatenate(lanes, axis=2)


def body(trial_block, ham_blocks, partners, stored_at, precond_diag):
    n_chan, n_rad = lax.axis_size("chan"), lax.axis_size("rad")
    ch, k, r = trial_block.shape
    ncoup, splines = ham_blocks.shape[1], ham_blocks.shape[3]
    lanes = ch * r
    total = float(n_chan * n_rad * lanes)
    share, nz = ch // n_rad, n_chan // 4

    barrier = lax.optimization_barrier
    smem = pl.BlockSpec(memory_space=pltpu.SMEM)
    any_ = pl.BlockSpec(memory_space=pl.ANY)
    whole = pl.BlockSpec(memory_space=pltpu.VMEM)

    def near_of(x):
        return plane_swap(x, (1, 2))

    def far_of(x, near):
        return plane_swap(jnp.concatenate([x, near]), (2, 1))

    def in_cores(x):
        return [x] + [swap(x, "rad", c) for c in range(1, n_rad)]

    own = own_share(trial_block)[None]
    z_even = jnp.concatenate([swap(own, "chan", 4 * z) for z in range(2, nz, 2)])
    z1 = swap(own, "chan", 4)
    near0 = near_of(own)
    z_even, z1, near0 = barrier((z_even, z1, near0))
    some = jnp.concatenate([z1, z_even])
    near1 = near_of(some)
    far0 = far_of(own, near0)
    z_odd = swap(z_even, "chan", 4)
    z_odd, near1, far0 = barrier((z_odd, near1, far0))
    near2 = near_of(z_odd)
    here = jnp.concatenate([some, z_odd])
    early1 = jnp.concatenate([own, here, near0])
    near2, near1, far0, here, early1 = barrier((near2, near1, far0, here, early1))
    near = jnp.concatenate([near1, near2])
    far = far_of(here, near)
    early1, early2 = in_cores(early1), in_cores(jnp.concatenate([far0, near]))

    inputs = (trial_block, precond_diag, partners, stored_at, ham_blocks)
    inputs, _ = barrier((inputs, near2))
    trial_block, precond_diag, partners, stored_at, ham_blocks = inputs
    ham, rows, zhm, zl, dc, gram_t = pl.pallas_call(
        functools.partial(prepare_kernel, n_chan, n_rad),
        in_specs=[whole] * 4 + [any_],
        out_specs=[whole] * 6,
        out_shape=[
            pltpu.VMEM(ham_blocks.shape, BF16),
            jax.ShapeDtypeStruct((ch, ncoup), jnp.int32),
            pltpu.VMEM((4 * k, lanes), BF16),
            pltpu.VMEM((2 * k, lanes), BF16),
            pltpu.VMEM((1, lanes), F32),
            pltpu.VMEM((k, 3 * k), F32),
        ],
        scratch_shapes=[pltpu.SemaphoreType.DMA],
        compiler_params=pltpu.CompilerParams(vmem_limit_bytes=VMEM_LIMIT),
        name="prepare",
    )(trial_block, precond_diag, partners, stored_at.reshape(-1, 128), in_hbm(ham_blocks))
    pieces = [x for pair in zip(early1, early2) for x in pair]
    table = pl.pallas_call(
        assemble_kernel,
        in_specs=[any_] * len(pieces),
        out_specs=whole,
        out_shape=pltpu.VMEM((4 * nz * n_rad,) + own.shape[1:], BF16),
        scratch_shapes=[pltpu.SemaphoreType.DMA((len(pieces),))],
        compiler_params=pltpu.CompilerParams(vmem_limit_bytes=VMEM_LIMIT),
        name="assemble",
    )(*pieces)
    far, table, rows = barrier((far, table, rows))
    last = [in_vmem(x) for x in in_cores(far)]

    a0, sums, _ = pl.pallas_call(
        apply_kernel,
        in_specs=[smem] + [whole] * (6 + n_rad),
        out_specs=[whole, whole, whole],
        out_shape=[
            pltpu.VMEM((k, lanes), F32),
            jax.ShapeDtypeStruct((k, 8 * k), F32),
            pltpu.VMEM(table.shape, BF16),
        ],
        input_output_aliases={2: 2},
        compiler_params=pltpu.CompilerParams(vmem_limit_bytes=VMEM_LIMIT),
        name="apply",
    )(rows, in_vmem(ham), in_vmem(table), in_vmem(zhm), in_vmem(zl), in_vmem(dc), gram_t, *last)

    az = pl.pallas_call(
        terms_kernel,
        in_specs=[whole, whole],
        out_specs=whole,
        out_shape=pltpu.VMEM((2 * k, lanes), BF16),
        compiler_params=pltpu.CompilerParams(vmem_limit_bytes=VMEM_LIMIT),
        name="terms",
    )(in_vmem(a0), in_vmem(dc))
    sums = gather_sums(sums)
    new_block, ritz = pl.pallas_call(
        functools.partial(finish_kernel, total),
        out_shape=[
            jax.ShapeDtypeStruct((ch, k, r), F32),
            jax.ShapeDtypeStruct((1, k), F32),
        ],
        compiler_params=pltpu.CompilerParams(vmem_limit_bytes=VMEM_LIMIT),
        name="finish",
    )(sums, in_vmem(az), in_vmem(zhm))
    return (new_block, ritz.reshape(k))


def solution(mesh):
    return jax.shard_map(
        body,
        mesh=mesh,
        in_specs=(
            P("chan", None, "rad"),
            P("chan", None, "rad", None),
            P("chan", None),
            P(),
            P("chan", "rad"),
        ),
        out_specs=(P("chan", None, "rad"), P()),
        check_vma=False,
    )
```

```python
import functools

import jax
import jax.numpy as jnp
from jax import lax
from jax.experimental import pallas as pl
from jax.experimental.pallas import tpu as pltpu
from jax.sharding import PartitionSpec as P

SCALE = 2.0 ** -8
F32 = jnp.float32
BF16 = jnp.bfloat16
NT = (((1,), (1,)), ((), ()))
TN = (((0,), (0,)), ((), ()))
NN = (((1,), (0,)), ((), ()))
VMEM_LIMIT = 4 * 1024 * 1024


def swap(x, axis, distance):
    n = lax.axis_size(axis)
    return lax.ppermute(x, axis, [(i, i ^ distance) for i in range(n)])


def plane_swap(x, order):
    n_chan, n_rad = lax.axis_size("chan"), lax.axis_size("rad")
    pairs = []
    for c in range(n_chan):
        for r in range(n_rad):
            pairs.append((c * n_rad + r, (c ^ order[r % 2]) * n_rad + r))
    return lax.ppermute(x, ("chan", "rad"), pairs)


def table_piece(z, part, nz):
    z = z if nz == 4 else jnp.where(z < 2, z, jnp.where((z & 1) == 1, (nz + z - 1) >> 1, 1 + (z >> 1)))
    near = jnp.where(z == 0, nz, nz + 2 + z)
    second = part & 1
    far = jnp.where(z == 0, nz + 1, jnp.where(z == 1, 4 * nz - 2, 2 * nz + z + second * (nz - 3))) + second
    return jnp.where(part == 0, z, jnp.where(part == 1, near, far))


def in_vmem(x):
    return pltpu.with_memory_space_constraint(x, pltpu.VMEM)


def in_hbm(x):
    return pltpu.with_memory_space_constraint(x, pltpu.HBM)


def split3(x):
    hi = x.astype(BF16)
    rest = x - hi.astype(F32)
    mid = rest.astype(BF16)
    return hi, mid, (rest - mid.astype(F32)).astype(BF16)


def dot32(x, y, dims=NN):
    return lax.dot_general(x, y, dims, precision=lax.Precision.HIGHEST, preferred_element_type=F32)


def block_sum(g, rows, cols):
    g = sum(g[i : i + rows] for i in range(0, g.shape[0], rows))
    return sum(g[:, i : i + cols] for i in range(0, g.shape[1], cols))


def prepare_kernel(
    n_chan, n_rad, t_hbm, d_hbm, partners_hbm, stored_hbm, ham_hbm,
    rows_ref, ham_ref, zhm_ref, zl_ref, dc_ref, gram_ref, t_ref, d_ref, partners_ref, stored_ref, sems,
):
    moves = (
        (t_hbm, t_ref), (d_hbm, d_ref), (partners_hbm, partners_ref), (stored_hbm, stored_ref), (ham_hbm, ham_ref)
    )
    copies = [pltpu.make_async_copy(x, y, sems.at[i]) for i, (x, y) in enumerate(moves)]
    for copy in copies:
        copy.start()
    for copy in copies[:4]:
        copy.wait()
    ch, k, r = t_ref.shape
    group = 128 // r
    for i in range(ch // group):
        lanes = pl.ds(i * 128, 128)
        t = jnp.concatenate([t_ref[i * group + g] for g in range(group)], axis=1)
        d = jnp.concatenate([d_ref[pl.ds(i * group + g, 1), :] for g in range(group)], axis=1)
        dc_ref[:, lanes] = d
        hi, mid, lo = split3(jnp.concatenate([t / d, t], axis=0))
        zhm_ref[:, lanes] = jnp.concatenate([hi, mid], axis=0)
        zl_ref[:, lanes] = lo
    z = jnp.concatenate([zhm_ref[...], zl_ref[...]], axis=0)
    g = block_sum(lax.dot_general(z, z, NT, preferred_element_type=F32), 2 * k, 2 * k)
    gram_ref[...] = jnp.concatenate([g[k:, :], g[:k, :k]], axis=1)

    share, nz = ch // n_rad, n_chan // 4
    q = stored_ref[...]
    owner, local = lax.div(q, ch), lax.rem(q, ch)
    core = lax.div(local, share)
    apart = (owner ^ lax.axis_index("chan")) & 3
    part = jnp.where((core & 1) == 1, ((apart & 1) << 1) | (apart >> 1), apart)
    piece = table_piece((owner ^ lax.axis_index("chan")) >> 2, part, nz)
    place = (core ^ lax.axis_index("rad")) * 4 * nz + piece
    place = (place * share + lax.rem(local, share)).astype(F32)
    lane = lax.broadcasted_iota(jnp.int32, (ch, 128), 1)
    columns = []
    partners = partners_ref[...].astype(F32).T.astype(jnp.int32)
    for j in range(partners.shape[1]):
        wanted = jnp.broadcast_to(partners[:, j : j + 1], (ch, 128)) - lane
        found = jnp.zeros((ch, 128), F32)
        for c in range(place.shape[0]):
            found = found + jnp.where(wanted == 128 * c, place[c : c + 1], 0.0)
        columns.append(jnp.sum(found, axis=1, keepdims=True))
    rows_ref[...] = jnp.concatenate(columns, axis=1).astype(jnp.int32)
    copies[4].wait()


def assemble_kernel(*refs):
    pieces, table_ref, sems = refs[:-2], refs[-2], refs[-1]
    cores = len(pieces) // 2
    copies = []
    for i, piece in enumerate(pieces):
        at = (i // 2) * (table_ref.shape[0] // cores) + (i % 2) * pieces[0].shape[0]
        copies.append(
            pltpu.make_async_copy(piece, table_ref.at[pl.ds(at, piece.shape[0])], sems.at[i])
        )
        copies[-1].start()
    for copy in copies:
        copy.wait()


def apply_kernel(rows_ref, ham_ref, _, zhm_ref, zl_ref, dc_ref, gt_ref, *rest):
    last, (az_ref, sums_ref, table_ref, a0_ref) = rest[:-4], rest[-4:]
    share = table_ref.shape[1]
    for c, piece in enumerate(last):
        start = (c + 1) * (table_ref.shape[0] // len(last)) - piece.shape[0]

        def put(i, carry, piece=piece, start=start):
            table_ref[start + i] = piece[i]
            return carry

        lax.fori_loop(0, piece.shape[0], put, 0)
    ch, ncoup, r, splines = ham_ref.shape
    k = zl_ref.shape[0] // 2
    group = 256 // r

    def row_of(n):
        return table_ref[lax.div(n, share), lax.rem(n, share)]

    def work(g, carry):
        left, right = [], []
        for i in range(group):
            p = g * group + i
            left.append(
                jnp.concatenate([row_of(rows_ref[p, j]) for j in range(ncoup)], axis=1)
            )
            right.append(jnp.concatenate([ham_ref[p, j] for j in range(ncoup)], axis=1))
        product = lax.dot_general(
            jnp.concatenate(left, axis=0),
            jnp.concatenate(right, axis=0),
            NT,
            preferred_element_type=F32,
        )
        own = [product[i * k : (i + 1) * k, i * r : (i + 1) * r] for i in range(group)]
        a0_ref[:, pl.ds(pl.multiple_of(g * 256, 256), 256)] = jnp.concatenate(own, axis=1) * SCALE
        return carry

    lax.fori_loop(0, ch // group, work, 0, unroll=min(2, ch // group))

    lanes = ch * r
    block = min(lanes, 1024)

    def gram_block(i, gram):
        at = pl.ds(pl.multiple_of(i * block, block), block)
        a0 = a0_ref[:, at]
        a1_terms = split3(a0 / dc_ref[:, at])
        az_ref[:, at] = jnp.concatenate(a1_terms[:2], axis=0)
        right = jnp.concatenate(a1_terms + split3(a0), axis=0)
        left = jnp.concatenate([zhm_ref[:, at], zl_ref[:, at], right[: 3 * k]], axis=0)
        return gram + lax.dot_general(left, right, NT, preferred_element_type=F32)

    gram = lax.fori_loop(0, lanes // block, gram_block, jnp.zeros((9 * k, 6 * k), F32))
    ta1 = block_sum(gram[: 6 * k, : 3 * k], 2 * k, k)
    ta0 = block_sum(gram[: 6 * k, 3 * k :], 2 * k, k)
    aa = block_sum(gram[6 * k :, : 3 * k], k, k)
    gt = gt_ref[...]
    parts = [ta1[k:], gt[:, : 2 * k], ta0[k:], ta1[:k], gt[:, 2 * k :], aa, jnp.zeros((k, k), F32)]
    sums_ref[...] = jnp.concatenate(parts, axis=1)


def spread(x, i):
    return jnp.broadcast_to(x[:, i : i + 1], (x.shape[0], 128))


def finish_kernel(total, sums_ref, az_ref, zhm_ref, out_ref, ritz_ref):
    ch, k, r = out_ref.shape
    s = jnp.sum(sums_ref[...], axis=0)
    row = lax.broadcasted_iota(jnp.int32, (k, 128), 0)
    cols = [spread(s, 2 * k + i) for i in range(k)]
    x = s
    for i in range(k):
        scale = 1.0 / cols[i][i : i + 1]
        pivot = x[i : i + 1] * scale
        x = jnp.where(row == i, pivot, x - cols[i] * pivot)
        for j in range(i + 1, k):
            part = cols[j][i : i + 1] * scale
            cols[j] = jnp.where(row == i, part, cols[j] - cols[i] * part)
    coef = x[:, 3 * k : 4 * k]
    eye = lax.broadcasted_iota(jnp.int32, (k, k), 0) == lax.broadcasted_iota(jnp.int32, (k, k), 1)
    ritz_ref[...] = jnp.sum(jnp.where(eye, coef, 0.0), axis=0, keepdims=True) * (1.0 / SCALE)
    s1, b1 = s[:, :k], s[:, k : 2 * k]
    s2, b2, aa = s[:, 4 * k : 5 * k], s[:, 5 * k : 6 * k], s[:, 6 * k : 7 * k]
    known = jnp.concatenate([x[:, :k], s1, s2], axis=0)
    known = known - dot32(jnp.concatenate([x[:, k : 2 * k], b1, b2], axis=0), coef)
    mix, corr, weighted = known[:k], known[k : 2 * k], known[2 * k :]
    gram = aa - dot32(
        jnp.concatenate([s2, coef, corr], axis=0), jnp.concatenate([coef, weighted, mix], axis=0), TN
    )
    cols = [spread(gram, i) for i in range(k)]
    pad = jnp.zeros((k, 128 - 3 * k), F32)
    x = jnp.concatenate([eye.astype(F32), -coef.T, -mix.T, pad], axis=1)
    for i in range(k):
        pivot = cols[i][i : i + 1]
        scale = 1.0 / pivot
        below = jnp.where(row > i, cols[i] * scale, 0.0)
        pivot_row = x[i : i + 1]
        x = jnp.where(row == i, pivot_row * (lax.rsqrt(pivot) * (total ** 0.5)), x - below * pivot_row)
        for j in range(i + 1, k):
            cols[j] = cols[j] - below * cols[j][i : i + 1]
    hi, mid, _ = split3(x[:, : 3 * k])
    lhs = jnp.concatenate([hi, hi, mid], axis=1)
    block = min(ch * r, 1024)

    def result(b, carry):
        at = pl.ds(pl.multiple_of(b * block, block), block)
        x_hi = jnp.concatenate([az_ref[:k, at], zhm_ref[: 2 * k, at]], axis=0)
        x_mid = jnp.concatenate([az_ref[k:, at], zhm_ref[2 * k :, at]], axis=0)
        new = lax.dot_general(
            lhs, jnp.concatenate([x_hi, x_mid, x_hi], axis=0), NN, preferred_element_type=F32
        )
        for i in range(block // r):
            out_ref[b * (block // r) + i] = new[:, i * r : (i + 1) * r]
        return carry

    lax.fori_loop(0, ch * r // block, result, 0)


def gather_sums(x):
    n_chan, n_rad = lax.axis_size("chan"), lax.axis_size("rad")
    step = 1
    while step < n_rad:
        x = x + swap(x, "rad", step)
        step *= 2
    every = jnp.broadcast_to(x, (n_chan,) + x.shape)
    return lax.all_to_all(every, "chan", split_axis=0, concat_axis=0, tiled=True)


def own_share(trial_block):
    n_rad = lax.axis_size("rad")
    ch, k, r = trial_block.shape
    me = lax.axis_index("rad")
    rounded = trial_block.astype(BF16).reshape(n_rad, ch // n_rad, k, r)
    got = []
    for d in range(n_rad):
        part = lax.dynamic_index_in_dim(rounded, me ^ d, 0, keepdims=False)
        got.append(swap(part, "rad", d) if d else part)
    lanes = []
    for c in range(n_rad):
        x = got[0]
        for d in range(1, n_rad):
            x = jnp.where(me ^ d == c, got[d], x)
        lanes.append(x)
    return jnp.concatenate(lanes, axis=2)


def body(trial_block, ham_blocks, partners, stored_at, precond_diag):
    n_chan, n_rad = lax.axis_size("chan"), lax.axis_size("rad")
    ch, k, r = trial_block.shape
    ncoup, splines = ham_blocks.shape[1], ham_blocks.shape[3]
    lanes = ch * r
    total = float(n_chan * n_rad * lanes)
    share, nz = ch // n_rad, n_chan // 4

    barrier = lax.optimization_barrier
    smem = pl.BlockSpec(memory_space=pltpu.SMEM)
    any_ = pl.BlockSpec(memory_space=pl.ANY)
    whole = pl.BlockSpec(memory_space=pltpu.VMEM)

    def near_of(x):
        return plane_swap(x, (1, 2))

    def far_of(x):
        return plane_swap(x, (2, 1))

    def in_cores(x):
        return [x] + [swap(x, "rad", c) for c in range(1, n_rad)]

    own = own_share(trial_block)[None]
    near0, far_own = near_of(own), far_of(own)
    z1 = swap(own, "chan", 4)
    z_even = jnp.concatenate([swap(own, "chan", 4 * z) for z in range(2, nz, 2)])
    rows, ham, zhm, zl, dc, gram_t = pl.pallas_call(
        functools.partial(prepare_kernel, n_chan, n_rad),
        in_specs=[any_] * 5,
        out_specs=[whole] * 6,
        out_shape=[
            jax.ShapeDtypeStruct((ch, ncoup), jnp.int32),
            pltpu.VMEM(ham_blocks.shape, BF16),
            pltpu.VMEM((4 * k, lanes), BF16),
            pltpu.VMEM((2 * k, lanes), BF16),
            pltpu.VMEM((1, lanes), F32),
            pltpu.VMEM((k, 3 * k), F32),
        ],
        scratch_shapes=[
            pltpu.VMEM(trial_block.shape, F32),
            pltpu.VMEM(precond_diag.shape, F32),
            pltpu.VMEM((ncoup, ch), jnp.int32),
            pltpu.VMEM((stored_at.shape[0] // 128, 128), jnp.int32),
            pltpu.SemaphoreType.DMA((5,)),
        ],
        compiler_params=pltpu.CompilerParams(vmem_limit_bytes=VMEM_LIMIT),
        name="prepare",
    )(
        in_hbm(trial_block),
        in_hbm(precond_diag),
        in_hbm(partners.T),
        in_hbm(stored_at.reshape(-1, 128)),
        in_hbm(ham_blocks),
    )
    far_own, near0, z1, z_even, rows = barrier((far_own, near0, z1, z_even, rows))
    z_odd = swap(z_even, "chan", 4)
    near1 = near_of(jnp.concatenate([z1, z_even]))
    far_near = far_of(near0)
    z_odd, near1, far_near = barrier((z_odd, near1, far_near))
    near2 = near_of(z_odd)
    early = in_cores(jnp.concatenate([own, z1, z_even, z_odd, near0, far_own, far_near, near1]))
    near2, near1, early, far_own, far_near = barrier((near2, near1, early, far_own, far_near))
    far = far_of(jnp.concatenate([z_even, z_odd, near1[1:], near2]))
    far1 = swap(jnp.concatenate([far_own, far_near]), "chan", 4)
    near2 = in_cores(near2)
    pieces = [x for pair in zip(early, near2) for x in pair]
    table = pl.pallas_call(
        assemble_kernel,
        in_specs=[any_] * len(pieces),
        out_specs=whole,
        out_shape=pltpu.VMEM((4 * nz * n_rad,) + own.shape[1:], BF16),
        scratch_shapes=[pltpu.SemaphoreType.DMA((len(pieces),))],
        compiler_params=pltpu.CompilerParams(vmem_limit_bytes=VMEM_LIMIT),
        name="assemble",
    )(*pieces)
    far, far1, table = barrier((far, far1, table))
    last = [in_vmem(x) for x in in_cores(jnp.concatenate([far, far1]))]

    az, sums, _ = pl.pallas_call(
        apply_kernel,
        in_specs=[smem] + [whole] * (6 + n_rad),
        out_specs=[whole, whole, whole],
        out_shape=[
            pltpu.VMEM((2 * k, lanes), BF16),
            jax.ShapeDtypeStruct((k, 8 * k), F32),
            pltpu.VMEM(table.shape, BF16),
        ],
        input_output_aliases={2: 2},
        scratch_shapes=[pltpu.VMEM((k, lanes), F32)],
        compiler_params=pltpu.CompilerParams(vmem_limit_bytes=VMEM_LIMIT),
        name="apply",
    )(rows, in_vmem(ham), in_vmem(table), in_vmem(zhm), in_vmem(zl), in_vmem(dc), gram_t, *last)

    sums = gather_sums(sums)
    new_block, ritz = pl.pallas_call(
        functools.partial(finish_kernel, total),
        out_shape=[
            jax.ShapeDtypeStruct((ch, k, r), F32),
            jax.ShapeDtypeStruct((1, k), F32),
        ],
        compiler_params=pltpu.CompilerParams(vmem_limit_bytes=VMEM_LIMIT),
        name="finish",
    )(sums, in_vmem(az), in_vmem(zhm))
    return (new_block, ritz.reshape(k))


def solution(mesh):
    return jax.shard_map(
        body,
        mesh=mesh,
        in_specs=(
            P("chan", None, "rad"),
            P("chan", None, "rad", None),
            P("chan", None),
            P(),
            P("chan", "rad"),
        ),
        out_specs=(P("chan", None, "rad"), P()),
        check_vma=False,
    )
```

```python
import functools

import jax
import jax.numpy as jnp
from jax import lax
from jax.experimental import pallas as pl
from jax.experimental.pallas import tpu as pltpu
from jax.sharding import PartitionSpec as P

SCALE = 2.0 ** -8
F32 = jnp.float32
BF16 = jnp.bfloat16
NT = (((1,), (1,)), ((), ()))
TN = (((0,), (0,)), ((), ()))
NN = (((1,), (0,)), ((), ()))
VMEM_LIMIT = 4 * 1024 * 1024


def swap(x, axis, distance):
    n = lax.axis_size(axis)
    return lax.ppermute(x, axis, [(i, i ^ distance) for i in range(n)])


def plane_swap(x, order):
    n_chan, n_rad = lax.axis_size("chan"), lax.axis_size("rad")
    pairs = []
    for c in range(n_chan):
        for r in range(n_rad):
            pairs.append((c * n_rad + r, (c ^ order[r % 2]) * n_rad + r))
    return lax.ppermute(x, ("chan", "rad"), pairs)


def table_piece(z, part, nz):
    some, odd = nz // 2, nz // 2 - 1
    is_odd = (z & 1 == 1) & (z > 1)
    i = jnp.where(is_odd, (z - 3) >> 1, jnp.where(z == 1, 0, z >> 1))
    base = 2 * some + odd + 4

    def pick(own, of_some, of_odd):
        return jnp.where(z == 0, own, jnp.where(is_odd, of_odd + i, of_some + i))

    here = pick(0, 1, 2 * some + 4)
    near = pick(some + 1, some + 4, base + odd + some)
    far = pick(some + 2, base + odd, base + 2 * odd + some)
    both = pick(some + 3, base + 3 * odd + some, base)
    return jnp.where(part == 0, here, jnp.where(part == 1, near, jnp.where(part == 2, far, both)))


def in_vmem(x):
    return pltpu.with_memory_space_constraint(x, pltpu.VMEM)


def in_hbm(x):
    return pltpu.with_memory_space_constraint(x, pltpu.HBM)


def split3(x):
    hi = x.astype(BF16)
    rest = x - hi.astype(F32)
    mid = rest.astype(BF16)
    return hi, mid, (rest - mid.astype(F32)).astype(BF16)


def dot32(x, y, dims=NN):
    return lax.dot_general(x, y, dims, precision=lax.Precision.HIGHEST, preferred_element_type=F32)


def block_sum(g, rows, cols):
    g = sum(g[i : i + rows] for i in range(0, g.shape[0], rows))
    return sum(g[:, i : i + cols] for i in range(0, g.shape[1], cols))


def prepare_kernel(
    n_chan, n_rad, t_hbm, d_hbm, partners_hbm, stored_hbm, ham_hbm,
    rows_ref, ham_ref, zhm_ref, zl_ref, dc_ref, gram_ref, t_ref, d_ref, partners_ref, stored_ref, sems,
):
    moves = (
        (t_hbm, t_ref), (d_hbm, d_ref), (partners_hbm, partners_ref), (stored_hbm, stored_ref), (ham_hbm, ham_ref)
    )
    copies = [pltpu.make_async_copy(x, y, sems.at[i]) for i, (x, y) in enumerate(moves)]
    for copy in copies:
        copy.start()
    for copy in copies[:4]:
        copy.wait()
    ch, k, r = t_ref.shape
    group = 128 // r
    for i in range(ch // group):
        lanes = pl.ds(i * 128, 128)
        t = jnp.concatenate([t_ref[i * group + g] for g in range(group)], axis=1)
        d = jnp.concatenate([d_ref[pl.ds(i * group + g, 1), :] for g in range(group)], axis=1)
        dc_ref[:, lanes] = d
        hi, mid, lo = split3(jnp.concatenate([t / d, t], axis=0))
        zhm_ref[:, lanes] = jnp.concatenate([hi, mid], axis=0)
        zl_ref[:, lanes] = lo
    z = jnp.concatenate([zhm_ref[...], zl_ref[...]], axis=0)
    g = block_sum(lax.dot_general(z, z, NT, preferred_element_type=F32), 2 * k, 2 * k)
    gram_ref[...] = jnp.concatenate([g[k:, :], g[:k, :k]], axis=1)

    share, nz = ch // n_rad, n_chan // 4
    q = stored_ref[...]
    owner, local = lax.div(q, ch), lax.rem(q, ch)
    core = lax.div(local, share)
    apart = (owner ^ lax.axis_index("chan")) & 3
    part = jnp.where((core & 1) == 1, ((apart & 1) << 1) | (apart >> 1), apart)
    piece = table_piece((owner ^ lax.axis_index("chan")) >> 2, part, nz)
    place = (core ^ lax.axis_index("rad")) * 4 * nz + piece
    place = (place * share + lax.rem(local, share)).astype(F32)
    lane = lax.broadcasted_iota(jnp.int32, (ch, 128), 1)
    columns = []
    partners = partners_ref[...].astype(F32).T.astype(jnp.int32)
    for j in range(partners.shape[1]):
        wanted = jnp.broadcast_to(partners[:, j : j + 1], (ch, 128)) - lane
        found = jnp.zeros((ch, 128), F32)
        for c in range(place.shape[0]):
            found = found + jnp.where(wanted == 128 * c, place[c : c + 1], 0.0)
        columns.append(jnp.sum(found, axis=1, keepdims=True))
    rows_ref[...] = jnp.concatenate(columns, axis=1).astype(jnp.int32)
    copies[4].wait()


def assemble_kernel(*refs):
    pieces, table_ref, sems = refs[:-2], refs[-2], refs[-1]
    each = table_ref.shape[0] // len(pieces)
    copies = []
    for i, piece in enumerate(pieces):
        place = table_ref.at[pl.ds(i * each, piece.shape[0])]
        copies.append(pltpu.make_async_copy(piece, place, sems.at[i]))
        copies[-1].start()
    for copy in copies:
        copy.wait()


def apply_kernel(rows_ref, ham_ref, _, zhm_ref, zl_ref, dc_ref, gt_ref, *rest):
    last, (az_ref, sums_ref, table_ref, a0_ref) = rest[:-4], rest[-4:]
    share = table_ref.shape[1]
    for c, piece in enumerate(last):
        start = (c + 1) * (table_ref.shape[0] // len(last)) - piece.shape[0]

        def put(i, carry, piece=piece, start=start):
            table_ref[start + i] = piece[i]
            return carry

        lax.fori_loop(0, piece.shape[0], put, 0)
    ch, ncoup, r, splines = ham_ref.shape
    k = zl_ref.shape[0] // 2
    group = 256 // r

    def row_of(n):
        return table_ref[lax.div(n, share), lax.rem(n, share)]

    def work(g, carry):
        left, right = [], []
        for i in range(group):
            p = g * group + i
            left.append(
                jnp.concatenate([row_of(rows_ref[p, j]) for j in range(ncoup)], axis=1)
            )
            right.append(jnp.concatenate([ham_ref[p, j] for j in range(ncoup)], axis=1))
        product = lax.dot_general(
            jnp.concatenate(left, axis=0),
            jnp.concatenate(right, axis=0),
            NT,
            preferred_element_type=F32,
        )
        own = [product[i * k : (i + 1) * k, i * r : (i + 1) * r] for i in range(group)]
        a0_ref[:, pl.ds(pl.multiple_of(g * 256, 256), 256)] = jnp.concatenate(own, axis=1) * SCALE
        return carry

    lax.fori_loop(0, ch // group, work, 0, unroll=min(2, ch // group))

    lanes = ch * r
    block = min(lanes, 1024)

    def gram_block(i, gram):
        at = pl.ds(pl.multiple_of(i * block, block), block)
        a0 = a0_ref[:, at]
        a1_terms = split3(a0 / dc_ref[:, at])
        az_ref[:, at] = jnp.concatenate(a1_terms[:2], axis=0)
        right = jnp.concatenate(a1_terms + split3(a0), axis=0)
        left = jnp.concatenate([zhm_ref[:, at], zl_ref[:, at], right[: 3 * k]], axis=0)
        return gram + lax.dot_general(left, right, NT, preferred_element_type=F32)

    gram = lax.fori_loop(0, lanes // block, gram_block, jnp.zeros((9 * k, 6 * k), F32))
    ta1 = block_sum(gram[: 6 * k, : 3 * k], 2 * k, k)
    ta0 = block_sum(gram[: 6 * k, 3 * k :], 2 * k, k)
    aa = block_sum(gram[6 * k :, : 3 * k], k, k)
    gt = gt_ref[...]
    parts = [ta1[k:], gt[:, : 2 * k], ta0[k:], ta1[:k], gt[:, 2 * k :], aa, jnp.zeros((k, k), F32)]
    sums_ref[...] = jnp.concatenate(parts, axis=1)


def spread(x, i):
    return jnp.broadcast_to(x[:, i : i + 1], (x.shape[0], 128))


def finish_kernel(total, sums_ref, az_ref, zhm_ref, out_ref, ritz_ref):
    ch, k, r = out_ref.shape
    s = jnp.sum(sums_ref[...], axis=0)
    row = lax.broadcasted_iota(jnp.int32, (k, 128), 0)
    cols = [spread(s, 2 * k + i) for i in range(k)]
    x = s
    for i in range(k):
        scale = 1.0 / cols[i][i : i + 1]
        pivot = x[i : i + 1] * scale
        x = jnp.where(row == i, pivot, x - cols[i] * pivot)
        for j in range(i + 1, k):
            part = cols[j][i : i + 1] * scale
            cols[j] = jnp.where(row == i, part, cols[j] - cols[i] * part)
    coef = x[:, 3 * k : 4 * k]
    eye = lax.broadcasted_iota(jnp.int32, (k, k), 0) == lax.broadcasted_iota(jnp.int32, (k, k), 1)
    ritz_ref[...] = jnp.sum(jnp.where(eye, coef, 0.0), axis=0, keepdims=True) * (1.0 / SCALE)
    s1, b1 = s[:, :k], s[:, k : 2 * k]
    s2, b2, aa = s[:, 4 * k : 5 * k], s[:, 5 * k : 6 * k], s[:, 6 * k : 7 * k]
    known = jnp.concatenate([x[:, :k], s1, s2], axis=0)
    known = known - dot32(jnp.concatenate([x[:, k : 2 * k], b1, b2], axis=0), coef)
    mix, corr, weighted = known[:k], known[k : 2 * k], known[2 * k :]
    gram = aa - dot32(
        jnp.concatenate([s2, coef, corr], axis=0), jnp.concatenate([coef, weighted, mix], axis=0), TN
    )
    cols = [spread(gram, i) for i in range(k)]
    pad = jnp.zeros((k, 128 - 3 * k), F32)
    x = jnp.concatenate([eye.astype(F32), -coef.T, -mix.T, pad], axis=1)
    for i in range(k):
        pivot = cols[i][i : i + 1]
        scale = 1.0 / pivot
        below = jnp.where(row > i, cols[i] * scale, 0.0)
        pivot_row = x[i : i + 1]
        x = jnp.where(row == i, pivot_row * (lax.rsqrt(pivot) * (total ** 0.5)), x - below * pivot_row)
        for j in range(i + 1, k):
            cols[j] = cols[j] - below * cols[j][i : i + 1]
    hi, mid, _ = split3(x[:, : 3 * k])
    lhs = jnp.concatenate([hi, hi, mid], axis=1)
    block = min(ch * r, 1024)

    def result(b, carry):
        at = pl.ds(pl.multiple_of(b * block, block), block)
        x_hi = jnp.concatenate([az_ref[:k, at], zhm_ref[: 2 * k, at]], axis=0)
        x_mid = jnp.concatenate([az_ref[k:, at], zhm_ref[2 * k :, at]], axis=0)
        new = lax.dot_general(
            lhs, jnp.concatenate([x_hi, x_mid, x_hi], axis=0), NN, preferred_element_type=F32
        )
        for i in range(block // r):
            out_ref[b * (block // r) + i] = new[:, i * r : (i + 1) * r]
        return carry

    lax.fori_loop(0, ch * r // block, result, 0)


def gather_sums(x):
    n_chan, n_rad = lax.axis_size("chan"), lax.axis_size("rad")
    step = 1
    while step < n_rad:
        x = x + swap(x, "rad", step)
        step *= 2
    every = jnp.broadcast_to(x, (n_chan,) + x.shape)
    return lax.all_to_all(every, "chan", split_axis=0, concat_axis=0, tiled=True)


def own_share(trial_block):
    n_rad = lax.axis_size("rad")
    ch, k, r = trial_block.shape
    me = lax.axis_index("rad")
    shares = trial_block.reshape(n_rad, ch // n_rad, k, r)
    got = []
    for d in range(n_rad):
        part = lax.dynamic_index_in_dim(shares, me ^ d, 0, keepdims=False).astype(BF16)
        got.append(swap(part, "rad", d) if d else part)
    lanes = []
    for c in range(n_rad):
        x = got[0]
        for d in range(1, n_rad):
            x = jnp.where(me ^ d == c, got[d], x)
        lanes.append(x)
    return jnp.concatenate(lanes, axis=2)


def body(trial_block, ham_blocks, partners, stored_at, precond_diag):
    n_chan, n_rad = lax.axis_size("chan"), lax.axis_size("rad")
    ch, k, r = trial_block.shape
    ncoup, splines = ham_blocks.shape[1], ham_blocks.shape[3]
    lanes = ch * r
    total = float(n_chan * n_rad * lanes)
    share, nz = ch // n_rad, n_chan // 4

    barrier = lax.optimization_barrier
    smem = pl.BlockSpec(memory_space=pltpu.SMEM)
    any_ = pl.BlockSpec(memory_space=pl.ANY)
    whole = pl.BlockSpec(memory_space=pltpu.VMEM)

    def near_of(x):
        return plane_swap(x, (1, 2))

    def far_of(x):
        return plane_swap(x, (2, 1))

    def in_cores(x):
        return [x] + [swap(x, "rad", c) for c in range(1, n_rad)]

    own = own_share(trial_block)[None]
    near0, far_own, diag0 = near_of(own), far_of(own), swap(own, "chan", 3)
    z1 = swap(own, "chan", 4)
    z_even = jnp.concatenate([swap(own, "chan", 4 * z) for z in range(2, nz, 2)])
    rows, ham, zhm, zl, dc, gram_t = pl.pallas_call(
        functools.partial(prepare_kernel, n_chan, n_rad),
        in_specs=[any_] * 5,
        out_specs=[whole] * 6,
        out_shape=[
            jax.ShapeDtypeStruct((ch, ncoup), jnp.int32),
            pltpu.VMEM(ham_blocks.shape, BF16),
            pltpu.VMEM((4 * k, lanes), BF16),
            pltpu.VMEM((2 * k, lanes), BF16),
            pltpu.VMEM((1, lanes), F32),
            pltpu.VMEM((k, 3 * k), F32),
        ],
        scratch_shapes=[
            pltpu.VMEM(trial_block.shape, F32),
            pltpu.VMEM(precond_diag.shape, F32),
            pltpu.VMEM((ncoup, ch), jnp.int32),
            pltpu.VMEM((stored_at.shape[0] // 128, 128), jnp.int32),
            pltpu.SemaphoreType.DMA((5,)),
        ],
        compiler_params=pltpu.CompilerParams(vmem_limit_bytes=VMEM_LIMIT),
        name="prepare",
    )(
        in_hbm(trial_block),
        in_hbm(precond_diag),
        in_hbm(partners.T),
        in_hbm(stored_at.reshape(-1, 128)),
        in_hbm(ham_blocks),
    )
    far_own, near0, diag0, z1, z_even, rows = barrier((far_own, near0, diag0, z1, z_even, rows))
    some = jnp.concatenate([z1, z_even])
    near1, far1 = near_of(some), far_of(some)
    z_odd = swap(z_even, "chan", 4)
    diag_odd = jnp.concatenate([swap(diag0, "chan", 4 * z) for z in range(3, nz, 2)])
    near1, z_odd = barrier((near1, z_odd))
    early = in_cores(jnp.concatenate([own, z1, z_even, near0, far_own, diag0, near1, z_odd]))
    near_odd = near_of(z_odd)
    far2 = far_of(jnp.concatenate([z_odd, near1]))
    table = pl.pallas_call(
        assemble_kernel,
        in_specs=[any_] * n_rad,
        out_specs=whole,
        out_shape=pltpu.VMEM((4 * nz * n_rad,) + own.shape[1:], BF16),
        scratch_shapes=[pltpu.SemaphoreType.DMA((n_rad,))],
        compiler_params=pltpu.CompilerParams(vmem_limit_bytes=VMEM_LIMIT),
        name="assemble",
    )(*early)
    last = barrier((diag_odd, far1, near_odd, far2, table))
    table = last[4]
    last = [in_vmem(x) for x in in_cores(jnp.concatenate(last[:4]))]

    az, sums, _ = pl.pallas_call(
        apply_kernel,
        in_specs=[smem] + [whole] * (6 + n_rad),
        out_specs=[whole, whole, whole],
        out_shape=[
            pltpu.VMEM((2 * k, lanes), BF16),
            jax.ShapeDtypeStruct((k, 8 * k), F32),
            pltpu.VMEM(table.shape, BF16),
        ],
        input_output_aliases={2: 2},
        scratch_shapes=[pltpu.VMEM((k, lanes), F32)],
        compiler_params=pltpu.CompilerParams(vmem_limit_bytes=VMEM_LIMIT),
        name="apply",
    )(rows, in_vmem(ham), in_vmem(table), in_vmem(zhm), in_vmem(zl), in_vmem(dc), gram_t, *last)

    sums = gather_sums(sums)
    new_block, ritz = pl.pallas_call(
        functools.partial(finish_kernel, total),
        out_shape=[
            jax.ShapeDtypeStruct((ch, k, r), F32),
            jax.ShapeDtypeStruct((1, k), F32),
        ],
        compiler_params=pltpu.CompilerParams(vmem_limit_bytes=VMEM_LIMIT),
        name="finish",
    )(sums, in_vmem(az), in_vmem(zhm))
    return (new_block, ritz.reshape(k))


def solution(mesh):
    return jax.shard_map(
        body,
        mesh=mesh,
        in_specs=(
            P("chan", None, "rad"),
            P("chan", None, "rad", None),
            P("chan", None),
            P(),
            P("chan", "rad"),
        ),
        out_specs=(P("chan", None, "rad"), P()),
        check_vma=False,
    )
```

```python
import functools

import jax
import jax.numpy as jnp
from jax import lax
from jax.experimental import pallas as pl
from jax.experimental.pallas import tpu as pltpu
from jax.sharding import PartitionSpec as P

SCALE = 2.0 ** -8
F32 = jnp.float32
BF16 = jnp.bfloat16
NT = (((1,), (1,)), ((), ()))
TN = (((0,), (0,)), ((), ()))
NN = (((1,), (0,)), ((), ()))
VMEM_LIMIT = 4 * 1024 * 1024


def swap(x, axis, distance):
    n = lax.axis_size(axis)
    return lax.ppermute(x, axis, [(i, i ^ distance) for i in range(n)])


def plane_swap(x, order):
    n_chan, n_rad = lax.axis_size("chan"), lax.axis_size("rad")
    pairs = []
    for c in range(n_chan):
        for r in range(n_rad):
            pairs.append((c * n_rad + r, (c ^ order[r % 2]) * n_rad + r))
    return lax.ppermute(x, ("chan", "rad"), pairs)


def table_piece(z, part, nz):
    some, odd = nz // 2, nz // 2 - 1
    is_odd = (z & 1 == 1) & (z > 1)
    i = jnp.where(is_odd, (z - 3) >> 1, jnp.where(z == 1, 0, z >> 1))
    base = 2 * some + odd + 4

    def pick(own, of_some, of_odd):
        return jnp.where(z == 0, own, jnp.where(is_odd, of_odd + i, of_some + i))

    here = pick(0, 1, 2 * some + 4)
    near = pick(some + 1, some + 4, base + odd + some)
    far = pick(some + 2, base + odd, base + 2 * odd + some)
    both = pick(some + 3, base + 3 * odd + some, base)
    return jnp.where(part == 0, here, jnp.where(part == 1, near, jnp.where(part == 2, far, both)))


def in_vmem(x):
    return pltpu.with_memory_space_constraint(x, pltpu.VMEM)


def in_hbm(x):
    return pltpu.with_memory_space_constraint(x, pltpu.HBM)


def split3(x):
    hi = x.astype(BF16)
    rest = x - hi.astype(F32)
    mid = rest.astype(BF16)
    return hi, mid, (rest - mid.astype(F32)).astype(BF16)


def dot32(x, y, dims=NN):
    return lax.dot_general(x, y, dims, precision=lax.Precision.HIGHEST, preferred_element_type=F32)


def block_sum(g, rows, cols):
    g = sum(g[i : i + rows] for i in range(0, g.shape[0], rows))
    return sum(g[:, i : i + cols] for i in range(0, g.shape[1], cols))


def prepare_kernel(
    n_chan, n_rad, t_hbm, d_hbm, partners_hbm, stored_hbm, ham_hbm,
    rows_ref, ham_ref, zhm_ref, zl_ref, dc_ref, gram_ref, t_ref, d_ref, partners_ref, stored_ref, sems,
):
    moves = (
        (t_hbm, t_ref), (d_hbm, d_ref), (partners_hbm, partners_ref), (stored_hbm, stored_ref), (ham_hbm, ham_ref)
    )
    copies = [pltpu.make_async_copy(x, y, sems.at[i]) for i, (x, y) in enumerate(moves)]
    for copy in copies:
        copy.start()
    for copy in copies[:4]:
        copy.wait()
    ch, k, r = t_ref.shape
    group = 128 // r
    for i in range(ch // group):
        lanes = pl.ds(i * 128, 128)
        t = jnp.concatenate([t_ref[i * group + g] for g in range(group)], axis=1)
        d = jnp.concatenate([d_ref[pl.ds(i * group + g, 1), :] for g in range(group)], axis=1)
        dc_ref[:, lanes] = d
        hi, mid, lo = split3(jnp.concatenate([t / d, t], axis=0))
        zhm_ref[:, lanes] = jnp.concatenate([hi, mid], axis=0)
        zl_ref[:, lanes] = lo
    z = jnp.concatenate([zhm_ref[...], zl_ref[...]], axis=0)
    g = block_sum(lax.dot_general(z, z, NT, preferred_element_type=F32), 2 * k, 2 * k)
    gram_ref[...] = jnp.concatenate([g[k:, :], g[:k, :k]], axis=1)

    share, nz = ch // n_rad, n_chan // 4
    q = stored_ref[...]
    owner, local = lax.div(q, ch), lax.rem(q, ch)
    core = lax.div(local, share)
    apart = (owner ^ lax.axis_index("chan")) & 3
    part = jnp.where((core & 1) == 1, ((apart & 1) << 1) | (apart >> 1), apart)
    piece = table_piece((owner ^ lax.axis_index("chan")) >> 2, part, nz)
    place = (core ^ lax.axis_index("rad")) * 4 * nz + piece
    place = (place * share + lax.rem(local, share)).astype(F32)
    lane = lax.broadcasted_iota(jnp.int32, (ch, 128), 1)
    columns = []
    partners = partners_ref[...].astype(F32).T.astype(jnp.int32)
    for j in range(partners.shape[1]):
        wanted = jnp.broadcast_to(partners[:, j : j + 1], (ch, 128)) - lane
        found = jnp.zeros((ch, 128), F32)
        for c in range(place.shape[0]):
            found = found + jnp.where(wanted == 128 * c, place[c : c + 1], 0.0)
        columns.append(jnp.sum(found, axis=1, keepdims=True))
    rows_ref[...] = jnp.concatenate(columns, axis=1).astype(jnp.int32)
    copies[4].wait()


def assemble_kernel(*refs):
    pieces, table_ref, sems = refs[:-2], refs[-2], refs[-1]
    each = table_ref.shape[0] // len(pieces)
    copies = []
    for i, piece in enumerate(pieces):
        place = table_ref.at[pl.ds(i * each, piece.shape[0])]
        copies.append(pltpu.make_async_copy(piece, place, sems.at[i]))
        copies[-1].start()
    for copy in copies:
        copy.wait()


def apply_kernel(rows_ref, ham_ref, _, zhm_ref, zl_ref, dc_ref, gt_ref, *rest):
    last, (az_ref, sums_ref, table_ref, a0_ref) = rest[:-4], rest[-4:]
    share = table_ref.shape[1]
    for c, piece in enumerate(last):
        start = (c + 1) * (table_ref.shape[0] // len(last)) - piece.shape[0]

        def put(i, carry, piece=piece, start=start):
            table_ref[start + i] = piece[i]
            return carry

        lax.fori_loop(0, piece.shape[0], put, 0)
    ch, ncoup, r, splines = ham_ref.shape
    k = zl_ref.shape[0] // 2
    group = 256 // r

    def row_of(n):
        return table_ref[lax.div(n, share), lax.rem(n, share)]

    def work(g, carry):
        left, right = [], []
        for i in range(group):
            p = g * group + i
            left.append(
                jnp.concatenate([row_of(rows_ref[p, j]) for j in range(ncoup)], axis=1)
            )
            right.append(jnp.concatenate([ham_ref[p, j] for j in range(ncoup)], axis=1))
        product = lax.dot_general(
            jnp.concatenate(left, axis=0),
            jnp.concatenate(right, axis=0),
            NT,
            preferred_element_type=F32,
        )
        own = [product[i * k : (i + 1) * k, i * r : (i + 1) * r] for i in range(group)]
        a0_ref[:, pl.ds(pl.multiple_of(g * 256, 256), 256)] = jnp.concatenate(own, axis=1) * SCALE
        return carry

    lax.fori_loop(0, ch // group, work, 0, unroll=min(4, ch // group))

    lanes = ch * r
    block = min(lanes, 1024)

    def gram_block(i, gram):
        at = pl.ds(pl.multiple_of(i * block, block), block)
        a0 = a0_ref[:, at]
        a1_terms = split3(a0 / dc_ref[:, at])
        az_ref[:, at] = jnp.concatenate(a1_terms[:2], axis=0)
        right = jnp.concatenate(a1_terms + split3(a0), axis=0)
        left = jnp.concatenate([zhm_ref[:, at], zl_ref[:, at], right[: 3 * k]], axis=0)
        return gram + lax.dot_general(left, right, NT, preferred_element_type=F32)

    gram = lax.fori_loop(0, lanes // block, gram_block, jnp.zeros((9 * k, 6 * k), F32))
    ta1 = block_sum(gram[: 6 * k, : 3 * k], 2 * k, k)
    ta0 = block_sum(gram[: 6 * k, 3 * k :], 2 * k, k)
    aa = block_sum(gram[6 * k :, : 3 * k], k, k)
    gt = gt_ref[...]
    parts = [ta1[k:], gt[:, : 2 * k], ta0[k:], ta1[:k], gt[:, 2 * k :], aa, jnp.zeros((k, k), F32)]
    sums_ref[...] = jnp.concatenate(parts, axis=1)


def spread(x, i):
    return jnp.broadcast_to(x[:, i : i + 1], (x.shape[0], 128))


def finish_kernel(total, sums_ref, az_ref, zhm_ref, out_ref, ritz_ref):
    ch, k, r = out_ref.shape
    s = jnp.sum(sums_ref[...], axis=0)
    row = lax.broadcasted_iota(jnp.int32, (k, 128), 0)
    cols = [spread(s, 2 * k + i) for i in range(k)]
    x = s
    for i in range(k):
        scale = 1.0 / cols[i][i : i + 1]
        pivot = x[i : i + 1] * scale
        x = jnp.where(row == i, pivot, x - cols[i] * pivot)
        for j in range(i + 1, k):
            part = cols[j][i : i + 1] * scale
            cols[j] = jnp.where(row == i, part, cols[j] - cols[i] * part)
    coef = x[:, 3 * k : 4 * k]
    eye = lax.broadcasted_iota(jnp.int32, (k, k), 0) == lax.broadcasted_iota(jnp.int32, (k, k), 1)
    ritz_ref[...] = jnp.sum(jnp.where(eye, coef, 0.0), axis=0, keepdims=True) * (1.0 / SCALE)
    s1, b1 = s[:, :k], s[:, k : 2 * k]
    s2, b2, aa = s[:, 4 * k : 5 * k], s[:, 5 * k : 6 * k], s[:, 6 * k : 7 * k]
    known = jnp.concatenate([x[:, :k], s1, s2], axis=0)
    known = known - dot32(jnp.concatenate([x[:, k : 2 * k], b1, b2], axis=0), coef)
    mix, corr, weighted = known[:k], known[k : 2 * k], known[2 * k :]
    gram = aa - dot32(
        jnp.concatenate([s2, coef, corr], axis=0), jnp.concatenate([coef, weighted, mix], axis=0), TN
    )
    cols = [spread(gram, i) for i in range(k)]
    pad = jnp.zeros((k, 128 - 3 * k), F32)
    x = jnp.concatenate([eye.astype(F32), -coef.T, -mix.T, pad], axis=1)
    for i in range(k):
        pivot = cols[i][i : i + 1]
        scale = 1.0 / pivot
        below = jnp.where(row > i, cols[i] * scale, 0.0)
        pivot_row = x[i : i + 1]
        x = jnp.where(row == i, pivot_row * (lax.rsqrt(pivot) * (total ** 0.5)), x - below * pivot_row)
        for j in range(i + 1, k):
            cols[j] = cols[j] - below * cols[j][i : i + 1]
    hi, mid, _ = split3(x[:, : 3 * k])
    lhs = jnp.concatenate([hi, hi, mid], axis=1)
    block = min(ch * r, 1024)

    def result(b, carry):
        at = pl.ds(pl.multiple_of(b * block, block), block)
        x_hi = jnp.concatenate([az_ref[:k, at], zhm_ref[: 2 * k, at]], axis=0)
        x_mid = jnp.concatenate([az_ref[k:, at], zhm_ref[2 * k :, at]], axis=0)
        new = lax.dot_general(
            lhs, jnp.concatenate([x_hi, x_mid, x_hi], axis=0), NN, preferred_element_type=F32
        )
        for i in range(block // r):
            out_ref[b * (block // r) + i] = new[:, i * r : (i + 1) * r]
        return carry

    lax.fori_loop(0, ch * r // block, result, 0)


def gather_sums(x):
    n_chan, n_rad = lax.axis_size("chan"), lax.axis_size("rad")
    step = 1
    while step < n_rad:
        x = x + swap(x, "rad", step)
        step *= 2
    every = jnp.broadcast_to(x, (n_chan,) + x.shape)
    return lax.all_to_all(every, "chan", split_axis=0, concat_axis=0, tiled=True)


def own_share(trial_block):
    n_rad = lax.axis_size("rad")
    ch, k, r = trial_block.shape
    me = lax.axis_index("rad")
    rounded = trial_block.astype(BF16).reshape(n_rad, ch // n_rad, k, r)
    got = []
    for d in range(n_rad):
        part = lax.dynamic_index_in_dim(rounded, me ^ d, 0, keepdims=False)
        got.append(swap(part, "rad", d) if d else part)
    lanes = []
    for c in range(n_rad):
        x = got[0]
        for d in range(1, n_rad):
            x = jnp.where(me ^ d == c, got[d], x)
        lanes.append(x)
    return jnp.concatenate(lanes, axis=2)


def body(trial_block, ham_blocks, partners, stored_at, precond_diag):
    n_chan, n_rad = lax.axis_size("chan"), lax.axis_size("rad")
    ch, k, r = trial_block.shape
    ncoup, splines = ham_blocks.shape[1], ham_blocks.shape[3]
    lanes = ch * r
    total = float(n_chan * n_rad * lanes)
    share, nz = ch // n_rad, n_chan // 4

    barrier = lax.optimization_barrier
    smem = pl.BlockSpec(memory_space=pltpu.SMEM)
    any_ = pl.BlockSpec(memory_space=pl.ANY)
    whole = pl.BlockSpec(memory_space=pltpu.VMEM)

    def near_of(x):
        return plane_swap(x, (1, 2))

    def far_of(x):
        return plane_swap(x, (2, 1))

    def in_cores(x):
        return [x] + [swap(x, "rad", c) for c in range(1, n_rad)]

    own = own_share(trial_block)[None]
    near0, far_own, diag0 = near_of(own), far_of(own), swap(own, "chan", 3)
    z1 = swap(own, "chan", 4)
    z_even = jnp.concatenate([swap(own, "chan", 4 * z) for z in range(2, nz, 2)])
    z1, far_own, near0, diag0, z_even = barrier((z1, far_own, near0, diag0, z_even))
    some = jnp.concatenate([z1, z_even])
    near1, far1 = near_of(some), far_of(some)
    z_odd = swap(z_even, "chan", 4)
    diag_odd = jnp.concatenate([swap(diag0, "chan", 4 * z) for z in range(3, nz, 2)])
    inputs = (trial_block, precond_diag, partners, stored_at, ham_blocks)
    diag_odd, z_odd, far1, near1, inputs = barrier((diag_odd, z_odd, far1, near1, inputs))
    trial_block, precond_diag, partners, stored_at, ham_blocks = inputs
    early = in_cores(
        jnp.concatenate([own, z1, z_even, near0, far_own, diag0, near1, z_odd, diag_odd, far1])
    )
    near_odd = near_of(z_odd)
    far2 = far_of(jnp.concatenate([z_odd, near1]))
    rows, ham, zhm, zl, dc, gram_t = pl.pallas_call(
        functools.partial(prepare_kernel, n_chan, n_rad),
        in_specs=[any_] * 5,
        out_specs=[whole] * 6,
        out_shape=[
            jax.ShapeDtypeStruct((ch, ncoup), jnp.int32),
            pltpu.VMEM(ham_blocks.shape, BF16),
            pltpu.VMEM((4 * k, lanes), BF16),
            pltpu.VMEM((2 * k, lanes), BF16),
            pltpu.VMEM((1, lanes), F32),
            pltpu.VMEM((k, 3 * k), F32),
        ],
        scratch_shapes=[
            pltpu.VMEM(trial_block.shape, F32),
            pltpu.VMEM(precond_diag.shape, F32),
            pltpu.VMEM((ncoup, ch), jnp.int32),
            pltpu.VMEM((stored_at.shape[0] // 128, 128), jnp.int32),
            pltpu.SemaphoreType.DMA((5,)),
        ],
        compiler_params=pltpu.CompilerParams(vmem_limit_bytes=VMEM_LIMIT),
        name="prepare",
    )(
        in_hbm(trial_block),
        in_hbm(precond_diag),
        in_hbm(partners.T),
        in_hbm(stored_at.reshape(-1, 128)),
        in_hbm(ham_blocks),
    )
    table = pl.pallas_call(
        assemble_kernel,
        in_specs=[any_] * n_rad,
        out_specs=whole,
        out_shape=pltpu.VMEM((4 * nz * n_rad,) + own.shape[1:], BF16),
        scratch_shapes=[pltpu.SemaphoreType.DMA((n_rad,))],
        compiler_params=pltpu.CompilerParams(vmem_limit_bytes=VMEM_LIMIT),
        name="assemble",
    )(*early)
    near_odd, far2, table, rows = barrier((near_odd, far2, table, rows))
    last = [in_vmem(x) for x in in_cores(jnp.concatenate([near_odd, far2]))]

    az, sums, _ = pl.pallas_call(
        apply_kernel,
        in_specs=[smem] + [whole] * (6 + n_rad),
        out_specs=[whole, whole, whole],
        out_shape=[
            pltpu.VMEM((2 * k, lanes), BF16),
            jax.ShapeDtypeStruct((k, 8 * k), F32),
            pltpu.VMEM(table.shape, BF16),
        ],
        input_output_aliases={2: 2},
        scratch_shapes=[pltpu.VMEM((k, lanes), F32)],
        compiler_params=pltpu.CompilerParams(vmem_limit_bytes=VMEM_LIMIT),
        name="apply",
    )(rows, in_vmem(ham), in_vmem(table), in_vmem(zhm), in_vmem(zl), in_vmem(dc), gram_t, *last)

    sums = gather_sums(sums)
    new_block, ritz = pl.pallas_call(
        functools.partial(finish_kernel, total),
        out_shape=[
            jax.ShapeDtypeStruct((ch, k, r), F32),
            jax.ShapeDtypeStruct((1, k), F32),
        ],
        compiler_params=pltpu.CompilerParams(vmem_limit_bytes=VMEM_LIMIT),
        name="finish",
    )(sums, in_vmem(az), in_vmem(zhm))
    return (new_block, ritz.reshape(k))


def solution(mesh):
    return jax.shard_map(
        body,
        mesh=mesh,
        in_specs=(
            P("chan", None, "rad"),
            P("chan", None, "rad", None),
            P("chan", None),
            P(),
            P("chan", "rad"),
        ),
        out_specs=(P("chan", None, "rad"), P()),
        check_vma=False,
    )
```

```python
import functools

import jax
import jax.numpy as jnp
from jax import lax
from jax.experimental import pallas as pl
from jax.experimental.pallas import tpu as pltpu
from jax.sharding import PartitionSpec as P

SCALE = 2.0 ** -8
F32 = jnp.float32
BF16 = jnp.bfloat16
NT = (((1,), (1,)), ((), ()))
TN = (((0,), (0,)), ((), ()))
NN = (((1,), (0,)), ((), ()))
VMEM_LIMIT = 4 * 1024 * 1024


def swap(x, axis, distance):
    n = lax.axis_size(axis)
    return lax.ppermute(x, axis, [(i, i ^ distance) for i in range(n)])


def plane_swap(x, order):
    n_chan, n_rad = lax.axis_size("chan"), lax.axis_size("rad")
    pairs = []
    for c in range(n_chan):
        for r in range(n_rad):
            pairs.append((c * n_rad + r, (c ^ order[r % 2]) * n_rad + r))
    return lax.ppermute(x, ("chan", "rad"), pairs)


def table_piece(z, part, nz):
    some, odd = nz // 2, nz // 2 - 1
    is_odd = (z & 1 == 1) & (z > 1)
    i = jnp.where(is_odd, (z - 3) >> 1, jnp.where(z == 1, 0, z >> 1))
    base = 2 * some + odd + 4

    def pick(own, of_some, of_odd):
        return jnp.where(z == 0, own, jnp.where(is_odd, of_odd + i, of_some + i))

    here = pick(0, 1, 2 * some + 4)
    near = pick(some + 1, some + 4, base + odd + some)
    far = pick(some + 2, base + odd, base + 2 * odd + some)
    both = jnp.where(z == 1, 4 * nz - 1, pick(some + 3, base + 3 * odd + some - 1, base))
    return jnp.where(part == 0, here, jnp.where(part == 1, near, jnp.where(part == 2, far, both)))


def in_vmem(x):
    return pltpu.with_memory_space_constraint(x, pltpu.VMEM)


def in_hbm(x):
    return pltpu.with_memory_space_constraint(x, pltpu.HBM)


def split3(x):
    hi = x.astype(BF16)
    rest = x - hi.astype(F32)
    mid = rest.astype(BF16)
    return hi, mid, (rest - mid.astype(F32)).astype(BF16)


def dot32(x, y, dims=NN):
    return lax.dot_general(x, y, dims, precision=lax.Precision.HIGHEST, preferred_element_type=F32)


def block_sum(g, rows, cols):
    g = sum(g[i : i + rows] for i in range(0, g.shape[0], rows))
    return sum(g[:, i : i + cols] for i in range(0, g.shape[1], cols))


def prepare_kernel(
    n_chan, n_rad, t_hbm, d_hbm, partners_hbm, stored_hbm, ham_hbm,
    rows_ref, ham_ref, zhm_ref, zl_ref, dc_ref, gram_ref, t_ref, d_ref, partners_ref, stored_ref, sems,
):
    moves = (
        (t_hbm, t_ref), (d_hbm, d_ref), (partners_hbm, partners_ref), (stored_hbm, stored_ref), (ham_hbm, ham_ref)
    )
    copies = [pltpu.make_async_copy(x, y, sems.at[i]) for i, (x, y) in enumerate(moves)]
    for copy in copies:
        copy.start()
    for copy in copies[:4]:
        copy.wait()
    ch, k, r = t_ref.shape
    group = 128 // r
    for i in range(ch // group):
        lanes = pl.ds(i * 128, 128)
        t = jnp.concatenate([t_ref[i * group + g] for g in range(group)], axis=1)
        d = jnp.concatenate([d_ref[pl.ds(i * group + g, 1), :] for g in range(group)], axis=1)
        dc_ref[:, lanes] = d
        hi, mid, lo = split3(jnp.concatenate([t / d, t], axis=0))
        zhm_ref[:, lanes] = jnp.concatenate([hi, mid], axis=0)
        zl_ref[:, lanes] = lo
    z = jnp.concatenate([zhm_ref[...], zl_ref[...]], axis=0)
    g = block_sum(lax.dot_general(z, z, NT, preferred_element_type=F32), 2 * k, 2 * k)
    gram_ref[...] = jnp.concatenate([g[k:, :], g[:k, :k]], axis=1)

    share, nz = ch // n_rad, n_chan // 4
    q = stored_ref[...]
    owner, local = lax.div(q, ch), lax.rem(q, ch)
    core = lax.div(local, share)
    apart = (owner ^ lax.axis_index("chan")) & 3
    part = jnp.where((core & 1) == 1, ((apart & 1) << 1) | (apart >> 1), apart)
    piece = table_piece((owner ^ lax.axis_index("chan")) >> 2, part, nz)
    place = (core ^ lax.axis_index("rad")) * 4 * nz + piece
    place = (place * share + lax.rem(local, share)).astype(F32)
    lane = lax.broadcasted_iota(jnp.int32, (ch, 128), 1)
    columns = []
    partners = partners_ref[...].astype(F32).T.astype(jnp.int32)
    for j in range(partners.shape[1]):
        wanted = jnp.broadcast_to(partners[:, j : j + 1], (ch, 128)) - lane
        found = jnp.zeros((ch, 128), F32)
        for c in range(place.shape[0]):
            found = found + jnp.where(wanted == 128 * c, place[c : c + 1], 0.0)
        columns.append(jnp.sum(found, axis=1, keepdims=True))
    rows_ref[...] = jnp.concatenate(columns, axis=1).astype(jnp.int32)
    copies[4].wait()


def assemble_kernel(*refs):
    pieces, table_ref, sems = refs[:-2], refs[-2], refs[-1]
    each = table_ref.shape[0] // len(pieces)
    copies = []
    for i, piece in enumerate(pieces):
        place = table_ref.at[pl.ds(i * each, piece.shape[0])]
        copies.append(pltpu.make_async_copy(piece, place, sems.at[i]))
        copies[-1].start()
    for copy in copies:
        copy.wait()


def apply_kernel(rows_ref, ham_ref, _, zhm_ref, zl_ref, dc_ref, gt_ref, *rest):
    last, (az_ref, sums_ref, table_ref, a0_ref) = rest[:-4], rest[-4:]
    for c, piece in enumerate(last):
        start = (c + 1) * (table_ref.shape[0] // len(last)) - piece.shape[0]
        step = min(32, piece.shape[0])

        def put(i, carry, piece=piece, start=start, step=step):
            table_ref[pl.ds(start + i * step, step)] = piece[pl.ds(i * step, step)]
            return carry

        lax.fori_loop(0, piece.shape[0] // step, put, 0)
    ch, ncoup, r, splines = ham_ref.shape
    k = zl_ref.shape[0] // 2
    group = 256 // r

    def work(g, carry):
        left, right = [], []
        for i in range(group):
            p = g * group + i
            left.append(
                jnp.concatenate([table_ref[rows_ref[p, j]] for j in range(ncoup)], axis=1)
            )
            right.append(jnp.concatenate([ham_ref[p, j] for j in range(ncoup)], axis=1))
        product = lax.dot_general(
            jnp.concatenate(left, axis=0),
            jnp.concatenate(right, axis=0),
            NT,
            preferred_element_type=F32,
        )
        own = [product[i * k : (i + 1) * k, i * r : (i + 1) * r] for i in range(group)]
        a0_ref[:, pl.ds(pl.multiple_of(g * 256, 256), 256)] = jnp.concatenate(own, axis=1) * SCALE
        return carry

    lax.fori_loop(0, ch // group, work, 0, unroll=min(4, ch // group))

    lanes = ch * r
    block = min(lanes, 1024)

    def gram_block(i, gram):
        at = pl.ds(pl.multiple_of(i * block, block), block)
        a0 = a0_ref[:, at]
        a1_terms = split3(a0 / dc_ref[:, at])
        az_ref[:, at] = jnp.concatenate(a1_terms[:2], axis=0)
        right = jnp.concatenate(a1_terms + split3(a0), axis=0)
        left = jnp.concatenate([zhm_ref[:, at], zl_ref[:, at], right[: 3 * k]], axis=0)
        return gram + lax.dot_general(left, right, NT, preferred_element_type=F32)

    gram = lax.fori_loop(0, lanes // block, gram_block, jnp.zeros((9 * k, 6 * k), F32))
    ta1 = block_sum(gram[: 6 * k, : 3 * k], 2 * k, k)
    ta0 = block_sum(gram[: 6 * k, 3 * k :], 2 * k, k)
    aa = block_sum(gram[6 * k :, : 3 * k], k, k)
    gt = gt_ref[...]
    parts = [ta1[k:], gt[:, : 2 * k], ta0[k:], ta1[:k], gt[:, 2 * k :], aa, jnp.zeros((k, k), F32)]
    sums_ref[...] = jnp.concatenate(parts, axis=1)


def spread(x, i):
    return jnp.broadcast_to(x[:, i : i + 1], (x.shape[0], 128))


def finish_kernel(total, sums_ref, az_ref, zhm_ref, out_ref, ritz_ref):
    ch, k, r = out_ref.shape
    s = jnp.sum(sums_ref[...], axis=0)
    row = lax.broadcasted_iota(jnp.int32, (k, 128), 0)
    cols = [spread(s, 2 * k + i) for i in range(k)]
    x = s
    for i in range(k):
        scale = 1.0 / cols[i][i : i + 1]
        pivot = x[i : i + 1] * scale
        x = jnp.where(row == i, pivot, x - cols[i] * pivot)
        for j in range(i + 1, k):
            part = cols[j][i : i + 1] * scale
            cols[j] = jnp.where(row == i, part, cols[j] - cols[i] * part)
    coef = x[:, 3 * k : 4 * k]
    eye = lax.broadcasted_iota(jnp.int32, (k, k), 0) == lax.broadcasted_iota(jnp.int32, (k, k), 1)
    ritz_ref[...] = jnp.sum(jnp.where(eye, coef, 0.0), axis=0, keepdims=True) * (1.0 / SCALE)
    s1, b1 = s[:, :k], s[:, k : 2 * k]
    s2, b2, aa = s[:, 4 * k : 5 * k], s[:, 5 * k : 6 * k], s[:, 6 * k : 7 * k]
    known = jnp.concatenate([x[:, :k], s1, s2], axis=0)
    known = known - dot32(jnp.concatenate([x[:, k : 2 * k], b1, b2], axis=0), coef)
    mix, corr, weighted = known[:k], known[k : 2 * k], known[2 * k :]
    gram = aa - dot32(
        jnp.concatenate([s2, coef, corr], axis=0), jnp.concatenate([coef, weighted, mix], axis=0), TN
    )
    cols = [spread(gram, i) for i in range(k)]
    pad = jnp.zeros((k, 128 - 3 * k), F32)
    x = jnp.concatenate([eye.astype(F32), -coef.T, -mix.T, pad], axis=1)
    for i in range(k):
        pivot = cols[i][i : i + 1]
        scale = 1.0 / pivot
        below = jnp.where(row > i, cols[i] * scale, 0.0)
        pivot_row = x[i : i + 1]
        x = jnp.where(row == i, pivot_row * (lax.rsqrt(pivot) * (total ** 0.5)), x - below * pivot_row)
        for j in range(i + 1, k):
            cols[j] = cols[j] - below * cols[j][i : i + 1]
    hi, mid, _ = split3(x[:, : 3 * k])
    lhs = jnp.concatenate([hi, hi, mid], axis=1)
    block = min(ch * r, 1024)

    def result(b, carry):
        at = pl.ds(pl.multiple_of(b * block, block), block)
        x_hi = jnp.concatenate([az_ref[:k, at], zhm_ref[: 2 * k, at]], axis=0)
        x_mid = jnp.concatenate([az_ref[k:, at], zhm_ref[2 * k :, at]], axis=0)
        new = lax.dot_general(
            lhs, jnp.concatenate([x_hi, x_mid, x_hi], axis=0), NN, preferred_element_type=F32
        )
        for i in range(block // r):
            out_ref[b * (block // r) + i] = new[:, i * r : (i + 1) * r]
        return carry

    lax.fori_loop(0, ch * r // block, result, 0)


def gather_sums(x):
    n_chan, n_rad = lax.axis_size("chan"), lax.axis_size("rad")
    step = 1
    while step < n_rad:
        x = x + swap(x, "rad", step)
        step *= 2
    every = jnp.broadcast_to(x, (n_chan,) + x.shape)
    return lax.all_to_all(every, "chan", split_axis=0, concat_axis=0, tiled=True)


def own_share(trial_block):
    n_rad = lax.axis_size("rad")
    ch, k, r = trial_block.shape
    me = lax.axis_index("rad")
    rounded = trial_block.astype(BF16).reshape(n_rad, ch // n_rad, k, r)
    got = []
    for d in range(n_rad):
        part = lax.dynamic_index_in_dim(rounded, me ^ d, 0, keepdims=False)
        got.append(swap(part, "rad", d) if d else part)
    lanes = []
    for c in range(n_rad):
        x = got[0]
        for d in range(1, n_rad):
            x = jnp.where(me ^ d == c, got[d], x)
        lanes.append(x)
    return jnp.concatenate(lanes, axis=2)


def body(trial_block, ham_blocks, partners, stored_at, precond_diag):
    n_chan, n_rad = lax.axis_size("chan"), lax.axis_size("rad")
    ch, k, r = trial_block.shape
    ncoup, splines = ham_blocks.shape[1], ham_blocks.shape[3]
    lanes = ch * r
    total = float(n_chan * n_rad * lanes)
    share, nz = ch // n_rad, n_chan // 4

    barrier = lax.optimization_barrier
    smem = pl.BlockSpec(memory_space=pltpu.SMEM)
    any_ = pl.BlockSpec(memory_space=pl.ANY)
    whole = pl.BlockSpec(memory_space=pltpu.VMEM)

    def near_of(x):
        return plane_swap(x, (1, 2))

    def far_of(x):
        return plane_swap(x, (2, 1))

    def flat(x):
        return x.reshape((-1,) + x.shape[2:])

    def in_cores(x):
        return [x] + [swap(x, "rad", c) for c in range(1, n_rad)]

    own = own_share(trial_block)[None]
    near0, far_own, diag0 = near_of(own), far_of(own), swap(own, "chan", 3)
    z1 = swap(own, "chan", 4)
    z_even = jnp.concatenate([swap(own, "chan", 4 * z) for z in range(2, nz, 2)])
    z1, far_own, near0, diag0, z_even = barrier((z1, far_own, near0, diag0, z_even))
    some, z_even, diag0 = barrier((jnp.concatenate([z1, z_even]), z_even, diag0))
    near1, far1 = near_of(some), far_of(some)
    z_odd = swap(z_even, "chan", 4)
    diag_odd = jnp.concatenate([swap(diag0, "chan", 4 * z) for z in range(3, nz, 2)])
    inputs = (trial_block, precond_diag, partners, stored_at, ham_blocks)
    diag_odd, z_odd, far1, near1, diag0, inputs = barrier(
        (diag_odd, z_odd, far1, near1, diag0, inputs)
    )
    trial_block, precond_diag, partners, stored_at, ham_blocks = inputs
    early = in_cores(
        jnp.concatenate([own, z1, z_even, near0, far_own, diag0, near1, z_odd, diag_odd, far1])
    )
    near_odd, diag1 = near_of(z_odd), swap(diag0, "chan", 4)
    far2 = far_of(jnp.concatenate([z_odd, near1[1:]]))
    rows, ham, zhm, zl, dc, gram_t = pl.pallas_call(
        functools.partial(prepare_kernel, n_chan, n_rad),
        in_specs=[any_] * 5,
        out_specs=[whole] * 6,
        out_shape=[
            jax.ShapeDtypeStruct((ch, ncoup), jnp.int32),
            pltpu.VMEM(ham_blocks.shape, BF16),
            pltpu.VMEM((4 * k, lanes), BF16),
            pltpu.VMEM((2 * k, lanes), BF16),
            pltpu.VMEM((1, lanes), F32),
            pltpu.VMEM((k, 3 * k), F32),
        ],
        scratch_shapes=[
            pltpu.VMEM(trial_block.shape, F32),
            pltpu.VMEM(precond_diag.shape, F32),
            pltpu.VMEM((ncoup, ch), jnp.int32),
            pltpu.VMEM((stored_at.shape[0] // 128, 128), jnp.int32),
            pltpu.SemaphoreType.DMA((5,)),
        ],
        compiler_params=pltpu.CompilerParams(vmem_limit_bytes=VMEM_LIMIT),
        name="prepare",
    )(
        in_hbm(trial_block),
        in_hbm(precond_diag),
        in_hbm(partners.T),
        in_hbm(stored_at.reshape(-1, 128)),
        in_hbm(ham_blocks),
    )
    table = pl.pallas_call(
        assemble_kernel,
        in_specs=[any_] * n_rad,
        out_specs=whole,
        out_shape=pltpu.VMEM((n_chan * ch, k, splines), BF16),
        scratch_shapes=[pltpu.SemaphoreType.DMA((n_rad,))],
        compiler_params=pltpu.CompilerParams(vmem_limit_bytes=VMEM_LIMIT),
        name="assemble",
    )(*[flat(x) for x in early])
    diag1, near_odd, far2, table, rows = barrier((diag1, near_odd, far2, table, rows))
    last = [in_vmem(flat(x)) for x in in_cores(jnp.concatenate([near_odd, far2, diag1]))]

    az, sums, _ = pl.pallas_call(
        apply_kernel,
        in_specs=[smem] + [whole] * (6 + n_rad),
        out_specs=[whole, whole, whole],
        out_shape=[
            pltpu.VMEM((2 * k, lanes), BF16),
            jax.ShapeDtypeStruct((k, 8 * k), F32),
            pltpu.VMEM(table.shape, BF16),
        ],
        input_output_aliases={2: 2},
        scratch_shapes=[pltpu.VMEM((k, lanes), F32)],
        compiler_params=pltpu.CompilerParams(vmem_limit_bytes=VMEM_LIMIT),
        name="apply",
    )(rows, in_vmem(ham), in_vmem(table), in_vmem(zhm), in_vmem(zl), in_vmem(dc), gram_t, *last)

    sums = gather_sums(sums)
    new_block, ritz = pl.pallas_call(
        functools.partial(finish_kernel, total),
        out_shape=[
            jax.ShapeDtypeStruct((ch, k, r), F32),
            jax.ShapeDtypeStruct((1, k), F32),
        ],
        compiler_params=pltpu.CompilerParams(vmem_limit_bytes=VMEM_LIMIT),
        name="finish",
    )(sums, in_vmem(az), in_vmem(zhm))
    return (new_block, ritz.reshape(k))


def solution(mesh):
    return jax.shard_map(
        body,
        mesh=mesh,
        in_specs=(
            P("chan", None, "rad"),
            P("chan", None, "rad", None),
            P("chan", None),
            P(),
            P("chan", "rad"),
        ),
        out_specs=(P("chan", None, "rad"), P()),
        check_vma=False,
    )
```

```python
import functools

import jax
import jax.numpy as jnp
from jax import lax
from jax.experimental import pallas as pl
from jax.experimental.pallas import tpu as pltpu
from jax.sharding import PartitionSpec as P

SCALE = 2.0 ** -8
F32 = jnp.float32
BF16 = jnp.bfloat16
NT = (((1,), (1,)), ((), ()))
TN = (((0,), (0,)), ((), ()))
NN = (((1,), (0,)), ((), ()))
VMEM_LIMIT = 4 * 1024 * 1024


def swap(x, axis, distance):
    n = lax.axis_size(axis)
    return lax.ppermute(x, axis, [(i, i ^ distance) for i in range(n)])


def plane_swap(x, order):
    n_chan, n_rad = lax.axis_size("chan"), lax.axis_size("rad")
    pairs = []
    for c in range(n_chan):
        for r in range(n_rad):
            pairs.append((c * n_rad + r, (c ^ order[r % 2]) * n_rad + r))
    return lax.ppermute(x, ("chan", "rad"), pairs)


def early_pieces(nz):
    some, odd = [1] + list(range(2, nz, 2)), list(range(3, nz, 2))
    order = [(0, 0)] + [(z, 0) for z in some] + [(0, 1), (0, 2), (0, 3)] + [(z, 1) for z in some]
    return order + [(z, 0) for z in odd] + [(z, 3) for z in odd] + [(z, 2) for z in some]


def late_pieces(nz):
    even, odd = list(range(2, nz, 2)), list(range(3, nz, 2))
    return [(z, 1) for z in odd] + [(z, 2) for z in odd] + [(z, 3) for z in even] + [(1, 3)]


def table_piece(z, part, nz):
    some, odd = nz // 2, nz // 2 - 1
    is_odd = (z & 1 == 1) & (z > 1)
    i = jnp.where(is_odd, (z - 3) >> 1, jnp.where(z == 1, 0, z >> 1))
    base = 2 * some + odd + 4

    def pick(own, of_some, of_odd):
        return jnp.where(z == 0, own, jnp.where(is_odd, of_odd + i, of_some + i))

    here = pick(0, 1, 2 * some + 4)
    near = pick(some + 1, some + 4, base + odd + some)
    far = pick(some + 2, base + odd, base + 2 * odd + some)
    both = jnp.where(z == 1, 4 * nz - 1, pick(some + 3, base + 3 * odd + some - 1, base))
    return jnp.where(part == 0, here, jnp.where(part == 1, near, jnp.where(part == 2, far, both)))


def merge(refs, table_ref, order, start, share):
    n_rad = len(refs)
    r = 128 // n_rad
    me = lax.axis_index("rad")

    def rows(n, carry):
        for i, (z, part) in enumerate(order):
            other = order.index((z, (0, 2, 1, 3)[part]))
            tiles = [ref[(other if s % 2 else i) * share + n] for s, ref in enumerate(refs)]
            by_core = []
            for c in range(n_rad):
                x = tiles[0]
                for s in range(1, n_rad):
                    x = jnp.where((me ^ s) == c, tiles[s], x)
                by_core.append(x)
            for g in range(n_rad):
                row = jnp.concatenate([x[:, g * r : (g + 1) * r] for x in by_core], axis=1)
                table_ref[((start + i) * n_rad + g) * share + n] = row
        return carry

    lax.fori_loop(0, share, rows, 0)


def in_vmem(x):
    return pltpu.with_memory_space_constraint(x, pltpu.VMEM)


def in_hbm(x):
    return pltpu.with_memory_space_constraint(x, pltpu.HBM)


def split3(x):
    hi = x.astype(BF16)
    rest = x - hi.astype(F32)
    mid = rest.astype(BF16)
    return hi, mid, (rest - mid.astype(F32)).astype(BF16)


def dot32(x, y, dims=NN):
    return lax.dot_general(x, y, dims, precision=lax.Precision.HIGHEST, preferred_element_type=F32)


def block_sum(g, rows, cols):
    g = sum(g[i : i + rows] for i in range(0, g.shape[0], rows))
    return sum(g[:, i : i + cols] for i in range(0, g.shape[1], cols))


def prepare_kernel(
    n_chan, n_rad, t_hbm, d_hbm, partners_hbm, stored_hbm, ham_hbm,
    rows_ref, ham_ref, zhm_ref, zl_ref, dc_ref, gram_ref, t_ref, d_ref, partners_ref, stored_ref, sems,
):
    moves = (
        (t_hbm, t_ref), (d_hbm, d_ref), (partners_hbm, partners_ref), (stored_hbm, stored_ref), (ham_hbm, ham_ref)
    )
    copies = [pltpu.make_async_copy(x, y, sems.at[i]) for i, (x, y) in enumerate(moves)]
    for copy in copies:
        copy.start()
    for copy in copies[:4]:
        copy.wait()
    ch, k, r = t_ref.shape
    group = 128 // r
    for i in range(ch // group):
        lanes = pl.ds(i * 128, 128)
        t = jnp.concatenate([t_ref[i * group + g] for g in range(group)], axis=1)
        d = jnp.concatenate([d_ref[pl.ds(i * group + g, 1), :] for g in range(group)], axis=1)
        dc_ref[:, lanes] = d
        hi, mid, lo = split3(jnp.concatenate([t / d, t], axis=0))
        zhm_ref[:, lanes] = jnp.concatenate([hi, mid], axis=0)
        zl_ref[:, lanes] = lo
    z = jnp.concatenate([zhm_ref[...], zl_ref[...]], axis=0)
    g = block_sum(lax.dot_general(z, z, NT, preferred_element_type=F32), 2 * k, 2 * k)
    gram_ref[...] = jnp.concatenate([g[k:, :], g[:k, :k]], axis=1)

    share, nz = ch // n_rad, n_chan // 4
    q = stored_ref[...]
    owner, local = lax.div(q, ch), lax.rem(q, ch)
    apart = (owner ^ lax.axis_index("chan")) & 3
    turned = ((apart & 1) << 1) | (apart >> 1)
    part = jnp.where((lax.axis_index("rad") & 1) == 1, turned, apart)
    piece = table_piece((owner ^ lax.axis_index("chan")) >> 2, part, nz)
    place = (piece * ch + local).astype(F32)
    lane = lax.broadcasted_iota(jnp.int32, (ch, 128), 1)
    columns = []
    partners = partners_ref[...].astype(F32).T.astype(jnp.int32)
    for j in range(partners.shape[1]):
        wanted = jnp.broadcast_to(partners[:, j : j + 1], (ch, 128)) - lane
        found = jnp.zeros((ch, 128), F32)
        for c in range(place.shape[0]):
            found = found + jnp.where(wanted == 128 * c, place[c : c + 1], 0.0)
        columns.append(jnp.sum(found, axis=1, keepdims=True))
    rows_ref[...] = jnp.concatenate(columns, axis=1).astype(jnp.int32)
    copies[4].wait()


def assemble_kernel(nz, share, *refs):
    merge(refs[:-1], refs[-1], early_pieces(nz), 0, share)


def apply_kernel(nz, share, rows_ref, ham_ref, _, zhm_ref, zl_ref, dc_ref, gt_ref, *rest):
    last, (az_ref, sums_ref, table_ref) = rest[:-3], rest[-3:]
    merge(last, table_ref, late_pieces(nz), len(early_pieces(nz)), share)
    ch, ncoup, r, splines = ham_ref.shape
    k = zl_ref.shape[0] // 2
    group = 256 // r

    def work(g, gram):
        left, right = [], []
        for i in range(group):
            p = g * group + i
            left.append(
                jnp.concatenate([table_ref[rows_ref[p, j]] for j in range(ncoup)], axis=1)
            )
            right.append(jnp.concatenate([ham_ref[p, j] for j in range(ncoup)], axis=1))
        product = lax.dot_general(
            jnp.concatenate(left, axis=0),
            jnp.concatenate(right, axis=0),
            NT,
            preferred_element_type=F32,
        )
        own = [product[i * k : (i + 1) * k, i * r : (i + 1) * r] for i in range(group)]
        at = pl.ds(pl.multiple_of(g * 256, 256), 256)
        a0 = jnp.concatenate(own, axis=1) * SCALE
        a1_terms = split3(a0 / dc_ref[:, at])
        az_ref[:, at] = jnp.concatenate(a1_terms[:2], axis=0)
        right = jnp.concatenate(a1_terms + split3(a0), axis=0)
        left = jnp.concatenate([zhm_ref[:, at], zl_ref[:, at], right[: 3 * k]], axis=0)
        return gram + lax.dot_general(left, right, NT, preferred_element_type=F32)

    groups = ch // group
    gram = lax.fori_loop(0, groups, work, jnp.zeros((9 * k, 6 * k), F32), unroll=min(4, groups))
    ta1 = block_sum(gram[: 6 * k, : 3 * k], 2 * k, k)
    ta0 = block_sum(gram[: 6 * k, 3 * k :], 2 * k, k)
    aa = block_sum(gram[6 * k :, : 3 * k], k, k)
    gt = gt_ref[...]
    parts = [ta1[k:], gt[:, : 2 * k], ta0[k:], ta1[:k], gt[:, 2 * k :], aa, jnp.zeros((k, k), F32)]
    sums_ref[...] = jnp.concatenate(parts, axis=1)


def spread(x, i):
    return jnp.broadcast_to(x[:, i : i + 1], (x.shape[0], 128))


def finish_kernel(total, sums_ref, az_ref, zhm_ref, out_ref, ritz_ref):
    ch, k, r = out_ref.shape
    s = jnp.sum(sums_ref[...], axis=0)
    row = lax.broadcasted_iota(jnp.int32, (k, 128), 0)
    cols = [spread(s, 2 * k + i) for i in range(k)]
    x = s
    for i in range(k):
        scale = 1.0 / cols[i][i : i + 1]
        pivot = x[i : i + 1] * scale
        x = jnp.where(row == i, pivot, x - cols[i] * pivot)
        for j in range(i + 1, k):
            part = cols[j][i : i + 1] * scale
            cols[j] = jnp.where(row == i, part, cols[j] - cols[i] * part)
    coef = x[:, 3 * k : 4 * k]
    eye = lax.broadcasted_iota(jnp.int32, (k, k), 0) == lax.broadcasted_iota(jnp.int32, (k, k), 1)
    ritz_ref[...] = jnp.sum(jnp.where(eye, coef, 0.0), axis=0, keepdims=True) * (1.0 / SCALE)
    s1, b1 = s[:, :k], s[:, k : 2 * k]
    s2, b2, aa = s[:, 4 * k : 5 * k], s[:, 5 * k : 6 * k], s[:, 6 * k : 7 * k]
    known = jnp.concatenate([x[:, :k], s1, s2], axis=0)
    known = known - dot32(jnp.concatenate([x[:, k : 2 * k], b1, b2], axis=0), coef)
    mix, corr, weighted = known[:k], known[k : 2 * k], known[2 * k :]
    gram = aa - dot32(
        jnp.concatenate([s2, coef, corr], axis=0), jnp.concatenate([coef, weighted, mix], axis=0), TN
    )
    cols = [spread(gram, i) for i in range(k)]
    pad = jnp.zeros((k, 128 - 3 * k), F32)
    x = jnp.concatenate([eye.astype(F32), -coef.T, -mix.T, pad], axis=1)
    for i in range(k):
        pivot = cols[i][i : i + 1]
        scale = 1.0 / pivot
        below = jnp.where(row > i, cols[i] * scale, 0.0)
        pivot_row = x[i : i + 1]
        x = jnp.where(row == i, pivot_row * (lax.rsqrt(pivot) * (total ** 0.5)), x - below * pivot_row)
        for j in range(i + 1, k):
            cols[j] = cols[j] - below * cols[j][i : i + 1]
    hi, mid, _ = split3(x[:, : 3 * k])
    lhs = jnp.concatenate([hi, hi, mid], axis=1)
    block = min(ch * r, 1024)

    def result(b, carry):
        at = pl.ds(pl.multiple_of(b * block, block), block)
        x_hi = jnp.concatenate([az_ref[:k, at], zhm_ref[: 2 * k, at]], axis=0)
        x_mid = jnp.concatenate([az_ref[k:, at], zhm_ref[2 * k :, at]], axis=0)
        new = lax.dot_general(
            lhs, jnp.concatenate([x_hi, x_mid, x_hi], axis=0), NN, preferred_element_type=F32
        )
        for i in range(block // r):
            out_ref[b * (block // r) + i] = new[:, i * r : (i + 1) * r]
        return carry

    lax.fori_loop(0, ch * r // block, result, 0)


def gather_sums(x):
    n_chan, n_rad = lax.axis_size("chan"), lax.axis_size("rad")
    step = 1
    while step < n_rad:
        x = x + swap(x, "rad", step)
        step *= 2
    every = jnp.broadcast_to(x, (n_chan,) + x.shape)
    return lax.all_to_all(every, "chan", split_axis=0, concat_axis=0, tiled=True)


def body(trial_block, ham_blocks, partners, stored_at, precond_diag):
    n_chan, n_rad = lax.axis_size("chan"), lax.axis_size("rad")
    ch, k, r = trial_block.shape
    ncoup, splines = ham_blocks.shape[1], ham_blocks.shape[3]
    lanes = ch * r
    total = float(n_chan * n_rad * lanes)
    share, nz = ch // n_rad, n_chan // 4

    barrier = lax.optimization_barrier
    smem = pl.BlockSpec(memory_space=pltpu.SMEM)
    any_ = pl.BlockSpec(memory_space=pl.ANY)
    whole = pl.BlockSpec(memory_space=pltpu.VMEM)

    def near_of(x):
        return plane_swap(x, (1, 2))

    def far_of(x):
        return plane_swap(x, (2, 1))

    def flat(x):
        return x.reshape((-1,) + x.shape[2:])

    def in_cores(x):
        return [x] + [swap(x, "rad", c) for c in range(1, n_rad)]

    own = jnp.concatenate(jnp.split(trial_block.astype(BF16), n_rad), axis=2)[None]
    near0, far_own, diag0 = near_of(own), far_of(own), swap(own, "chan", 3)
    z1 = swap(own, "chan", 4)
    z_even = jnp.concatenate([swap(own, "chan", 4 * z) for z in range(2, nz, 2)])
    rows, ham, zhm, zl, dc, gram_t = pl.pallas_call(
        functools.partial(prepare_kernel, n_chan, n_rad),
        in_specs=[any_] * 5,
        out_specs=[whole] * 6,
        out_shape=[
            jax.ShapeDtypeStruct((ch, ncoup), jnp.int32),
            pltpu.VMEM(ham_blocks.shape, BF16),
            pltpu.VMEM((4 * k, lanes), BF16),
            pltpu.VMEM((2 * k, lanes), BF16),
            pltpu.VMEM((1, lanes), F32),
            pltpu.VMEM((k, 3 * k), F32),
        ],
        scratch_shapes=[
            pltpu.VMEM(trial_block.shape, F32),
            pltpu.VMEM(precond_diag.shape, F32),
            pltpu.VMEM((ncoup, ch), jnp.int32),
            pltpu.VMEM((stored_at.shape[0] // 128, 128), jnp.int32),
            pltpu.SemaphoreType.DMA((5,)),
        ],
        compiler_params=pltpu.CompilerParams(vmem_limit_bytes=VMEM_LIMIT),
        name="prepare",
    )(
        in_hbm(trial_block),
        in_hbm(precond_diag),
        in_hbm(partners.T),
        in_hbm(stored_at.reshape(-1, 128)),
        in_hbm(ham_blocks),
    )
    far_own, near0, z1, z_even, diag0, rows = barrier((far_own, near0, z1, z_even, diag0, rows))
    some, z_even, diag0 = barrier((jnp.concatenate([z1, z_even]), z_even, diag0))
    near1, far1 = near_of(some), far_of(some)
    z_odd = swap(z_even, "chan", 4)
    diag_odd = jnp.concatenate([swap(diag0, "chan", 4 * z) for z in range(3, nz, 2)])
    diag_odd, z_odd, far1, near1, diag0 = barrier(
        (diag_odd, z_odd, far1, near1, diag0)
    )
    early = in_cores(
        jnp.concatenate([own, z1, z_even, near0, far_own, diag0, near1, z_odd, diag_odd, far1])
    )
    near_odd, diag1 = near_of(z_odd), swap(diag0, "chan", 4)
    far2 = far_of(jnp.concatenate([z_odd, near1[1:]]))
    table = pl.pallas_call(
        functools.partial(assemble_kernel, nz, share),
        in_specs=[whole] * n_rad,
        out_specs=whole,
        out_shape=pltpu.VMEM((n_chan * ch, k, splines), BF16),
        compiler_params=pltpu.CompilerParams(vmem_limit_bytes=VMEM_LIMIT),
        name="assemble",
    )(*[in_vmem(flat(x)) for x in early])
    diag1, near_odd, far2, table, rows = barrier((diag1, near_odd, far2, table, rows))
    last = [in_vmem(flat(x)) for x in in_cores(jnp.concatenate([near_odd, far2, diag1]))]

    az, sums, _ = pl.pallas_call(
        functools.partial(apply_kernel, nz, share),
        in_specs=[smem] + [whole] * (6 + n_rad),
        out_specs=[whole, whole, whole],
        out_shape=[
            pltpu.VMEM((2 * k, lanes), BF16),
            jax.ShapeDtypeStruct((k, 8 * k), F32),
            pltpu.VMEM(table.shape, BF16),
        ],
        input_output_aliases={2: 2},
        compiler_params=pltpu.CompilerParams(vmem_limit_bytes=VMEM_LIMIT),
        name="apply",
    )(rows, in_vmem(ham), in_vmem(table), in_vmem(zhm), in_vmem(zl), in_vmem(dc), gram_t, *last)

    sums = gather_sums(sums)
    new_block, ritz = pl.pallas_call(
        functools.partial(finish_kernel, total),
        out_shape=[
            jax.ShapeDtypeStruct((ch, k, r), F32),
            jax.ShapeDtypeStruct((1, k), F32),
        ],
        compiler_params=pltpu.CompilerParams(vmem_limit_bytes=VMEM_LIMIT),
        name="finish",
    )(sums, in_vmem(az), in_vmem(zhm))
    return (new_block, ritz.reshape(k))


def solution(mesh):
    return jax.shard_map(
        body,
        mesh=mesh,
        in_specs=(
            P("chan", None, "rad"),
            P("chan", None, "rad", None),
            P("chan", None),
            P(),
            P("chan", "rad"),
        ),
        out_specs=(P("chan", None, "rad"), P()),
        check_vma=False,
    )
```

```python
import functools

import jax
import jax.numpy as jnp
from jax import lax
from jax.experimental import pallas as pl
from jax.experimental.pallas import tpu as pltpu
from jax.sharding import PartitionSpec as P

SCALE = 2.0 ** -8
F32 = jnp.float32
BF16 = jnp.bfloat16
NT = (((1,), (1,)), ((), ()))
TN = (((0,), (0,)), ((), ()))
NN = (((1,), (0,)), ((), ()))
VMEM_LIMIT = 4 * 1024 * 1024


def swap(x, axis, distance):
    n = lax.axis_size(axis)
    return lax.ppermute(x, axis, [(i, i ^ distance) for i in range(n)])


def plane_swap(x, order):
    n_chan, n_rad = lax.axis_size("chan"), lax.axis_size("rad")
    pairs = []
    for c in range(n_chan):
        for r in range(n_rad):
            pairs.append((c * n_rad + r, (c ^ order[r % 2]) * n_rad + r))
    return lax.ppermute(x, ("chan", "rad"), pairs)


def early_pieces(nz):
    some, odd = [1] + list(range(2, nz, 2)), list(range(3, nz, 2))
    order = [(0, 0)] + [(z, 0) for z in some] + [(0, 1), (0, 2), (0, 3)] + [(z, 1) for z in some]
    return order + [(z, 0) for z in odd] + [(z, 2) for z in some]


def late_pieces(nz):
    even, odd = list(range(2, nz, 2)), list(range(3, nz, 2))
    return [(z, 1) for z in odd] + [(z, 2) for z in odd] + [(z, 3) for z in even + [1] + odd]


def table_piece(z, part, nz):
    some, odd = nz // 2, nz // 2 - 1
    is_odd = (z & 1 == 1) & (z > 1)
    i = jnp.where(is_odd, (z - 3) >> 1, jnp.where(z == 1, 0, z >> 1))
    base = 2 * some + odd + 4

    def pick(own, of_some, of_odd):
        return jnp.where(z == 0, own, jnp.where(is_odd, of_odd + i, of_some + i))

    here = pick(0, 1, 2 * some + 4)
    near = pick(some + 1, some + 4, base + some)
    far = pick(some + 2, base, base + some + odd)
    last = base + 2 * some + 2 * odd
    both = jnp.where(z == 1, last - 1, pick(some + 3, last - some - 1, last))
    return jnp.where(part == 0, here, jnp.where(part == 1, near, jnp.where(part == 2, far, both)))


def merge(refs, table_ref, order, start, share):
    n_rad = len(refs)
    r = 128 // n_rad
    lane = lax.broadcasted_iota(jnp.int32, (1, 128), 1)
    masks = [jnp.where(lane // r == c, 1.0, 0.0).astype(BF16) for c in range(n_rad)]

    for me in range(n_rad):

        @pl.when(lax.axis_index("rad") == me)
        def _():
            def rows(n, carry):
                for i, (z, part) in enumerate(order):
                    other = order.index((z, (0, 2, 1, 3)[part]))
                    tiles = [refs[me ^ c][((other if (me ^ c) % 2 else i) * share) + n] for c in range(n_rad)]
                    for g in range(n_rad):
                        row = None
                        for c, x in enumerate(tiles):
                            if c != g:
                                x = pltpu.roll(x, (c - g) % n_rad * r, 1)
                            row = x * masks[c] if row is None else row + x * masks[c]
                        table_ref[((start + i) * n_rad + g) * share + n] = row
                return carry

            lax.fori_loop(0, share, rows, 0)


def in_vmem(x):
    return pltpu.with_memory_space_constraint(x, pltpu.VMEM)


def in_hbm(x):
    return pltpu.with_memory_space_constraint(x, pltpu.HBM)


def split3(x):
    hi = x.astype(BF16)
    rest = x - hi.astype(F32)
    mid = rest.astype(BF16)
    return hi, mid, (rest - mid.astype(F32)).astype(BF16)


def dot32(x, y, dims=NN):
    return lax.dot_general(x, y, dims, precision=lax.Precision.HIGHEST, preferred_element_type=F32)


def block_sum(g, rows, cols):
    g = sum(g[i : i + rows] for i in range(0, g.shape[0], rows))
    return sum(g[:, i : i + cols] for i in range(0, g.shape[1], cols))


def prepare_kernel(
    n_chan, n_rad, t_hbm, d_hbm, partners_hbm, stored_hbm, ham_hbm,
    rows_ref, ham_ref, zhm_ref, zl_ref, dc_ref, gram_ref, t_ref, d_ref, partners_ref, stored_ref, sems,
):
    moves = (
        (t_hbm, t_ref), (d_hbm, d_ref), (partners_hbm, partners_ref), (stored_hbm, stored_ref), (ham_hbm, ham_ref)
    )
    copies = [pltpu.make_async_copy(x, y, sems.at[i]) for i, (x, y) in enumerate(moves)]
    for copy in copies:
        copy.start()
    for copy in copies[:4]:
        copy.wait()
    ch, k, r = t_ref.shape
    group = 128 // r
    for i in range(ch // group):
        lanes = pl.ds(i * 128, 128)
        t = jnp.concatenate([t_ref[i * group + g] for g in range(group)], axis=1)
        d = jnp.concatenate([d_ref[pl.ds(i * group + g, 1), :] for g in range(group)], axis=1)
        dc_ref[:, lanes] = d
        hi, mid, lo = split3(jnp.concatenate([t / d, t], axis=0))
        zhm_ref[:, lanes] = jnp.concatenate([hi, mid], axis=0)
        zl_ref[:, lanes] = lo
    z = jnp.concatenate([zhm_ref[...], zl_ref[...]], axis=0)
    g = block_sum(lax.dot_general(z, z, NT, preferred_element_type=F32), 2 * k, 2 * k)
    gram_ref[...] = jnp.concatenate([g[k:, :], g[:k, :k]], axis=1)

    share, nz = ch // n_rad, n_chan // 4
    q = stored_ref[...]
    owner, local = lax.div(q, ch), lax.rem(q, ch)
    apart = (owner ^ lax.axis_index("chan")) & 3
    turned = ((apart & 1) << 1) | (apart >> 1)
    part = jnp.where((lax.axis_index("rad") & 1) == 1, turned, apart)
    piece = table_piece((owner ^ lax.axis_index("chan")) >> 2, part, nz)
    place = (piece * ch + local).astype(F32)
    lane = lax.broadcasted_iota(jnp.int32, (ch, 128), 1)
    columns = []
    partners = partners_ref[...].astype(F32).T.astype(jnp.int32)
    for j in range(partners.shape[1]):
        wanted = jnp.broadcast_to(partners[:, j : j + 1], (ch, 128)) - lane
        found = jnp.zeros((ch, 128), F32)
        for c in range(place.shape[0]):
            found = found + jnp.where(wanted == 128 * c, place[c : c + 1], 0.0)
        columns.append(jnp.sum(found, axis=1, keepdims=True))
    rows_ref[...] = jnp.concatenate(columns, axis=1).astype(jnp.int32)
    copies[4].wait()


def assemble_kernel(nz, share, *refs):
    merge(refs[:-1], refs[-1], early_pieces(nz), 0, share)


def apply_kernel(nz, share, rows_ref, ham_ref, _, zhm_ref, zl_ref, dc_ref, gt_ref, *rest):
    last, (az_ref, sums_ref, table_ref, a0_ref) = rest[:-4], rest[-4:]
    merge(last, table_ref, late_pieces(nz), len(early_pieces(nz)), share)
    ch, ncoup, r, splines = ham_ref.shape
    k = zl_ref.shape[0] // 2
    group = 256 // r

    def work(g, carry):
        left, right = [], []
        for i in range(group):
            p = g * group + i
            left.append(
                jnp.concatenate([table_ref[rows_ref[p, j]] for j in range(ncoup)], axis=1)
            )
            right.append(jnp.concatenate([ham_ref[p, j] for j in range(ncoup)], axis=1))
        product = lax.dot_general(
            jnp.concatenate(left, axis=0),
            jnp.concatenate(right, axis=0),
            NT,
            preferred_element_type=F32,
        )
        own = [product[i * k : (i + 1) * k, i * r : (i + 1) * r] for i in range(group)]
        a0_ref[:, pl.ds(pl.multiple_of(g * 256, 256), 256)] = jnp.concatenate(own, axis=1) * SCALE
        return carry

    lax.fori_loop(0, ch // group, work, 0, unroll=min(8, ch // group))

    lanes = ch * r
    block = min(lanes, 1024)

    def gram_block(i, gram):
        at = pl.ds(pl.multiple_of(i * block, block), block)
        a0 = a0_ref[:, at]
        a1_terms = split3(a0 / dc_ref[:, at])
        az_ref[:, at] = jnp.concatenate(a1_terms[:2], axis=0)
        right = jnp.concatenate(a1_terms + split3(a0), axis=0)
        left = jnp.concatenate([zhm_ref[:, at], zl_ref[:, at], right[: 3 * k]], axis=0)
        return gram + lax.dot_general(left, right, NT, preferred_element_type=F32)

    gram = lax.fori_loop(
        0, lanes // block, gram_block, jnp.zeros((9 * k, 6 * k), F32), unroll=min(2, lanes // block)
    )
    ta1 = block_sum(gram[: 6 * k, : 3 * k], 2 * k, k)
    ta0 = block_sum(gram[: 6 * k, 3 * k :], 2 * k, k)
    aa = block_sum(gram[6 * k :, : 3 * k], k, k)
    gt = gt_ref[...]
    parts = [ta1[k:], gt[:, : 2 * k], ta0[k:], ta1[:k], gt[:, 2 * k :], aa, jnp.zeros((k, k), F32)]
    sums_ref[...] = jnp.concatenate(parts, axis=1)


def spread(x, i):
    return jnp.broadcast_to(x[:, i : i + 1], (x.shape[0], 128))


def finish_kernel(total, sums_ref, az_ref, zhm_ref, out_ref, ritz_ref):
    ch, k, r = out_ref.shape
    s = jnp.sum(sums_ref[...], axis=0)
    row = lax.broadcasted_iota(jnp.int32, (k, 128), 0)
    cols = [spread(s, 2 * k + i) for i in range(k)]
    x = s
    for i in range(k):
        scale = 1.0 / cols[i][i : i + 1]
        pivot = x[i : i + 1] * scale
        x = jnp.where(row == i, pivot, x - cols[i] * pivot)
        for j in range(i + 1, k):
            part = cols[j][i : i + 1] * scale
            cols[j] = jnp.where(row == i, part, cols[j] - cols[i] * part)
    coef = x[:, 3 * k : 4 * k]
    eye = lax.broadcasted_iota(jnp.int32, (k, k), 0) == lax.broadcasted_iota(jnp.int32, (k, k), 1)
    ritz_ref[...] = jnp.sum(jnp.where(eye, coef, 0.0), axis=0, keepdims=True) * (1.0 / SCALE)
    s1, b1 = s[:, :k], s[:, k : 2 * k]
    s2, b2, aa = s[:, 4 * k : 5 * k], s[:, 5 * k : 6 * k], s[:, 6 * k : 7 * k]
    known = jnp.concatenate([x[:, :k], s1, s2], axis=0)
    known = known - dot32(jnp.concatenate([x[:, k : 2 * k], b1, b2], axis=0), coef)
    mix, corr, weighted = known[:k], known[k : 2 * k], known[2 * k :]
    gram = aa - dot32(
        jnp.concatenate([s2, coef, corr], axis=0), jnp.concatenate([coef, weighted, mix], axis=0), TN
    )
    cols = [spread(gram, i) for i in range(k)]
    pad = jnp.zeros((k, 128 - 3 * k), F32)
    x = jnp.concatenate([eye.astype(F32), -coef.T, -mix.T, pad], axis=1)
    for i in range(k):
        pivot = cols[i][i : i + 1]
        scale = 1.0 / pivot
        below = jnp.where(row > i, cols[i] * scale, 0.0)
        pivot_row = x[i : i + 1]
        x = jnp.where(row == i, pivot_row * (lax.rsqrt(pivot) * (total ** 0.5)), x - below * pivot_row)
        for j in range(i + 1, k):
            cols[j] = cols[j] - below * cols[j][i : i + 1]
    hi, mid, _ = split3(x[:, : 3 * k])
    lhs = jnp.concatenate([hi, hi, mid], axis=1)
    block = min(ch * r, 1024)

    def result(b, carry):
        at = pl.ds(pl.multiple_of(b * block, block), block)
        x_hi = jnp.concatenate([az_ref[:k, at], zhm_ref[: 2 * k, at]], axis=0)
        x_mid = jnp.concatenate([az_ref[k:, at], zhm_ref[2 * k :, at]], axis=0)
        new = lax.dot_general(
            lhs, jnp.concatenate([x_hi, x_mid, x_hi], axis=0), NN, preferred_element_type=F32
        )
        for i in range(block // r):
            out_ref[b * (block // r) + i] = new[:, i * r : (i + 1) * r]
        return carry

    lax.fori_loop(0, ch * r // block, result, 0)


def gather_sums(x):
    n_chan, n_rad = lax.axis_size("chan"), lax.axis_size("rad")
    step = 1
    while step < n_rad:
        x = x + swap(x, "rad", step)
        step *= 2
    every = jnp.broadcast_to(x, (n_chan,) + x.shape)
    return lax.all_to_all(every, "chan", split_axis=0, concat_axis=0, tiled=True)


def body(trial_block, ham_blocks, partners, stored_at, precond_diag):
    n_chan, n_rad = lax.axis_size("chan"), lax.axis_size("rad")
    ch, k, r = trial_block.shape
    ncoup, splines = ham_blocks.shape[1], ham_blocks.shape[3]
    lanes = ch * r
    total = float(n_chan * n_rad * lanes)
    share, nz = ch // n_rad, n_chan // 4

    barrier = lax.optimization_barrier
    smem = pl.BlockSpec(memory_space=pltpu.SMEM)
    any_ = pl.BlockSpec(memory_space=pl.ANY)
    whole = pl.BlockSpec(memory_space=pltpu.VMEM)

    def near_of(x):
        return plane_swap(x, (1, 2))

    def far_of(x):
        return plane_swap(x, (2, 1))

    def flat(x):
        return x.reshape((-1,) + x.shape[2:])

    def in_cores(x):
        return [x] + [swap(x, "rad", c) for c in range(1, n_rad)]

    own = jnp.concatenate(jnp.split(trial_block.astype(BF16), n_rad), axis=2)[None]
    near0, far_own, diag0 = near_of(own), far_of(own), swap(own, "chan", 3)
    z1 = swap(own, "chan", 4)
    z_even = jnp.concatenate([swap(own, "chan", 4 * z) for z in range(2, nz, 2)])
    rows, ham, zhm, zl, dc, gram_t = pl.pallas_call(
        functools.partial(prepare_kernel, n_chan, n_rad),
        in_specs=[any_] * 5,
        out_specs=[whole] * 6,
        out_shape=[
            jax.ShapeDtypeStruct((ch, ncoup), jnp.int32),
            pltpu.VMEM(ham_blocks.shape, BF16),
            pltpu.VMEM((4 * k, lanes), BF16),
            pltpu.VMEM((2 * k, lanes), BF16),
            pltpu.VMEM((1, lanes), F32),
            pltpu.VMEM((k, 3 * k), F32),
        ],
        scratch_shapes=[
            pltpu.VMEM(trial_block.shape, F32),
            pltpu.VMEM(precond_diag.shape, F32),
            pltpu.VMEM((ncoup, ch), jnp.int32),
            pltpu.VMEM((stored_at.shape[0] // 128, 128), jnp.int32),
            pltpu.SemaphoreType.DMA((5,)),
        ],
        compiler_params=pltpu.CompilerParams(vmem_limit_bytes=VMEM_LIMIT),
        name="prepare",
    )(
        in_hbm(trial_block),
        in_hbm(precond_diag),
        in_hbm(partners.T),
        in_hbm(stored_at.reshape(-1, 128)),
        in_hbm(ham_blocks),
    )
    far_own, near0, z1, z_even, diag0, rows = barrier((far_own, near0, z1, z_even, diag0, rows))
    some, z_even, diag0 = barrier((jnp.concatenate([z1, z_even]), z_even, diag0))
    near1, far1 = near_of(some), far_of(some)
    z_odd = swap(z_even, "chan", 4)
    z_odd, far1, near1, diag0 = barrier((z_odd, far1, near1, diag0))
    early = in_cores(
        jnp.concatenate([own, z1, z_even, near0, far_own, diag0, near1, z_odd, far1])
    )
    diag_odd = jnp.concatenate([swap(diag0, "chan", 4 * z) for z in range(3, nz, 2)])
    near_odd, diag1 = near_of(z_odd), swap(diag0, "chan", 4)
    far2 = far_of(jnp.concatenate([z_odd, near1[1:]]))
    table = pl.pallas_call(
        functools.partial(assemble_kernel, nz, share),
        in_specs=[whole] * n_rad,
        out_specs=whole,
        out_shape=pltpu.VMEM((n_chan * ch, k, splines), BF16),
        compiler_params=pltpu.CompilerParams(vmem_limit_bytes=VMEM_LIMIT),
        name="assemble",
    )(*[in_vmem(flat(x)) for x in early])
    diag1, near_odd, diag_odd, far2, table = barrier((diag1, near_odd, diag_odd, far2, table))
    last = [in_vmem(flat(x)) for x in in_cores(jnp.concatenate([near_odd, far2, diag1, diag_odd]))]

    az, sums, _ = pl.pallas_call(
        functools.partial(apply_kernel, nz, share),
        in_specs=[smem] + [whole] * (6 + n_rad),
        out_specs=[whole, whole, whole],
        out_shape=[
            pltpu.VMEM((2 * k, lanes), BF16),
            jax.ShapeDtypeStruct((k, 8 * k), F32),
            pltpu.VMEM(table.shape, BF16),
        ],
        input_output_aliases={2: 2},
        scratch_shapes=[pltpu.VMEM((k, lanes), F32)],
        compiler_params=pltpu.CompilerParams(vmem_limit_bytes=VMEM_LIMIT),
        name="apply",
    )(rows, in_vmem(ham), in_vmem(table), in_vmem(zhm), in_vmem(zl), in_vmem(dc), gram_t, *last)

    sums = gather_sums(sums)
    new_block, ritz = pl.pallas_call(
        functools.partial(finish_kernel, total),
        out_shape=[
            jax.ShapeDtypeStruct((ch, k, r), F32),
            jax.ShapeDtypeStruct((1, k), F32),
        ],
        compiler_params=pltpu.CompilerParams(vmem_limit_bytes=VMEM_LIMIT),
        name="finish",
    )(sums, in_vmem(az), in_vmem(zhm))
    return (new_block, ritz.reshape(k))


def solution(mesh):
    return jax.shard_map(
        body,
        mesh=mesh,
        in_specs=(
            P("chan", None, "rad"),
            P("chan", None, "rad", None),
            P("chan", None),
            P(),
            P("chan", "rad"),
        ),
        out_specs=(P("chan", None, "rad"), P()),
        check_vma=False,
    )
```

```python
import functools

import jax
import jax.numpy as jnp
from jax import lax
from jax.experimental import pallas as pl
from jax.experimental.pallas import tpu as pltpu
from jax.sharding import PartitionSpec as P

SCALE = 2.0 ** -8
F32 = jnp.float32
BF16 = jnp.bfloat16
NT = (((1,), (1,)), ((), ()))
TN = (((0,), (0,)), ((), ()))
NN = (((1,), (0,)), ((), ()))
VMEM_LIMIT = 4 * 1024 * 1024


def swap(x, axis, distance):
    n = lax.axis_size(axis)
    return lax.ppermute(x, axis, [(i, i ^ distance) for i in range(n)])


def plane_swap(x, order):
    n_chan, n_rad = lax.axis_size("chan"), lax.axis_size("rad")
    pairs = []
    for c in range(n_chan):
        for r in range(n_rad):
            pairs.append((c * n_rad + r, (c ^ order[r % 2]) * n_rad + r))
    return lax.ppermute(x, ("chan", "rad"), pairs)


def table_piece(z, part, nz):
    some, odd = nz // 2, nz // 2 - 1
    is_odd = (z & 1 == 1) & (z > 1)
    i = jnp.where(is_odd, (z - 3) >> 1, jnp.where(z == 1, 0, z >> 1))
    base = 2 * some + odd + 4

    def pick(own, of_some, of_odd):
        return jnp.where(z == 0, own, jnp.where(is_odd, of_odd + i, of_some + i))

    here = pick(0, 1, 2 * some + 4)
    near = pick(some + 1, some + 4, base + some)
    far = pick(some + 2, base, base + some + odd)
    both = pick(some + 3, base + some + 2 * odd, base + 2 * some + 2 * odd)
    return jnp.where(part == 0, here, jnp.where(part == 1, near, jnp.where(part == 2, far, both)))


def in_vmem(x):
    return pltpu.with_memory_space_constraint(x, pltpu.VMEM)


def in_hbm(x):
    return pltpu.with_memory_space_constraint(x, pltpu.HBM)


def split3(x):
    hi = x.astype(BF16)
    rest = x - hi.astype(F32)
    mid = rest.astype(BF16)
    return hi, mid, (rest - mid.astype(F32)).astype(BF16)


def dot32(x, y, dims=NN):
    return lax.dot_general(x, y, dims, precision=lax.Precision.HIGHEST, preferred_element_type=F32)


def block_sum(g, rows, cols):
    g = sum(g[i : i + rows] for i in range(0, g.shape[0], rows))
    return sum(g[:, i : i + cols] for i in range(0, g.shape[1], cols))


def prepare_kernel(
    n_chan, n_rad, t_hbm, d_hbm, partners_hbm, stored_hbm, ham_hbm,
    rows_ref, ham_ref, zhm_ref, zl_ref, dc_ref, gram_ref, t_ref, d_ref, partners_ref, stored_ref, sems,
):
    moves = (
        (t_hbm, t_ref), (d_hbm, d_ref), (partners_hbm, partners_ref), (stored_hbm, stored_ref), (ham_hbm, ham_ref)
    )
    copies = [pltpu.make_async_copy(x, y, sems.at[i]) for i, (x, y) in enumerate(moves)]
    for copy in copies:
        copy.start()
    for copy in copies[:4]:
        copy.wait()
    ch, k, r = t_ref.shape
    group = 128 // r
    for i in range(ch // group):
        lanes = pl.ds(i * 128, 128)
        t = jnp.concatenate([t_ref[i * group + g] for g in range(group)], axis=1)
        d = jnp.concatenate([d_ref[pl.ds(i * group + g, 1), :] for g in range(group)], axis=1)
        dc_ref[:, lanes] = d
        hi, mid, lo = split3(jnp.concatenate([t / d, t], axis=0))
        zhm_ref[:, lanes] = jnp.concatenate([hi, mid], axis=0)
        zl_ref[:, lanes] = lo
    z = jnp.concatenate([zhm_ref[...], zl_ref[...]], axis=0)
    g = block_sum(lax.dot_general(z, z, NT, preferred_element_type=F32), 2 * k, 2 * k)
    gram_ref[...] = jnp.concatenate([g[k:, :], g[:k, :k]], axis=1)

    share, nz = ch // n_rad, n_chan // 4
    q = stored_ref[...]
    owner, local = lax.div(q, ch), lax.rem(q, ch)
    core = lax.div(local, share)
    apart = (owner ^ lax.axis_index("chan")) & 3
    part = jnp.where((core & 1) == 1, ((apart & 1) << 1) | (apart >> 1), apart)
    piece = table_piece((owner ^ lax.axis_index("chan")) >> 2, part, nz)
    place = (core ^ lax.axis_index("rad")) * 4 * nz + piece
    place = (place * share + lax.rem(local, share)).astype(F32)
    lane = lax.broadcasted_iota(jnp.int32, (ch, 128), 1)
    columns = []
    partners = partners_ref[...].astype(F32).T.astype(jnp.int32)
    for j in range(partners.shape[1]):
        wanted = jnp.broadcast_to(partners[:, j : j + 1], (ch, 128)) - lane
        found = jnp.zeros((ch, 128), F32)
        for c in range(place.shape[0]):
            found = found + jnp.where(wanted == 128 * c, place[c : c + 1], 0.0)
        columns.append(jnp.sum(found, axis=1, keepdims=True))
    rows_ref[...] = jnp.concatenate(columns, axis=1).T.astype(jnp.int32)
    copies[4].wait()


def assemble_kernel(*refs):
    pieces, table_ref, sems = refs[:-2], refs[-2], refs[-1]
    each = table_ref.shape[0] // len(pieces)
    copies = []
    for i, piece in enumerate(pieces):
        place = table_ref.at[pl.ds(i * each, piece.shape[0])]
        copies.append(pltpu.make_async_copy(piece, place, sems.at[i]))
        copies[-1].start()
    for copy in copies:
        copy.wait()


def apply_kernel(rows_ref, ham_ref, _, zhm_ref, zl_ref, dc_ref, gt_ref, *rest):
    last, (az_ref, sums_ref, table_ref, a0_ref) = rest[:-4], rest[-4:]
    for c, piece in enumerate(last):
        start = (c + 1) * (table_ref.shape[0] // len(last)) - piece.shape[0]
        step = min(32, piece.shape[0])

        def put(i, carry, piece=piece, start=start, step=step):
            table_ref[pl.ds(start + i * step, step)] = piece[pl.ds(i * step, step)]
            return carry

        lax.fori_loop(0, piece.shape[0] // step, put, 0)
    ch, ncoup, r, splines = ham_ref.shape
    k = zl_ref.shape[0] // 2
    group = 256 // r

    def work(g, carry):
        left, right = [], []
        for i in range(group):
            p = g * group + i
            left.append(
                jnp.concatenate([table_ref[rows_ref[j, p]] for j in range(ncoup)], axis=1)
            )
            right.append(jnp.concatenate([ham_ref[p, j] for j in range(ncoup)], axis=1))
        product = lax.dot_general(
            jnp.concatenate(left, axis=0),
            jnp.concatenate(right, axis=0),
            NT,
            preferred_element_type=F32,
        )
        own = [product[i * k : (i + 1) * k, i * r : (i + 1) * r] for i in range(group)]
        a0_ref[:, pl.ds(pl.multiple_of(g * 256, 256), 256)] = jnp.concatenate(own, axis=1) * SCALE
        return carry

    lax.fori_loop(0, ch // group, work, 0, unroll=min(4, ch // group))

    lanes = ch * r
    block = min(lanes, 1024)

    def gram_block(i, gram):
        at = pl.ds(pl.multiple_of(i * block, block), block)
        a0 = a0_ref[:, at]
        a1_terms = split3(a0 / dc_ref[:, at])
        az_ref[:, at] = jnp.concatenate(a1_terms[:2], axis=0)
        right = jnp.concatenate(a1_terms + split3(a0), axis=0)
        left = jnp.concatenate([zhm_ref[:, at], zl_ref[:, at], right[: 3 * k]], axis=0)
        return gram + lax.dot_general(left, right, NT, preferred_element_type=F32)

    gram = lax.fori_loop(0, lanes // block, gram_block, jnp.zeros((9 * k, 6 * k), F32))
    ta1 = block_sum(gram[: 6 * k, : 3 * k], 2 * k, k)
    ta0 = block_sum(gram[: 6 * k, 3 * k :], 2 * k, k)
    aa = block_sum(gram[6 * k :, : 3 * k], k, k)
    gt = gt_ref[...]
    parts = [ta1[k:], gt[:, : 2 * k], ta0[k:], ta1[:k], gt[:, 2 * k :], aa, jnp.zeros((k, k), F32)]
    sums_ref[...] = jnp.concatenate(parts, axis=1)


def spread(x, i):
    return jnp.broadcast_to(x[:, i : i + 1], (x.shape[0], 128))


def finish_kernel(total, sums_ref, az_ref, zhm_ref, out_ref, ritz_ref):
    ch, k, r = out_ref.shape
    s = jnp.sum(sums_ref[...], axis=0)
    row = lax.broadcasted_iota(jnp.int32, (k, 128), 0)
    cols = [spread(s, 2 * k + i) for i in range(k)]
    x = s
    for i in range(k):
        scale = 1.0 / cols[i][i : i + 1]
        pivot = x[i : i + 1] * scale
        x = jnp.where(row == i, pivot, x - cols[i] * pivot)
        for j in range(i + 1, k):
            part = cols[j][i : i + 1] * scale
            cols[j] = jnp.where(row == i, part, cols[j] - cols[i] * part)
    coef = x[:, 3 * k : 4 * k]
    eye = lax.broadcasted_iota(jnp.int32, (k, k), 0) == lax.broadcasted_iota(jnp.int32, (k, k), 1)
    ritz_ref[...] = jnp.sum(jnp.where(eye, coef, 0.0), axis=0, keepdims=True) * (1.0 / SCALE)
    s1, b1 = s[:, :k], s[:, k : 2 * k]
    s2, b2, aa = s[:, 4 * k : 5 * k], s[:, 5 * k : 6 * k], s[:, 6 * k : 7 * k]
    known = jnp.concatenate([x[:, :k], s1, s2], axis=0)
    known = known - dot32(jnp.concatenate([x[:, k : 2 * k], b1, b2], axis=0), coef)
    mix, corr, weighted = known[:k], known[k : 2 * k], known[2 * k :]
    gram = aa - dot32(
        jnp.concatenate([s2, coef, corr], axis=0), jnp.concatenate([coef, weighted, mix], axis=0), TN
    )
    cols = [spread(gram, i) for i in range(k)]
    pad = jnp.zeros((k, 128 - 3 * k), F32)
    x = jnp.concatenate([eye.astype(F32), -coef.T, -mix.T, pad], axis=1)
    for i in range(k):
        pivot = cols[i][i : i + 1]
        scale = 1.0 / pivot
        below = jnp.where(row > i, cols[i] * scale, 0.0)
        pivot_row = x[i : i + 1]
        x = jnp.where(row == i, pivot_row * (lax.rsqrt(pivot) * (total ** 0.5)), x - below * pivot_row)
        for j in range(i + 1, k):
            cols[j] = cols[j] - below * cols[j][i : i + 1]
    hi, mid, _ = split3(x[:, : 3 * k])
    lhs = jnp.concatenate([hi, hi, mid], axis=1)
    block = min(ch * r, 1024)

    def result(b, carry):
        at = pl.ds(pl.multiple_of(b * block, block), block)
        x_hi = jnp.concatenate([az_ref[:k, at], zhm_ref[: 2 * k, at]], axis=0)
        x_mid = jnp.concatenate([az_ref[k:, at], zhm_ref[2 * k :, at]], axis=0)
        new = lax.dot_general(
            lhs, jnp.concatenate([x_hi, x_mid, x_hi], axis=0), NN, preferred_element_type=F32
        )
        for i in range(block // r):
            out_ref[b * (block // r) + i] = new[:, i * r : (i + 1) * r]
        return carry

    lax.fori_loop(0, ch * r // block, result, 0)


def gather_sums(x):
    n_chan, n_rad = lax.axis_size("chan"), lax.axis_size("rad")
    step = 1
    while step < n_rad:
        x = x + swap(x, "rad", step)
        step *= 2
    every = jnp.broadcast_to(x, (n_chan,) + x.shape)
    return lax.all_to_all(every, "chan", split_axis=0, concat_axis=0, tiled=True)


def own_share(trial_block):
    n_rad = lax.axis_size("rad")
    ch, k, r = trial_block.shape
    me = lax.axis_index("rad")
    rounded = trial_block.astype(BF16).reshape(n_rad, ch // n_rad, k, r)
    got = []
    for d in range(n_rad):
        part = lax.dynamic_index_in_dim(rounded, me ^ d, 0, keepdims=False)
        got.append(swap(part, "rad", d) if d else part)
    lanes = []
    for c in range(n_rad):
        x = got[0]
        for d in range(1, n_rad):
            x = jnp.where(me ^ d == c, got[d], x)
        lanes.append(x)
    return jnp.concatenate(lanes, axis=2)


def body(trial_block, ham_blocks, partners, stored_at, precond_diag):
    n_chan, n_rad = lax.axis_size("chan"), lax.axis_size("rad")
    ch, k, r = trial_block.shape
    ncoup, splines = ham_blocks.shape[1], ham_blocks.shape[3]
    lanes = ch * r
    total = float(n_chan * n_rad * lanes)
    share, nz = ch // n_rad, n_chan // 4

    barrier = lax.optimization_barrier
    smem = pl.BlockSpec(memory_space=pltpu.SMEM)
    any_ = pl.BlockSpec(memory_space=pl.ANY)
    whole = pl.BlockSpec(memory_space=pltpu.VMEM)

    def near_of(x):
        return plane_swap(x, (1, 2))

    def far_of(x):
        return plane_swap(x, (2, 1))

    def flat(x):
        return x.reshape((-1,) + x.shape[2:])

    def in_cores(x):
        return [x] + [swap(x, "rad", c) for c in range(1, n_rad)]

    own = own_share(trial_block)[None]
    near0, far_own, diag0 = near_of(own), far_of(own), swap(own, "chan", 3)
    z1 = swap(own, "chan", 4)
    z_even = jnp.concatenate([swap(own, "chan", 4 * z) for z in range(2, nz, 2)])
    rows, ham, zhm, zl, dc, gram_t = pl.pallas_call(
        functools.partial(prepare_kernel, n_chan, n_rad),
        in_specs=[any_] * 5,
        out_specs=[whole] * 6,
        out_shape=[
            jax.ShapeDtypeStruct((ncoup, ch), jnp.int32),
            pltpu.VMEM(ham_blocks.shape, BF16),
            pltpu.VMEM((4 * k, lanes), BF16),
            pltpu.VMEM((2 * k, lanes), BF16),
            pltpu.VMEM((1, lanes), F32),
            pltpu.VMEM((k, 3 * k), F32),
        ],
        scratch_shapes=[
            pltpu.VMEM(trial_block.shape, F32),
            pltpu.VMEM(precond_diag.shape, F32),
            pltpu.VMEM((ncoup, ch), jnp.int32),
            pltpu.VMEM((stored_at.shape[0] // 128, 128), jnp.int32),
            pltpu.SemaphoreType.DMA((5,)),
        ],
        compiler_params=pltpu.CompilerParams(vmem_limit_bytes=VMEM_LIMIT),
        name="prepare",
    )(
        in_hbm(trial_block),
        in_hbm(precond_diag),
        in_hbm(partners.T),
        in_hbm(stored_at.reshape(-1, 128)),
        in_hbm(ham_blocks),
    )
    far_own, near0, z1, z_even, diag0, rows = barrier((far_own, near0, z1, z_even, diag0, rows))
    some, z_even, diag0 = barrier((jnp.concatenate([z1, z_even]), z_even, diag0))
    near1, far1 = near_of(some), far_of(some)
    z_odd = swap(z_even, "chan", 4)
    z_odd, far1, near1, diag0 = barrier((z_odd, far1, near1, diag0))
    early = in_cores(
        jnp.concatenate([own, z1, z_even, near0, far_own, diag0, near1, z_odd, far1])
    )
    near_odd = near_of(z_odd)
    diag_odd = jnp.concatenate([swap(diag0, "chan", 4 * z) for z in range(3, nz, 2)])
    far2 = far_of(jnp.concatenate([z_odd, near1]))
    table = pl.pallas_call(
        assemble_kernel,
        in_specs=[any_] * n_rad,
        out_specs=whole,
        out_shape=pltpu.VMEM((n_chan * ch, k, splines), BF16),
        scratch_shapes=[pltpu.SemaphoreType.DMA((n_rad,))],
        compiler_params=pltpu.CompilerParams(vmem_limit_bytes=VMEM_LIMIT),
        name="assemble",
    )(*[flat(x) for x in early])
    near_odd, diag_odd, far2, table = barrier((near_odd, diag_odd, far2, table))
    last = [in_vmem(flat(x)) for x in in_cores(jnp.concatenate([near_odd, far2, diag_odd]))]

    az, sums, _ = pl.pallas_call(
        apply_kernel,
        in_specs=[smem] + [whole] * (6 + n_rad),
        out_specs=[whole, whole, whole],
        out_shape=[
            pltpu.VMEM((2 * k, lanes), BF16),
            jax.ShapeDtypeStruct((k, 8 * k), F32),
            pltpu.VMEM(table.shape, BF16),
        ],
        input_output_aliases={2: 2},
        scratch_shapes=[pltpu.VMEM((k, lanes), F32)],
        compiler_params=pltpu.CompilerParams(vmem_limit_bytes=VMEM_LIMIT),
        name="apply",
    )(rows, in_vmem(ham), in_vmem(table), in_vmem(zhm), in_vmem(zl), in_vmem(dc), gram_t, *last)

    sums = gather_sums(sums)
    new_block, ritz = pl.pallas_call(
        functools.partial(finish_kernel, total),
        out_shape=[
            jax.ShapeDtypeStruct((ch, k, r), F32),
            jax.ShapeDtypeStruct((1, k), F32),
        ],
        compiler_params=pltpu.CompilerParams(vmem_limit_bytes=VMEM_LIMIT),
        name="finish",
    )(sums, in_vmem(az), in_vmem(zhm))
    return (new_block, ritz.reshape(k))


def solution(mesh):
    return jax.shard_map(
        body,
        mesh=mesh,
        in_specs=(
            P("chan", None, "rad"),
            P("chan", None, "rad", None),
            P("chan", None),
            P(),
            P("chan", "rad"),
        ),
        out_specs=(P("chan", None, "rad"), P()),
        check_vma=False,
    )
```

```python
import functools

import jax
import jax.numpy as jnp
from jax import lax
from jax.experimental import pallas as pl
from jax.experimental.pallas import tpu as pltpu
from jax.sharding import PartitionSpec as P

SCALE = 2.0 ** -8
F32 = jnp.float32
BF16 = jnp.bfloat16
NT = (((1,), (1,)), ((), ()))
TN = (((0,), (0,)), ((), ()))
NN = (((1,), (0,)), ((), ()))
VMEM_LIMIT = 4 * 1024 * 1024


def swap(x, axis, distance):
    n = lax.axis_size(axis)
    return lax.ppermute(x, axis, [(i, i ^ distance) for i in range(n)])


def plane_swap(x, order):
    n_chan, n_rad = lax.axis_size("chan"), lax.axis_size("rad")
    pairs = []
    for c in range(n_chan):
        for r in range(n_rad):
            pairs.append((c * n_rad + r, (c ^ order[r % 2]) * n_rad + r))
    return lax.ppermute(x, ("chan", "rad"), pairs)


def table_piece(z, part, nz):
    some, odd = nz // 2, nz // 2 - 1
    is_odd = (z & 1 == 1) & (z > 1)
    i = jnp.where(is_odd, (z - 3) >> 1, jnp.where(z == 1, 0, z >> 1))
    base = 2 * some + odd + 4

    def pick(own, of_some, of_odd):
        return jnp.where(z == 0, own, jnp.where(is_odd, of_odd + i, of_some + i))

    here = pick(0, 1, 2 * some + 4)
    near = pick(some + 1, some + 4, base + some)
    far = pick(some + 2, base, base + some + odd)
    both = pick(some + 3, base + some + 2 * odd, base + 2 * some + 2 * odd)
    return jnp.where(part == 0, here, jnp.where(part == 1, near, jnp.where(part == 2, far, both)))


def in_vmem(x):
    return pltpu.with_memory_space_constraint(x, pltpu.VMEM)


def in_hbm(x):
    return pltpu.with_memory_space_constraint(x, pltpu.HBM)


def split3(x):
    hi = x.astype(BF16)
    rest = x - hi.astype(F32)
    mid = rest.astype(BF16)
    return hi, mid, (rest - mid.astype(F32)).astype(BF16)


def dot32(x, y, dims=NN):
    return lax.dot_general(x, y, dims, precision=lax.Precision.HIGHEST, preferred_element_type=F32)


def block_sum(g, rows, cols):
    g = sum(g[i : i + rows] for i in range(0, g.shape[0], rows))
    return sum(g[:, i : i + cols] for i in range(0, g.shape[1], cols))


def prepare_kernel(
    n_chan, n_rad, t_hbm, d_hbm, partners_hbm, stored_hbm, ham_hbm,
    rows_ref, ham_ref, zhm_ref, zl_ref, dc_ref, gram_ref, t_ref, d_ref, partners_ref, stored_ref, sems,
):
    moves = (
        (t_hbm, t_ref), (d_hbm, d_ref), (partners_hbm, partners_ref), (stored_hbm, stored_ref), (ham_hbm, ham_ref)
    )
    copies = [pltpu.make_async_copy(x, y, sems.at[i]) for i, (x, y) in enumerate(moves)]
    for copy in copies:
        copy.start()
    for copy in copies[:4]:
        copy.wait()
    ch, k, r = t_ref.shape
    group = 128 // r
    for i in range(ch // group):
        lanes = pl.ds(i * 128, 128)
        t = jnp.concatenate([t_ref[i * group + g] for g in range(group)], axis=1)
        d = jnp.concatenate([d_ref[pl.ds(i * group + g, 1), :] for g in range(group)], axis=1)
        dc_ref[:, lanes] = d
        hi, mid, lo = split3(jnp.concatenate([t / d, t], axis=0))
        zhm_ref[:, lanes] = jnp.concatenate([hi, mid], axis=0)
        zl_ref[:, lanes] = lo
    z = jnp.concatenate([zhm_ref[...], zl_ref[...]], axis=0)
    g = block_sum(lax.dot_general(z, z, NT, preferred_element_type=F32), 2 * k, 2 * k)
    gram_ref[...] = jnp.concatenate([g[k:, :], g[:k, :k]], axis=1)

    share, nz = ch // n_rad, n_chan // 4
    q = stored_ref[...]
    owner, local = lax.div(q, ch), lax.rem(q, ch)
    core = lax.div(local, share)
    apart = (owner ^ lax.axis_index("chan")) & 3
    part = jnp.where((core & 1) == 1, ((apart & 1) << 1) | (apart >> 1), apart)
    piece = table_piece((owner ^ lax.axis_index("chan")) >> 2, part, nz)
    place = (core ^ lax.axis_index("rad")) * 4 * nz + piece
    place = (place * share + lax.rem(local, share)).astype(F32)
    lane = lax.broadcasted_iota(jnp.int32, (ch, 128), 1)
    columns = []
    partners = partners_ref[...].astype(F32).T.astype(jnp.int32)
    for j in range(partners.shape[1]):
        wanted = jnp.broadcast_to(partners[:, j : j + 1], (ch, 128)) - lane
        found = jnp.zeros((ch, 128), F32)
        for c in range(place.shape[0]):
            found = found + jnp.where(wanted == 128 * c, place[c : c + 1], 0.0)
        columns.append(jnp.sum(found, axis=1, keepdims=True))
    rows_ref[...] = jnp.concatenate(columns, axis=1).T.astype(jnp.int32)
    copies[4].wait()


def assemble_kernel(*refs):
    pieces, table_ref, sems = refs[:-2], refs[-2], refs[-1]
    each = table_ref.shape[0] // len(pieces)
    copies = []
    for i, piece in enumerate(pieces):
        place = table_ref.at[pl.ds(i * each, piece.shape[0])]
        copies.append(pltpu.make_async_copy(piece, place, sems.at[i]))
        copies[-1].start()
    for copy in copies:
        copy.wait()


def apply_kernel(rows_ref, ham_ref, _, zhm_ref, zl_ref, dc_ref, gt_ref, *rest):
    last, (az_ref, sums_ref, table_ref, a0_ref) = rest[:-4], rest[-4:]
    for c, piece in enumerate(last):
        start = (c + 1) * (table_ref.shape[0] // len(last)) - piece.shape[0]
        step = min(32, piece.shape[0])

        def put(i, carry, piece=piece, start=start, step=step):
            table_ref[pl.ds(start + i * step, step)] = piece[pl.ds(i * step, step)]
            return carry

        lax.fori_loop(0, piece.shape[0] // step, put, 0)
    ch, ncoup, r, splines = ham_ref.shape
    k = zl_ref.shape[0] // 2
    group = 256 // r

    def work(g, carry):
        left, right = [], []
        for i in range(group):
            p = g * group + i
            left.append(
                jnp.concatenate([table_ref[rows_ref[j, p]] for j in range(ncoup)], axis=1)
            )
            right.append(jnp.concatenate([ham_ref[p, j] for j in range(ncoup)], axis=1))
        product = lax.dot_general(
            jnp.concatenate(left, axis=0),
            jnp.concatenate(right, axis=0),
            NT,
            preferred_element_type=F32,
        )
        own = [product[i * k : (i + 1) * k, i * r : (i + 1) * r] for i in range(group)]
        a0_ref[:, pl.ds(pl.multiple_of(g * 256, 256), 256)] = jnp.concatenate(own, axis=1) * SCALE
        return carry

    lax.fori_loop(0, ch // group, work, 0, unroll=min(4, ch // group))

    lanes = ch * r
    block = min(lanes, 1024)

    def gram_block(i, gram):
        at = pl.ds(pl.multiple_of(i * block, block), block)
        a0 = a0_ref[:, at]
        a1_terms = split3(a0 / dc_ref[:, at])
        az_ref[:, at] = jnp.concatenate(a1_terms[:2], axis=0)
        right = jnp.concatenate(a1_terms + split3(a0), axis=0)
        left = jnp.concatenate([zhm_ref[:, at], zl_ref[:, at], right[: 3 * k]], axis=0)
        return gram + lax.dot_general(left, right, NT, preferred_element_type=F32)

    gram = lax.fori_loop(0, lanes // block, gram_block, jnp.zeros((9 * k, 6 * k), F32))
    ta1 = block_sum(gram[: 6 * k, : 3 * k], 2 * k, k)
    ta0 = block_sum(gram[: 6 * k, 3 * k :], 2 * k, k)
    aa = block_sum(gram[6 * k :, : 3 * k], k, k)
    gt = gt_ref[...]
    parts = [ta1[k:], gt[:, : 2 * k], ta0[k:], ta1[:k], gt[:, 2 * k :], aa, jnp.zeros((k, k), F32)]
    sums_ref[...] = jnp.concatenate(parts, axis=1)


def spread(x, i):
    return jnp.broadcast_to(x[:, i : i + 1], (x.shape[0], 128))


def reciprocal(x):
    y = pl.reciprocal(x, approx=True)
    y = y * (2.0 - x * y)
    return y * (2.0 - x * y)


def finish_kernel(total, sums_ref, az_ref, zhm_ref, out_ref, ritz_ref):
    ch, k, r = out_ref.shape
    s = jnp.sum(sums_ref[...], axis=0)
    row = lax.broadcasted_iota(jnp.int32, (k, 128), 0)
    cols = [spread(s, 2 * k + i) for i in range(k)]
    x = s
    for i in range(k):
        scale = reciprocal(cols[i][i : i + 1])
        pivot = x[i : i + 1] * scale
        x = jnp.where(row == i, pivot, x - cols[i] * pivot)
        for j in range(i + 1, k):
            part = cols[j][i : i + 1] * scale
            cols[j] = jnp.where(row == i, part, cols[j] - cols[i] * part)
    coef = x[:, 3 * k : 4 * k]
    eye = lax.broadcasted_iota(jnp.int32, (k, k), 0) == lax.broadcasted_iota(jnp.int32, (k, k), 1)
    ritz_ref[...] = jnp.sum(jnp.where(eye, coef, 0.0), axis=0, keepdims=True) * (1.0 / SCALE)
    s1, b1 = s[:, :k], s[:, k : 2 * k]
    s2, b2, aa = s[:, 4 * k : 5 * k], s[:, 5 * k : 6 * k], s[:, 6 * k : 7 * k]
    known = jnp.concatenate([x[:, :k], s1, s2], axis=0)
    known = known - dot32(jnp.concatenate([x[:, k : 2 * k], b1, b2], axis=0), coef)
    mix, corr, weighted = known[:k], known[k : 2 * k], known[2 * k :]
    gram = aa - dot32(
        jnp.concatenate([s2, coef, corr], axis=0), jnp.concatenate([coef, weighted, mix], axis=0), TN
    )
    cols = [spread(gram, i) for i in range(k)]
    pad = jnp.zeros((k, 128 - 3 * k), F32)
    x = jnp.concatenate([eye.astype(F32), -coef.T, -mix.T, pad], axis=1)
    for i in range(k):
        pivot = cols[i][i : i + 1]
        scale = reciprocal(pivot)
        below = jnp.where(row > i, cols[i] * scale, 0.0)
        pivot_row = x[i : i + 1]
        x = jnp.where(row == i, pivot_row * (lax.rsqrt(pivot) * (total ** 0.5)), x - below * pivot_row)
        for j in range(i + 1, k):
            cols[j] = cols[j] - below * cols[j][i : i + 1]
    hi, mid, _ = split3(x[:, : 3 * k])
    lhs = jnp.concatenate([hi, hi, mid], axis=1)
    block = min(ch * r, 1024)

    def result(b, carry):
        at = pl.ds(pl.multiple_of(b * block, block), block)
        x_hi = jnp.concatenate([az_ref[:k, at], zhm_ref[: 2 * k, at]], axis=0)
        x_mid = jnp.concatenate([az_ref[k:, at], zhm_ref[2 * k :, at]], axis=0)
        new = lax.dot_general(
            lhs, jnp.concatenate([x_hi, x_mid, x_hi], axis=0), NN, preferred_element_type=F32
        )
        for i in range(block // r):
            out_ref[b * (block // r) + i] = new[:, i * r : (i + 1) * r]
        return carry

    lax.fori_loop(0, ch * r // block, result, 0)


def gather_sums(x):
    n_chan, n_rad = lax.axis_size("chan"), lax.axis_size("rad")
    step = 1
    while step < n_rad:
        x = x + swap(x, "rad", step)
        step *= 2
    every = jnp.broadcast_to(x, (n_chan,) + x.shape)
    return lax.all_to_all(every, "chan", split_axis=0, concat_axis=0, tiled=True)


def own_share(trial_block):
    n_rad = lax.axis_size("rad")
    ch, k, r = trial_block.shape
    me = lax.axis_index("rad")
    rounded = trial_block.astype(BF16).reshape(n_rad, ch // n_rad, k, r)
    got = []
    for d in range(n_rad):
        part = lax.dynamic_index_in_dim(rounded, me ^ d, 0, keepdims=False)
        got.append(swap(part, "rad", d) if d else part)
    lanes = []
    for c in range(n_rad):
        x = got[0]
        for d in range(1, n_rad):
            x = jnp.where(me ^ d == c, got[d], x)
        lanes.append(x)
    return jnp.concatenate(lanes, axis=2)


def body(trial_block, ham_blocks, partners, stored_at, precond_diag):
    n_chan, n_rad = lax.axis_size("chan"), lax.axis_size("rad")
    ch, k, r = trial_block.shape
    ncoup, splines = ham_blocks.shape[1], ham_blocks.shape[3]
    lanes = ch * r
    total = float(n_chan * n_rad * lanes)
    share, nz = ch // n_rad, n_chan // 4

    barrier = lax.optimization_barrier
    smem = pl.BlockSpec(memory_space=pltpu.SMEM)
    any_ = pl.BlockSpec(memory_space=pl.ANY)
    whole = pl.BlockSpec(memory_space=pltpu.VMEM)

    def near_of(x):
        return plane_swap(x, (1, 2))

    def far_of(x):
        return plane_swap(x, (2, 1))

    def flat(x):
        return x.reshape((-1,) + x.shape[2:])

    def in_cores(x):
        return [x] + [swap(x, "rad", c) for c in range(1, n_rad)]

    own = own_share(trial_block)[None]
    near0, far_own, diag0 = near_of(own), far_of(own), swap(own, "chan", 3)
    z1 = swap(own, "chan", 4)
    z_even = jnp.concatenate([swap(own, "chan", 4 * z) for z in range(2, nz, 2)])
    far_own, near0, z1, z_even, diag0 = barrier((far_own, near0, z1, z_even, diag0))
    some, z_even, diag0 = barrier((jnp.concatenate([z1, z_even]), z_even, diag0))
    near1, far1 = near_of(some), far_of(some)
    z_odd = swap(z_even, "chan", 4)
    inputs = (trial_block, precond_diag, partners, stored_at, ham_blocks)
    z_odd, far1, near1, diag0, inputs = barrier((z_odd, far1, near1, diag0, inputs))
    trial_block, precond_diag, partners, stored_at, ham_blocks = inputs
    early = in_cores(
        jnp.concatenate([own, z1, z_even, near0, far_own, diag0, near1, z_odd, far1])
    )
    near_odd = near_of(z_odd)
    diag_odd = jnp.concatenate([swap(diag0, "chan", 4 * z) for z in range(3, nz, 2)])
    far2 = far_of(jnp.concatenate([z_odd, near1]))
    rows, ham, zhm, zl, dc, gram_t = pl.pallas_call(
        functools.partial(prepare_kernel, n_chan, n_rad),
        in_specs=[any_] * 5,
        out_specs=[whole] * 6,
        out_shape=[
            jax.ShapeDtypeStruct((ncoup, ch), jnp.int32),
            pltpu.VMEM(ham_blocks.shape, BF16),
            pltpu.VMEM((4 * k, lanes), BF16),
            pltpu.VMEM((2 * k, lanes), BF16),
            pltpu.VMEM((1, lanes), F32),
            pltpu.VMEM((k, 3 * k), F32),
        ],
        scratch_shapes=[
            pltpu.VMEM(trial_block.shape, F32),
            pltpu.VMEM(precond_diag.shape, F32),
            pltpu.VMEM((ncoup, ch), jnp.int32),
            pltpu.VMEM((stored_at.shape[0] // 128, 128), jnp.int32),
            pltpu.SemaphoreType.DMA((5,)),
        ],
        compiler_params=pltpu.CompilerParams(vmem_limit_bytes=VMEM_LIMIT),
        name="prepare",
    )(
        in_hbm(trial_block),
        in_hbm(precond_diag),
        in_hbm(partners.T),
        in_hbm(stored_at.reshape(-1, 128)),
        in_hbm(ham_blocks),
    )
    table = pl.pallas_call(
        assemble_kernel,
        in_specs=[any_] * n_rad,
        out_specs=whole,
        out_shape=pltpu.VMEM((n_chan * ch, k, splines), BF16),
        scratch_shapes=[pltpu.SemaphoreType.DMA((n_rad,))],
        compiler_params=pltpu.CompilerParams(vmem_limit_bytes=VMEM_LIMIT),
        name="assemble",
    )(*[flat(x) for x in early])
    near_odd, diag_odd, far2, table, rows = barrier((near_odd, diag_odd, far2, table, rows))
    last = [in_vmem(flat(x)) for x in in_cores(jnp.concatenate([near_odd, far2, diag_odd]))]

    az, sums, _ = pl.pallas_call(
        apply_kernel,
        in_specs=[smem] + [whole] * (6 + n_rad),
        out_specs=[whole, whole, whole],
        out_shape=[
            pltpu.VMEM((2 * k, lanes), BF16),
            jax.ShapeDtypeStruct((k, 8 * k), F32),
            pltpu.VMEM(table.shape, BF16),
        ],
        input_output_aliases={2: 2},
        scratch_shapes=[pltpu.VMEM((k, lanes), F32)],
        compiler_params=pltpu.CompilerParams(vmem_limit_bytes=VMEM_LIMIT),
        name="apply",
    )(rows, in_vmem(ham), in_vmem(table), in_vmem(zhm), in_vmem(zl), in_vmem(dc), gram_t, *last)

    sums = gather_sums(sums)
    new_block, ritz = pl.pallas_call(
        functools.partial(finish_kernel, total),
        out_shape=[
            jax.ShapeDtypeStruct((ch, k, r), F32),
            jax.ShapeDtypeStruct((1, k), F32),
        ],
        compiler_params=pltpu.CompilerParams(vmem_limit_bytes=VMEM_LIMIT),
        name="finish",
    )(sums, in_vmem(az), in_vmem(zhm))
    return (new_block, ritz.reshape(k))


def solution(mesh):
    return jax.shard_map(
        body,
        mesh=mesh,
        in_specs=(
            P("chan", None, "rad"),
            P("chan", None, "rad", None),
            P("chan", None),
            P(),
            P("chan", "rad"),
        ),
        out_specs=(P("chan", None, "rad"), P()),
        check_vma=False,
    )
```

```python
import functools

import jax
import jax.numpy as jnp
from jax import lax
from jax.experimental import pallas as pl
from jax.experimental.pallas import tpu as pltpu
from jax.sharding import PartitionSpec as P

SCALE = 2.0 ** -8
F32 = jnp.float32
BF16 = jnp.bfloat16
NT = (((1,), (1,)), ((), ()))
TN = (((0,), (0,)), ((), ()))
NN = (((1,), (0,)), ((), ()))
VMEM_LIMIT = 4 * 1024 * 1024


def swap(x, axis, distance):
    n = lax.axis_size(axis)
    return lax.ppermute(x, axis, [(i, i ^ distance) for i in range(n)])


def plane_swap(x, order):
    n_chan, n_rad = lax.axis_size("chan"), lax.axis_size("rad")
    pairs = []
    for c in range(n_chan):
        for r in range(n_rad):
            pairs.append((c * n_rad + r, (c ^ order[r % 2]) * n_rad + r))
    return lax.ppermute(x, ("chan", "rad"), pairs)


def table_piece(z, part, nz):
    some, odd = nz // 2, nz // 2 - 1
    is_odd = (z & 1 == 1) & (z > 1)
    i = jnp.where(is_odd, (z - 3) >> 1, jnp.where(z == 1, 0, z >> 1))
    base = 2 * some + odd + 4

    def pick(own, of_some, of_odd):
        return jnp.where(z == 0, own, jnp.where(is_odd, of_odd + i, of_some + i))

    here = pick(0, 1, 2 * some + 4)
    near = pick(some + 1, some + 4, base + some)
    far = pick(some + 2, base, base + some + odd)
    both = pick(some + 3, base + some + 2 * odd, base + 2 * some + 2 * odd)
    return jnp.where(part == 0, here, jnp.where(part == 1, near, jnp.where(part == 2, far, both)))


def early_pieces(nz):
    some, odd = [1] + list(range(2, nz, 2)), list(range(3, nz, 2))
    order = [(0, 0)] + [(z, 0) for z in some] + [(0, 1), (0, 2), (0, 3)] + [(z, 1) for z in some]
    return order + [(z, 0) for z in odd] + [(z, 2) for z in some]


def late_pieces(nz):
    some, odd = [1] + list(range(2, nz, 2)), list(range(3, nz, 2))
    return [(z, 1) for z in odd] + [(z, 2) for z in odd] + [(z, 3) for z in some + odd]


def merge(refs, table_ref, order, start, share):
    n_rad = len(refs)
    r = 128 // n_rad
    me = lax.axis_index("rad")

    def rows(n, carry):
        for i, (z, part) in enumerate(order):
            other = order.index((z, (0, 2, 1, 3)[part]))
            tiles = [ref[(other if s % 2 else i) * share + n] for s, ref in enumerate(refs)]
            by_core = []
            for c in range(n_rad):
                x = tiles[0]
                for s in range(1, n_rad):
                    x = jnp.where((me ^ s) == c, tiles[s], x)
                by_core.append(x)
            for g in range(n_rad):
                row = jnp.concatenate([x[:, g * r : (g + 1) * r] for x in by_core], axis=1)
                table_ref[((start + i) * n_rad + g) * share + n] = row
        return carry

    lax.fori_loop(0, share, rows, 0, unroll=min(8, share))


def in_vmem(x):
    return pltpu.with_memory_space_constraint(x, pltpu.VMEM)


def in_hbm(x):
    return pltpu.with_memory_space_constraint(x, pltpu.HBM)


def split3(x):
    hi = x.astype(BF16)
    rest = x - hi.astype(F32)
    mid = rest.astype(BF16)
    return hi, mid, (rest - mid.astype(F32)).astype(BF16)


def dot32(x, y, dims=NN):
    return lax.dot_general(x, y, dims, precision=lax.Precision.HIGHEST, preferred_element_type=F32)


def block_sum(g, rows, cols):
    g = sum(g[i : i + rows] for i in range(0, g.shape[0], rows))
    return sum(g[:, i : i + cols] for i in range(0, g.shape[1], cols))


def prepare_kernel(
    n_chan, n_rad, t_hbm, d_hbm, partners_hbm, stored_hbm, ham_hbm,
    rows_ref, ham_ref, zhm_ref, zl_ref, dc_ref, gram_ref, t_ref, d_ref, partners_ref, stored_ref, sems,
):
    moves = (
        (t_hbm, t_ref), (d_hbm, d_ref), (partners_hbm, partners_ref), (stored_hbm, stored_ref), (ham_hbm, ham_ref)
    )
    copies = [pltpu.make_async_copy(x, y, sems.at[i]) for i, (x, y) in enumerate(moves)]
    for copy in copies:
        copy.start()
    for copy in copies[:4]:
        copy.wait()
    ch, k, r = t_ref.shape
    group = 128 // r
    for i in range(ch // group):
        lanes = pl.ds(i * 128, 128)
        t = jnp.concatenate([t_ref[i * group + g] for g in range(group)], axis=1)
        d = jnp.concatenate([d_ref[pl.ds(i * group + g, 1), :] for g in range(group)], axis=1)
        dc_ref[:, lanes] = d
        hi, mid, lo = split3(jnp.concatenate([t / d, t], axis=0))
        zhm_ref[:, lanes] = jnp.concatenate([hi, mid], axis=0)
        zl_ref[:, lanes] = lo
    z = jnp.concatenate([zhm_ref[...], zl_ref[...]], axis=0)
    g = block_sum(lax.dot_general(z, z, NT, preferred_element_type=F32), 2 * k, 2 * k)
    gram_ref[...] = jnp.concatenate([g[k:, :], g[:k, :k]], axis=1)

    share, nz = ch // n_rad, n_chan // 4
    q = stored_ref[...]
    owner, local = lax.div(q, ch), lax.rem(q, ch)
    apart = (owner ^ lax.axis_index("chan")) & 3
    turned = ((apart & 1) << 1) | (apart >> 1)
    part = jnp.where((lax.axis_index("rad") & 1) == 1, turned, apart)
    piece = table_piece((owner ^ lax.axis_index("chan")) >> 2, part, nz)
    place = (piece * ch + local).astype(F32)
    lane = lax.broadcasted_iota(jnp.int32, (ch, 128), 1)
    columns = []
    partners = partners_ref[...].astype(F32).T.astype(jnp.int32)
    for j in range(partners.shape[1]):
        wanted = jnp.broadcast_to(partners[:, j : j + 1], (ch, 128)) - lane
        found = jnp.zeros((ch, 128), F32)
        for c in range(place.shape[0]):
            found = found + jnp.where(wanted == 128 * c, place[c : c + 1], 0.0)
        columns.append(jnp.sum(found, axis=1, keepdims=True))
    rows_ref[...] = jnp.concatenate(columns, axis=1).T.astype(jnp.int32)
    copies[4].wait()


def assemble_kernel(nz, share, *refs):
    merge(refs[:-1], refs[-1], early_pieces(nz), 0, share)


def apply_kernel(nz, share, rows_ref, ham_ref, _, zhm_ref, zl_ref, dc_ref, gt_ref, *rest):
    last, (az_ref, sums_ref, table_ref, a0_ref) = rest[:-4], rest[-4:]
    merge(last, table_ref, late_pieces(nz), len(early_pieces(nz)), share)
    ch, ncoup, r, splines = ham_ref.shape
    k = zl_ref.shape[0] // 2
    group = 256 // r

    def work(g, carry):
        left, right = [], []
        for i in range(group):
            p = g * group + i
            left.append(
                jnp.concatenate([table_ref[rows_ref[j, p]] for j in range(ncoup)], axis=1)
            )
            right.append(jnp.concatenate([ham_ref[p, j] for j in range(ncoup)], axis=1))
        product = lax.dot_general(
            jnp.concatenate(left, axis=0),
            jnp.concatenate(right, axis=0),
            NT,
            preferred_element_type=F32,
        )
        own = [product[i * k : (i + 1) * k, i * r : (i + 1) * r] for i in range(group)]
        a0_ref[:, pl.ds(pl.multiple_of(g * 256, 256), 256)] = jnp.concatenate(own, axis=1) * SCALE
        return carry

    lax.fori_loop(0, ch // group, work, 0, unroll=min(4, ch // group))

    lanes = ch * r
    block = min(lanes, 1024)

    def gram_block(i, gram):
        at = pl.ds(pl.multiple_of(i * block, block), block)
        a0 = a0_ref[:, at]
        a1_terms = split3(a0 / dc_ref[:, at])
        az_ref[:, at] = jnp.concatenate(a1_terms[:2], axis=0)
        right = jnp.concatenate(a1_terms + split3(a0), axis=0)
        left = jnp.concatenate([zhm_ref[:, at], zl_ref[:, at], right[: 3 * k]], axis=0)
        return gram + lax.dot_general(left, right, NT, preferred_element_type=F32)

    gram = lax.fori_loop(0, lanes // block, gram_block, jnp.zeros((9 * k, 6 * k), F32))
    ta1 = block_sum(gram[: 6 * k, : 3 * k], 2 * k, k)
    ta0 = block_sum(gram[: 6 * k, 3 * k :], 2 * k, k)
    aa = block_sum(gram[6 * k :, : 3 * k], k, k)
    gt = gt_ref[...]
    parts = [ta1[k:], gt[:, : 2 * k], ta0[k:], ta1[:k], gt[:, 2 * k :], aa, jnp.zeros((k, k), F32)]
    sums_ref[...] = jnp.concatenate(parts, axis=1)


def spread(x, i):
    return jnp.broadcast_to(x[:, i : i + 1], (x.shape[0], 128))


def finish_kernel(total, sums_ref, az_ref, zhm_ref, out_ref, ritz_ref):
    ch, k, r = out_ref.shape
    s = jnp.sum(sums_ref[...], axis=0)
    row = lax.broadcasted_iota(jnp.int32, (k, 128), 0)
    cols = [spread(s, 2 * k + i) for i in range(k)]
    x = s
    for i in range(k):
        scale = 1.0 / cols[i][i : i + 1]
        pivot = x[i : i + 1] * scale
        x = jnp.where(row == i, pivot, x - cols[i] * pivot)
        for j in range(i + 1, k):
            part = cols[j][i : i + 1] * scale
            cols[j] = jnp.where(row == i, part, cols[j] - cols[i] * part)
    coef = x[:, 3 * k : 4 * k]
    eye = lax.broadcasted_iota(jnp.int32, (k, k), 0) == lax.broadcasted_iota(jnp.int32, (k, k), 1)
    ritz_ref[...] = jnp.sum(jnp.where(eye, coef, 0.0), axis=0, keepdims=True) * (1.0 / SCALE)
    s1, b1 = s[:, :k], s[:, k : 2 * k]
    s2, b2, aa = s[:, 4 * k : 5 * k], s[:, 5 * k : 6 * k], s[:, 6 * k : 7 * k]
    known = jnp.concatenate([x[:, :k], s1, s2], axis=0)
    known = known - dot32(jnp.concatenate([x[:, k : 2 * k], b1, b2], axis=0), coef)
    mix, corr, weighted = known[:k], known[k : 2 * k], known[2 * k :]
    gram = aa - dot32(
        jnp.concatenate([s2, coef, corr], axis=0), jnp.concatenate([coef, weighted, mix], axis=0), TN
    )
    cols = [spread(gram, i) for i in range(k)]
    pad = jnp.zeros((k, 128 - 3 * k), F32)
    x = jnp.concatenate([eye.astype(F32), -coef.T, -mix.T, pad], axis=1)
    for i in range(k):
        pivot = cols[i][i : i + 1]
        scale = 1.0 / pivot
        below = jnp.where(row > i, cols[i] * scale, 0.0)
        pivot_row = x[i : i + 1]
        x = jnp.where(row == i, pivot_row * (lax.rsqrt(pivot) * (total ** 0.5)), x - below * pivot_row)
        for j in range(i + 1, k):
            cols[j] = cols[j] - below * cols[j][i : i + 1]
    hi, mid, _ = split3(x[:, : 3 * k])
    lhs = jnp.concatenate([hi, hi, mid], axis=1)
    block = min(ch * r, 1024)

    def result(b, carry):
        at = pl.ds(pl.multiple_of(b * block, block), block)
        x_hi = jnp.concatenate([az_ref[:k, at], zhm_ref[: 2 * k, at]], axis=0)
        x_mid = jnp.concatenate([az_ref[k:, at], zhm_ref[2 * k :, at]], axis=0)
        new = lax.dot_general(
            lhs, jnp.concatenate([x_hi, x_mid, x_hi], axis=0), NN, preferred_element_type=F32
        )
        for i in range(block // r):
            out_ref[b * (block // r) + i] = new[:, i * r : (i + 1) * r]
        return carry

    lax.fori_loop(0, ch * r // block, result, 0)


def gather_sums(x):
    n_chan, n_rad = lax.axis_size("chan"), lax.axis_size("rad")
    step = 1
    while step < n_rad:
        x = x + swap(x, "rad", step)
        step *= 2
    every = jnp.broadcast_to(x, (n_chan,) + x.shape)
    return lax.all_to_all(every, "chan", split_axis=0, concat_axis=0, tiled=True)


def body(trial_block, ham_blocks, partners, stored_at, precond_diag):
    n_chan, n_rad = lax.axis_size("chan"), lax.axis_size("rad")
    ch, k, r = trial_block.shape
    ncoup, splines = ham_blocks.shape[1], ham_blocks.shape[3]
    lanes = ch * r
    total = float(n_chan * n_rad * lanes)
    share, nz = ch // n_rad, n_chan // 4

    barrier = lax.optimization_barrier
    smem = pl.BlockSpec(memory_space=pltpu.SMEM)
    any_ = pl.BlockSpec(memory_space=pl.ANY)
    whole = pl.BlockSpec(memory_space=pltpu.VMEM)

    def near_of(x):
        return plane_swap(x, (1, 2))

    def far_of(x):
        return plane_swap(x, (2, 1))

    def flat(x):
        return x.reshape((-1,) + x.shape[2:])

    def in_cores(x):
        return [x] + [swap(x, "rad", c) for c in range(1, n_rad)]

    own = jnp.concatenate(jnp.split(trial_block.astype(BF16), n_rad), axis=2)[None]
    near0, far_own, diag0 = near_of(own), far_of(own), swap(own, "chan", 3)
    z1 = swap(own, "chan", 4)
    z_even = jnp.concatenate([swap(own, "chan", 4 * z) for z in range(2, nz, 2)])
    rows, ham, zhm, zl, dc, gram_t = pl.pallas_call(
        functools.partial(prepare_kernel, n_chan, n_rad),
        in_specs=[any_] * 5,
        out_specs=[whole] * 6,
        out_shape=[
            jax.ShapeDtypeStruct((ncoup, ch), jnp.int32),
            pltpu.VMEM(ham_blocks.shape, BF16),
            pltpu.VMEM((4 * k, lanes), BF16),
            pltpu.VMEM((2 * k, lanes), BF16),
            pltpu.VMEM((1, lanes), F32),
            pltpu.VMEM((k, 3 * k), F32),
        ],
        scratch_shapes=[
            pltpu.VMEM(trial_block.shape, F32),
            pltpu.VMEM(precond_diag.shape, F32),
            pltpu.VMEM((ncoup, ch), jnp.int32),
            pltpu.VMEM((stored_at.shape[0] // 128, 128), jnp.int32),
            pltpu.SemaphoreType.DMA((5,)),
        ],
        compiler_params=pltpu.CompilerParams(vmem_limit_bytes=VMEM_LIMIT),
        name="prepare",
    )(
        in_hbm(trial_block),
        in_hbm(precond_diag),
        in_hbm(partners.T),
        in_hbm(stored_at.reshape(-1, 128)),
        in_hbm(ham_blocks),
    )
    far_own, near0, z1, z_even, diag0, rows = barrier((far_own, near0, z1, z_even, diag0, rows))
    some, z_even, diag0 = barrier((jnp.concatenate([z1, z_even]), z_even, diag0))
    near1, far1 = near_of(some), far_of(some)
    z_odd = swap(z_even, "chan", 4)
    z_odd, far1, near1, diag0 = barrier((z_odd, far1, near1, diag0))
    early = in_cores(
        jnp.concatenate([own, z1, z_even, near0, far_own, diag0, near1, z_odd, far1])
    )
    near_odd = near_of(z_odd)
    diag_odd = jnp.concatenate([swap(diag0, "chan", 4 * z) for z in range(3, nz, 2)])
    far2 = far_of(jnp.concatenate([z_odd, near1]))
    table = pl.pallas_call(
        functools.partial(assemble_kernel, nz, share),
        in_specs=[whole] * n_rad,
        out_specs=whole,
        out_shape=pltpu.VMEM((n_chan * ch, k, splines), BF16),
        compiler_params=pltpu.CompilerParams(vmem_limit_bytes=VMEM_LIMIT),
        name="assemble",
    )(*[in_vmem(flat(x)) for x in early])
    near_odd, diag_odd, far2, table = barrier((near_odd, diag_odd, far2, table))
    last = [in_vmem(flat(x)) for x in in_cores(jnp.concatenate([near_odd, far2, diag_odd]))]

    az, sums, _ = pl.pallas_call(
        functools.partial(apply_kernel, nz, share),
        in_specs=[smem] + [whole] * (6 + n_rad),
        out_specs=[whole, whole, whole],
        out_shape=[
            pltpu.VMEM((2 * k, lanes), BF16),
            jax.ShapeDtypeStruct((k, 8 * k), F32),
            pltpu.VMEM(table.shape, BF16),
        ],
        input_output_aliases={2: 2},
        scratch_shapes=[pltpu.VMEM((k, lanes), F32)],
        compiler_params=pltpu.CompilerParams(vmem_limit_bytes=VMEM_LIMIT),
        name="apply",
    )(rows, in_vmem(ham), in_vmem(table), in_vmem(zhm), in_vmem(zl), in_vmem(dc), gram_t, *last)

    sums = gather_sums(sums)
    new_block, ritz = pl.pallas_call(
        functools.partial(finish_kernel, total),
        out_shape=[
            jax.ShapeDtypeStruct((ch, k, r), F32),
            jax.ShapeDtypeStruct((1, k), F32),
        ],
        compiler_params=pltpu.CompilerParams(vmem_limit_bytes=VMEM_LIMIT),
        name="finish",
    )(sums, in_vmem(az), in_vmem(zhm))
    return (new_block, ritz.reshape(k))


def solution(mesh):
    return jax.shard_map(
        body,
        mesh=mesh,
        in_specs=(
            P("chan", None, "rad"),
            P("chan", None, "rad", None),
            P("chan", None),
            P(),
            P("chan", "rad"),
        ),
        out_specs=(P("chan", None, "rad"), P()),
        check_vma=False,
    )
```

```python
import functools

import jax
import jax.numpy as jnp
from jax import lax
from jax.experimental import pallas as pl
from jax.experimental.pallas import tpu as pltpu
from jax.sharding import PartitionSpec as P

SCALE = 2.0 ** -8
F32 = jnp.float32
BF16 = jnp.bfloat16
NT = (((1,), (1,)), ((), ()))
TN = (((0,), (0,)), ((), ()))
NN = (((1,), (0,)), ((), ()))
VMEM_LIMIT = 4 * 1024 * 1024


def swap(x, axis, distance):
    n = lax.axis_size(axis)
    return lax.ppermute(x, axis, [(i, i ^ distance) for i in range(n)])


def plane_swap(x, order):
    n_chan, n_rad = lax.axis_size("chan"), lax.axis_size("rad")
    pairs = []
    for c in range(n_chan):
        for r in range(n_rad):
            pairs.append((c * n_rad + r, (c ^ order[r % 2]) * n_rad + r))
    return lax.ppermute(x, ("chan", "rad"), pairs)


def table_piece(z, part, nz):
    some, odd = nz // 2, nz // 2 - 1
    is_odd = (z & 1 == 1) & (z > 1)
    i = jnp.where(is_odd, (z - 3) >> 1, jnp.where(z == 1, 0, z >> 1))
    base = 2 * some + odd + 3
    late = base + some + 1

    def pick(own, of_some, of_odd):
        return jnp.where(z == 0, own, jnp.where(is_odd, of_odd + i, of_some + i))

    here = pick(0, 1, 2 * some + 3)
    near = pick(some + 1, some + 3, late)
    far = pick(some + 2, base, late + odd)
    both = pick(late - 1, late + 2 * odd, late + 2 * odd + some)
    return jnp.where(part == 0, here, jnp.where(part == 1, near, jnp.where(part == 2, far, both)))


def early_pieces(nz):
    some, odd = [1] + list(range(2, nz, 2)), list(range(3, nz, 2))
    order = [(0, 0)] + [(z, 0) for z in some] + [(0, 1), (0, 2)] + [(z, 1) for z in some]
    return order + [(z, 0) for z in odd] + [(z, 2) for z in some] + [(0, 3)]


def late_pieces(nz):
    some, odd = [1] + list(range(2, nz, 2)), list(range(3, nz, 2))
    return [(z, 1) for z in odd] + [(z, 2) for z in odd] + [(z, 3) for z in some + odd]


def merge(refs, table_ref, order, start, share):
    n_rad = len(refs)
    r = 128 // n_rad
    me = lax.axis_index("rad")

    def rows(n, carry):
        for i, (z, part) in enumerate(order):
            other = order.index((z, (0, 2, 1, 3)[part]))
            tiles = [ref[(other if s % 2 else i) * share + n] for s, ref in enumerate(refs)]
            by_core = []
            for c in range(n_rad):
                x = tiles[0]
                for s in range(1, n_rad):
                    x = jnp.where((me ^ s) == c, tiles[s], x)
                by_core.append(x)
            for g in range(n_rad):
                row = jnp.concatenate([x[:, g * r : (g + 1) * r] for x in by_core], axis=1)
                table_ref[((start + i) * n_rad + g) * share + n] = row
        return carry

    lax.fori_loop(0, share, rows, 0, unroll=min(8, share))


def in_vmem(x):
    return pltpu.with_memory_space_constraint(x, pltpu.VMEM)


def in_hbm(x):
    return pltpu.with_memory_space_constraint(x, pltpu.HBM)


def split3(x):
    hi = x.astype(BF16)
    rest = x - hi.astype(F32)
    mid = rest.astype(BF16)
    return hi, mid, (rest - mid.astype(F32)).astype(BF16)


def dot32(x, y, dims=NN):
    return lax.dot_general(x, y, dims, precision=lax.Precision.HIGHEST, preferred_element_type=F32)


def block_sum(g, rows, cols):
    g = sum(g[i : i + rows] for i in range(0, g.shape[0], rows))
    return sum(g[:, i : i + cols] for i in range(0, g.shape[1], cols))


def prepare_kernel(
    n_chan, n_rad, t_hbm, d_hbm, partners_hbm, stored_hbm, ham_hbm,
    rows_ref, ham_ref, zhm_ref, zl_ref, dc_ref, gram_ref, t_ref, d_ref, partners_ref, stored_ref, sems,
):
    moves = (
        (t_hbm, t_ref), (d_hbm, d_ref), (partners_hbm, partners_ref), (stored_hbm, stored_ref), (ham_hbm, ham_ref)
    )
    copies = [pltpu.make_async_copy(x, y, sems.at[i]) for i, (x, y) in enumerate(moves)]
    for copy in copies:
        copy.start()
    for copy in copies[:4]:
        copy.wait()
    ch, k, r = t_ref.shape
    group = 128 // r
    for i in range(ch // group):
        lanes = pl.ds(i * 128, 128)
        t = jnp.concatenate([t_ref[i * group + g] for g in range(group)], axis=1)
        d = jnp.concatenate([d_ref[pl.ds(i * group + g, 1), :] for g in range(group)], axis=1)
        dc_ref[:, lanes] = d
        hi, mid, lo = split3(jnp.concatenate([t / d, t], axis=0))
        zhm_ref[:, lanes] = jnp.concatenate([hi, mid], axis=0)
        zl_ref[:, lanes] = lo
    z = jnp.concatenate([zhm_ref[...], zl_ref[...]], axis=0)
    g = block_sum(lax.dot_general(z, z, NT, preferred_element_type=F32), 2 * k, 2 * k)
    gram_ref[...] = jnp.concatenate([g[k:, :], g[:k, :k]], axis=1)

    share, nz = ch // n_rad, n_chan // 4
    q = stored_ref[...]
    owner, local = lax.div(q, ch), lax.rem(q, ch)
    apart = (owner ^ lax.axis_index("chan")) & 3
    turned = ((apart & 1) << 1) | (apart >> 1)
    part = jnp.where((lax.axis_index("rad") & 1) == 1, turned, apart)
    piece = table_piece((owner ^ lax.axis_index("chan")) >> 2, part, nz)
    place = (piece * ch + local).astype(F32)
    lane = lax.broadcasted_iota(jnp.int32, (ch, 128), 1)
    columns = []
    partners = partners_ref[...].astype(F32).T.astype(jnp.int32)
    for j in range(partners.shape[1]):
        wanted = jnp.broadcast_to(partners[:, j : j + 1], (ch, 128)) - lane
        found = jnp.zeros((ch, 128), F32)
        for c in range(place.shape[0]):
            found = found + jnp.where(wanted == 128 * c, place[c : c + 1], 0.0)
        columns.append(jnp.sum(found, axis=1, keepdims=True))
    rows_ref[...] = jnp.concatenate(columns, axis=1).T.astype(jnp.int32)
    copies[4].wait()


def assemble_kernel(nz, share, *refs):
    merge(refs[:-1], refs[-1], early_pieces(nz), 0, share)


def apply_kernel(nz, share, rows_ref, ham_ref, _, zhm_ref, zl_ref, dc_ref, gt_ref, *rest):
    last, (az_ref, sums_ref, table_ref, a0_ref) = rest[:-4], rest[-4:]
    merge(last, table_ref, late_pieces(nz), len(early_pieces(nz)), share)
    ch, ncoup, r, splines = ham_ref.shape
    k = zl_ref.shape[0] // 2
    group = 256 // r

    def work(g, carry):
        left, right = [], []
        for i in range(group):
            p = g * group + i
            left.append(
                jnp.concatenate([table_ref[rows_ref[j, p]] for j in range(ncoup)], axis=1)
            )
            right.append(jnp.concatenate([ham_ref[p, j] for j in range(ncoup)], axis=1))
        product = lax.dot_general(
            jnp.concatenate(left, axis=0),
            jnp.concatenate(right, axis=0),
            NT,
            preferred_element_type=F32,
        )
        own = [product[i * k : (i + 1) * k, i * r : (i + 1) * r] for i in range(group)]
        a0_ref[:, pl.ds(pl.multiple_of(g * 256, 256), 256)] = jnp.concatenate(own, axis=1) * SCALE
        return carry

    lax.fori_loop(0, ch // group, work, 0, unroll=min(4, ch // group))

    lanes = ch * r
    block = min(lanes, 1024)

    def gram_block(i, gram):
        at = pl.ds(pl.multiple_of(i * block, block), block)
        a0 = a0_ref[:, at]
        a1_terms = split3(a0 / dc_ref[:, at])
        az_ref[:, at] = jnp.concatenate(a1_terms[:2], axis=0)
        right = jnp.concatenate(a1_terms + split3(a0), axis=0)
        left = jnp.concatenate([zhm_ref[:, at], zl_ref[:, at], right[: 3 * k]], axis=0)
        return gram + lax.dot_general(left, right, NT, preferred_element_type=F32)

    gram = lax.fori_loop(0, lanes // block, gram_block, jnp.zeros((9 * k, 6 * k), F32))
    ta1 = block_sum(gram[: 6 * k, : 3 * k], 2 * k, k)
    ta0 = block_sum(gram[: 6 * k, 3 * k :], 2 * k, k)
    aa = block_sum(gram[6 * k :, : 3 * k], k, k)
    gt = gt_ref[...]
    parts = [ta1[k:], gt[:, : 2 * k], ta0[k:], ta1[:k], gt[:, 2 * k :], aa, jnp.zeros((k, k), F32)]
    sums_ref[...] = jnp.concatenate(parts, axis=1)


def spread(x, i):
    return jnp.broadcast_to(x[:, i : i + 1], (x.shape[0], 128))


def finish_kernel(total, sums_ref, az_ref, zhm_ref, out_ref, ritz_ref):
    ch, k, r = out_ref.shape
    s = jnp.sum(sums_ref[...], axis=0)
    row = lax.broadcasted_iota(jnp.int32, (k, 128), 0)
    cols = [spread(s, 2 * k + i) for i in range(k)]
    x = s
    for i in range(k):
        scale = 1.0 / cols[i][i : i + 1]
        pivot = x[i : i + 1] * scale
        x = jnp.where(row == i, pivot, x - cols[i] * pivot)
        for j in range(i + 1, k):
            part = cols[j][i : i + 1] * scale
            cols[j] = jnp.where(row == i, part, cols[j] - cols[i] * part)
    coef = x[:, 3 * k : 4 * k]
    eye = lax.broadcasted_iota(jnp.int32, (k, k), 0) == lax.broadcasted_iota(jnp.int32, (k, k), 1)
    ritz_ref[...] = jnp.sum(jnp.where(eye, coef, 0.0), axis=0, keepdims=True) * (1.0 / SCALE)
    s1, b1 = s[:, :k], s[:, k : 2 * k]
    s2, b2, aa = s[:, 4 * k : 5 * k], s[:, 5 * k : 6 * k], s[:, 6 * k : 7 * k]
    known = jnp.concatenate([x[:, :k], s1, s2], axis=0)
    known = known - dot32(jnp.concatenate([x[:, k : 2 * k], b1, b2], axis=0), coef)
    mix, corr, weighted = known[:k], known[k : 2 * k], known[2 * k :]
    gram = aa - dot32(
        jnp.concatenate([s2, coef, corr], axis=0), jnp.concatenate([coef, weighted, mix], axis=0), TN
    )
    cols = [spread(gram, i) for i in range(k)]
    pad = jnp.zeros((k, 128 - 3 * k), F32)
    x = jnp.concatenate([eye.astype(F32), -coef.T, -mix.T, pad], axis=1)
    for i in range(k):
        pivot = cols[i][i : i + 1]
        scale = 1.0 / pivot
        below = jnp.where(row > i, cols[i] * scale, 0.0)
        pivot_row = x[i : i + 1]
        x = jnp.where(row == i, pivot_row * (lax.rsqrt(pivot) * (total ** 0.5)), x - below * pivot_row)
        for j in range(i + 1, k):
            cols[j] = cols[j] - below * cols[j][i : i + 1]
    hi, mid, _ = split3(x[:, : 3 * k])
    lhs = jnp.concatenate([hi, hi, mid], axis=1)
    block = min(ch * r, 1024)

    def result(b, carry):
        at = pl.ds(pl.multiple_of(b * block, block), block)
        x_hi = jnp.concatenate([az_ref[:k, at], zhm_ref[: 2 * k, at]], axis=0)
        x_mid = jnp.concatenate([az_ref[k:, at], zhm_ref[2 * k :, at]], axis=0)
        new = lax.dot_general(
            lhs, jnp.concatenate([x_hi, x_mid, x_hi], axis=0), NN, preferred_element_type=F32
        )
        for i in range(block // r):
            out_ref[b * (block // r) + i] = new[:, i * r : (i + 1) * r]
        return carry

    lax.fori_loop(0, ch * r // block, result, 0, unroll=True)


def gather_sums(x):
    n_chan, n_rad = lax.axis_size("chan"), lax.axis_size("rad")
    step = 1
    while step < n_rad:
        x = x + swap(x, "rad", step)
        step *= 2
    every = jnp.broadcast_to(x, (n_chan,) + x.shape)
    return lax.all_to_all(every, "chan", split_axis=0, concat_axis=0, tiled=True)


def body(trial_block, ham_blocks, partners, stored_at, precond_diag):
    n_chan, n_rad = lax.axis_size("chan"), lax.axis_size("rad")
    ch, k, r = trial_block.shape
    ncoup, splines = ham_blocks.shape[1], ham_blocks.shape[3]
    lanes = ch * r
    total = float(n_chan * n_rad * lanes)
    share, nz = ch // n_rad, n_chan // 4

    barrier = lax.optimization_barrier
    smem = pl.BlockSpec(memory_space=pltpu.SMEM)
    any_ = pl.BlockSpec(memory_space=pl.ANY)
    whole = pl.BlockSpec(memory_space=pltpu.VMEM)

    def near_of(x):
        return plane_swap(x, (1, 2))

    def far_of(x):
        return plane_swap(x, (2, 1))

    def flat(x):
        return x.reshape((-1,) + x.shape[2:])

    def in_cores(x):
        return [x] + [swap(x, "rad", c) for c in range(1, n_rad)]

    own = jnp.concatenate(jnp.split(trial_block.astype(BF16), n_rad), axis=2)[None]
    near0, far_own = near_of(own), far_of(own)
    z1 = swap(own, "chan", 4)
    z_even = jnp.concatenate([swap(own, "chan", 4 * z) for z in range(2, nz, 2)])
    rows, ham, zhm, zl, dc, gram_t = pl.pallas_call(
        functools.partial(prepare_kernel, n_chan, n_rad),
        in_specs=[any_] * 5,
        out_specs=[whole] * 6,
        out_shape=[
            jax.ShapeDtypeStruct((ncoup, ch), jnp.int32),
            pltpu.VMEM(ham_blocks.shape, BF16),
            pltpu.VMEM((4 * k, lanes), BF16),
            pltpu.VMEM((2 * k, lanes), BF16),
            pltpu.VMEM((1, lanes), F32),
            pltpu.VMEM((k, 3 * k), F32),
        ],
        scratch_shapes=[
            pltpu.VMEM(trial_block.shape, F32),
            pltpu.VMEM(precond_diag.shape, F32),
            pltpu.VMEM((ncoup, ch), jnp.int32),
            pltpu.VMEM((stored_at.shape[0] // 128, 128), jnp.int32),
            pltpu.SemaphoreType.DMA((5,)),
        ],
        compiler_params=pltpu.CompilerParams(vmem_limit_bytes=VMEM_LIMIT),
        name="prepare",
    )(
        in_hbm(trial_block),
        in_hbm(precond_diag),
        in_hbm(partners.T),
        in_hbm(stored_at.reshape(-1, 128)),
        in_hbm(ham_blocks),
    )
    far_own, near0, z1, z_even, rows = barrier((far_own, near0, z1, z_even, rows))
    some = jnp.concatenate([z1, z_even])
    some, more, z_even = barrier((some, jnp.concatenate([some, near0]), z_even))
    near1, far1 = near_of(some), far_of(more)
    z_odd = swap(z_even, "chan", 4)
    z_odd, far1, near1 = barrier((z_odd, far1, near1))
    diag0 = far1[-1:]
    early = in_cores(
        jnp.concatenate([own, z1, z_even, near0, far_own, near1, z_odd, far1])
    )
    near_odd = near_of(z_odd)
    diag_odd = jnp.concatenate([swap(diag0, "chan", 4 * z) for z in range(3, nz, 2)])
    far2 = far_of(jnp.concatenate([z_odd, near1]))
    table = pl.pallas_call(
        functools.partial(assemble_kernel, nz, share),
        in_specs=[whole] * n_rad,
        out_specs=whole,
        out_shape=pltpu.VMEM((n_chan * ch, k, splines), BF16),
        compiler_params=pltpu.CompilerParams(vmem_limit_bytes=VMEM_LIMIT),
        name="assemble",
    )(*[in_vmem(flat(x)) for x in early])
    near_odd, diag_odd, far2, table = barrier((near_odd, diag_odd, far2, table))
    last = [in_vmem(flat(x)) for x in in_cores(jnp.concatenate([near_odd, far2, diag_odd]))]

    az, sums, _ = pl.pallas_call(
        functools.partial(apply_kernel, nz, share),
        in_specs=[smem] + [whole] * (6 + n_rad),
        out_specs=[whole, whole, whole],
        out_shape=[
            pltpu.VMEM((2 * k, lanes), BF16),
            jax.ShapeDtypeStruct((k, 8 * k), F32),
            pltpu.VMEM(table.shape, BF16),
        ],
        input_output_aliases={2: 2},
        scratch_shapes=[pltpu.VMEM((k, lanes), F32)],
        compiler_params=pltpu.CompilerParams(vmem_limit_bytes=VMEM_LIMIT),
        name="apply",
    )(rows, in_vmem(ham), in_vmem(table), in_vmem(zhm), in_vmem(zl), in_vmem(dc), gram_t, *last)

    sums = gather_sums(sums)
    new_block, ritz = pl.pallas_call(
        functools.partial(finish_kernel, total),
        out_shape=[
            jax.ShapeDtypeStruct((ch, k, r), F32),
            jax.ShapeDtypeStruct((1, k), F32),
        ],
        compiler_params=pltpu.CompilerParams(vmem_limit_bytes=VMEM_LIMIT),
        name="finish",
    )(sums, in_vmem(az), in_vmem(zhm))
    return (new_block, ritz.reshape(k))


def solution(mesh):
    return jax.shard_map(
        body,
        mesh=mesh,
        in_specs=(
            P("chan", None, "rad"),
            P("chan", None, "rad", None),
            P("chan", None),
            P(),
            P("chan", "rad"),
        ),
        out_specs=(P("chan", None, "rad"), P()),
        check_vma=False,
    )
```

```python
import functools

import jax
import jax.numpy as jnp
from jax import lax
from jax.experimental import pallas as pl
from jax.experimental.pallas import tpu as pltpu
from jax.sharding import PartitionSpec as P

SCALE = 2.0 ** -8
F32 = jnp.float32
BF16 = jnp.bfloat16
NT = (((1,), (1,)), ((), ()))
TN = (((0,), (0,)), ((), ()))
NN = (((1,), (0,)), ((), ()))
VMEM_LIMIT = 4 * 1024 * 1024


def swap(x, axis, distance):
    n = lax.axis_size(axis)
    return lax.ppermute(x, axis, [(i, i ^ distance) for i in range(n)])


def plane_swap(x, order):
    n_chan, n_rad = lax.axis_size("chan"), lax.axis_size("rad")
    pairs = []
    for c in range(n_chan):
        for r in range(n_rad):
            pairs.append((c * n_rad + r, (c ^ order[r % 2]) * n_rad + r))
    return lax.ppermute(x, ("chan", "rad"), pairs)


def table_piece(z, part, nz):
    some, odd = nz // 2, nz // 2 - 1
    is_odd = (z & 1 == 1) & (z > 1)
    i = jnp.where(is_odd, (z - 3) >> 1, jnp.where(z == 1, 0, z >> 1))
    base = 2 * some + odd + 4

    def pick(own, of_some, of_odd):
        return jnp.where(z == 0, own, jnp.where(is_odd, of_odd + i, of_some + i))

    here = pick(0, 1, 2 * some + 4)
    near = pick(some + 1, some + 4, base + some)
    far = pick(some + 2, base, base + some + odd)
    both = pick(some + 3, base + some + 2 * odd, base + 2 * some + 2 * odd)
    return jnp.where(part == 0, here, jnp.where(part == 1, near, jnp.where(part == 2, far, both)))


def early_pieces(nz):
    some, odd = [1] + list(range(2, nz, 2)), list(range(3, nz, 2))
    order = [(0, 0)] + [(z, 0) for z in some] + [(0, 1), (0, 2), (0, 3)] + [(z, 1) for z in some]
    return order + [(z, 0) for z in odd] + [(z, 2) for z in some]


def late_pieces(nz):
    some, odd = [1] + list(range(2, nz, 2)), list(range(3, nz, 2))
    return [(z, 1) for z in odd] + [(z, 2) for z in odd] + [(z, 3) for z in some + odd]


def merge(refs, table_ref, order, start, share):
    n_rad = len(refs)
    r = 128 // n_rad
    me = lax.axis_index("rad")

    def rows(n, carry):
        for i, (z, part) in enumerate(order):
            other = order.index((z, (0, 2, 1, 3)[part]))
            tiles = [ref[(other if s % 2 else i) * share + n] for s, ref in enumerate(refs)]
            by_core = []
            for c in range(n_rad):
                x = tiles[0]
                for s in range(1, n_rad):
                    x = jnp.where((me ^ s) == c, tiles[s], x)
                by_core.append(x)
            for g in range(n_rad):
                row = jnp.concatenate([x[:, g * r : (g + 1) * r] for x in by_core], axis=1)
                table_ref[((start + i) * n_rad + g) * share + n] = row
        return carry

    lax.fori_loop(0, share, rows, 0, unroll=min(8, share))


def in_vmem(x):
    return pltpu.with_memory_space_constraint(x, pltpu.VMEM)


def in_hbm(x):
    return pltpu.with_memory_space_constraint(x, pltpu.HBM)


def split3(x):
    hi = x.astype(BF16)
    rest = x - hi.astype(F32)
    mid = rest.astype(BF16)
    return hi, mid, (rest - mid.astype(F32)).astype(BF16)


def dot32(x, y, dims=NN):
    return lax.dot_general(x, y, dims, precision=lax.Precision.HIGHEST, preferred_element_type=F32)


def block_sum(g, rows, cols):
    g = sum(g[i : i + rows] for i in range(0, g.shape[0], rows))
    return sum(g[:, i : i + cols] for i in range(0, g.shape[1], cols))


def prepare_kernel(
    n_chan, n_rad, t_hbm, d_hbm, partners_hbm, stored_hbm, ham_hbm,
    rows_ref, ham_ref, zhm_ref, zl_ref, dc_ref, gram_ref, t_ref, d_ref, partners_ref, stored_ref, sems,
):
    moves = (
        (t_hbm, t_ref), (d_hbm, d_ref), (partners_hbm, partners_ref), (stored_hbm, stored_ref), (ham_hbm, ham_ref)
    )
    copies = [pltpu.make_async_copy(x, y, sems.at[i]) for i, (x, y) in enumerate(moves)]
    for copy in copies:
        copy.start()
    for copy in copies[:4]:
        copy.wait()
    ch, k, r = t_ref.shape
    group = 128 // r
    for i in range(ch // group):
        lanes = pl.ds(i * 128, 128)
        t = jnp.concatenate([t_ref[i * group + g] for g in range(group)], axis=1)
        d = jnp.concatenate([d_ref[pl.ds(i * group + g, 1), :] for g in range(group)], axis=1)
        dc_ref[:, lanes] = d
        hi, mid, lo = split3(jnp.concatenate([t / d, t], axis=0))
        zhm_ref[:, lanes] = jnp.concatenate([hi, mid], axis=0)
        zl_ref[:, lanes] = lo
    z = jnp.concatenate([zhm_ref[...], zl_ref[...]], axis=0)
    g = block_sum(lax.dot_general(z, z, NT, preferred_element_type=F32), 2 * k, 2 * k)
    gram_ref[...] = jnp.concatenate([g[k:, :], g[:k, :k]], axis=1)

    share, nz = ch // n_rad, n_chan // 4
    q = stored_ref[...]
    owner, local = lax.div(q, ch), lax.rem(q, ch)
    apart = (owner ^ lax.axis_index("chan")) & 3
    turned = ((apart & 1) << 1) | (apart >> 1)
    part = jnp.where((lax.axis_index("rad") & 1) == 1, turned, apart)
    piece = table_piece((owner ^ lax.axis_index("chan")) >> 2, part, nz)
    place = (piece * ch + local).astype(F32)
    lane = lax.broadcasted_iota(jnp.int32, (ch, 128), 1)
    columns = []
    partners = partners_ref[...].astype(F32).T.astype(jnp.int32)
    for j in range(partners.shape[1]):
        wanted = jnp.broadcast_to(partners[:, j : j + 1], (ch, 128)) - lane
        found = jnp.zeros((ch, 128), F32)
        for c in range(place.shape[0]):
            found = found + jnp.where(wanted == 128 * c, place[c : c + 1], 0.0)
        columns.append(jnp.sum(found, axis=1, keepdims=True))
    rows_ref[...] = jnp.concatenate(columns, axis=1).T.astype(jnp.int32)
    copies[4].wait()


def assemble_kernel(nz, share, *refs):
    merge(refs[:-1], refs[-1], early_pieces(nz), 0, share)


def apply_kernel(nz, share, rows_ref, ham_ref, _, zhm_ref, zl_ref, dc_ref, gt_ref, *rest):
    last, (az_ref, sums_ref, table_ref, a0_ref) = rest[:-4], rest[-4:]
    merge(last, table_ref, late_pieces(nz), len(early_pieces(nz)), share)
    ch, ncoup, r, splines = ham_ref.shape
    k = zl_ref.shape[0] // 2
    group = 256 // r

    def work(g, carry):
        left, right = [], []
        for i in range(group):
            p = g * group + i
            left.append(
                jnp.concatenate([table_ref[rows_ref[j, p]] for j in range(ncoup)], axis=1)
            )
            right.append(jnp.concatenate([ham_ref[p, j] for j in range(ncoup)], axis=1))
        product = lax.dot_general(
            jnp.concatenate(left, axis=0),
            jnp.concatenate(right, axis=0),
            NT,
            preferred_element_type=F32,
        )
        own = [product[i * k : (i + 1) * k, i * r : (i + 1) * r] for i in range(group)]
        a0_ref[:, pl.ds(pl.multiple_of(g * 256, 256), 256)] = jnp.concatenate(own, axis=1) * SCALE
        return carry

    lax.fori_loop(0, ch // group, work, 0, unroll=min(4, ch // group))

    lanes = ch * r
    block = min(lanes, 1024)

    def gram_block(i, gram):
        at = pl.ds(pl.multiple_of(i * block, block), block)
        a0 = a0_ref[:, at]
        a1_terms = split3(a0 / dc_ref[:, at])
        az_ref[:, at] = jnp.concatenate(a1_terms[:2], axis=0)
        right = jnp.concatenate(a1_terms + split3(a0), axis=0)
        left = jnp.concatenate([zhm_ref[:, at], zl_ref[:, at], right[: 3 * k]], axis=0)
        return gram + lax.dot_general(left, right, NT, preferred_element_type=F32)

    gram = lax.fori_loop(
        0, lanes // block, gram_block, jnp.zeros((9 * k, 6 * k), F32), unroll=True
    )
    ta1 = block_sum(gram[: 6 * k, : 3 * k], 2 * k, k)
    ta0 = block_sum(gram[: 6 * k, 3 * k :], 2 * k, k)
    aa = block_sum(gram[6 * k :, : 3 * k], k, k)
    gt = gt_ref[...]
    parts = [ta1[k:], gt[:, : 2 * k], ta0[k:], ta1[:k], gt[:, 2 * k :], aa, jnp.zeros((k, k), F32)]
    sums_ref[...] = jnp.concatenate(parts, axis=1)


def spread(x, i):
    return jnp.broadcast_to(x[:, i : i + 1], (x.shape[0], 128))


def finish_kernel(total, sums_ref, az_ref, zhm_ref, out_ref, ritz_ref):
    ch, k, r = out_ref.shape
    s = jnp.sum(sums_ref[...], axis=0)
    row = lax.broadcasted_iota(jnp.int32, (k, 128), 0)
    cols = [spread(s, 2 * k + i) for i in range(k)]
    x = s
    for i in range(k):
        scale = 1.0 / cols[i][i : i + 1]
        pivot = x[i : i + 1] * scale
        x = jnp.where(row == i, pivot, x - cols[i] * pivot)
        for j in range(i + 1, k):
            part = cols[j][i : i + 1] * scale
            cols[j] = jnp.where(row == i, part, cols[j] - cols[i] * part)
    coef = x[:, 3 * k : 4 * k]
    eye = lax.broadcasted_iota(jnp.int32, (k, k), 0) == lax.broadcasted_iota(jnp.int32, (k, k), 1)
    ritz_ref[...] = jnp.sum(jnp.where(eye, coef, 0.0), axis=0, keepdims=True) * (1.0 / SCALE)
    s1, b1 = s[:, :k], s[:, k : 2 * k]
    s2, b2, aa = s[:, 4 * k : 5 * k], s[:, 5 * k : 6 * k], s[:, 6 * k : 7 * k]
    known = jnp.concatenate([x[:, :k], s1, s2], axis=0)
    known = known - dot32(jnp.concatenate([x[:, k : 2 * k], b1, b2], axis=0), coef)
    mix, corr, weighted = known[:k], known[k : 2 * k], known[2 * k :]
    gram = aa - dot32(
        jnp.concatenate([s2, coef, corr], axis=0), jnp.concatenate([coef, weighted, mix], axis=0), TN
    )
    cols = [spread(gram, i) for i in range(k)]
    pad = jnp.zeros((k, 128 - 3 * k), F32)
    x = jnp.concatenate([eye.astype(F32), -coef.T, -mix.T, pad], axis=1)
    for i in range(k):
        pivot = cols[i][i : i + 1]
        scale = 1.0 / pivot
        below = jnp.where(row > i, cols[i] * scale, 0.0)
        pivot_row = x[i : i + 1]
        x = jnp.where(row == i, pivot_row * (lax.rsqrt(pivot) * (total ** 0.5)), x - below * pivot_row)
        for j in range(i + 1, k):
            cols[j] = cols[j] - below * cols[j][i : i + 1]
    hi, mid, _ = split3(x[:, : 3 * k])
    lhs = jnp.concatenate([hi, hi, mid], axis=1)
    block = min(ch * r, 1024)

    def result(b, carry):
        at = pl.ds(pl.multiple_of(b * block, block), block)
        x_hi = jnp.concatenate([az_ref[:k, at], zhm_ref[: 2 * k, at]], axis=0)
        x_mid = jnp.concatenate([az_ref[k:, at], zhm_ref[2 * k :, at]], axis=0)
        new = lax.dot_general(
            lhs, jnp.concatenate([x_hi, x_mid, x_hi], axis=0), NN, preferred_element_type=F32
        )
        for i in range(block // r):
            out_ref[b * (block // r) + i] = new[:, i * r : (i + 1) * r]
        return carry

    lax.fori_loop(0, ch * r // block, result, 0, unroll=True)


def gather_sums(x):
    n_chan, n_rad = lax.axis_size("chan"), lax.axis_size("rad")
    step = 1
    while step < n_rad:
        x = x + swap(x, "rad", step)
        step *= 2
    every = jnp.broadcast_to(x, (n_chan,) + x.shape)
    return lax.all_to_all(every, "chan", split_axis=0, concat_axis=0, tiled=True)


def body(trial_block, ham_blocks, partners, stored_at, precond_diag):
    n_chan, n_rad = lax.axis_size("chan"), lax.axis_size("rad")
    ch, k, r = trial_block.shape
    ncoup, splines = ham_blocks.shape[1], ham_blocks.shape[3]
    lanes = ch * r
    total = float(n_chan * n_rad * lanes)
    share, nz = ch // n_rad, n_chan // 4

    barrier = lax.optimization_barrier
    smem = pl.BlockSpec(memory_space=pltpu.SMEM)
    any_ = pl.BlockSpec(memory_space=pl.ANY)
    whole = pl.BlockSpec(memory_space=pltpu.VMEM)

    def near_of(x):
        return plane_swap(x, (1, 2))

    def far_of(x):
        return plane_swap(x, (2, 1))

    def flat(x):
        return x.reshape((-1,) + x.shape[2:])

    def in_cores(x):
        return [x] + [swap(x, "rad", c) for c in range(1, n_rad)]

    own = jnp.concatenate(jnp.split(trial_block.astype(BF16), n_rad), axis=2)[None]
    near0, far_own, diag0 = near_of(own), far_of(own), swap(own, "chan", 3)
    z1 = swap(own, "chan", 4)
    z_even = jnp.concatenate([swap(own, "chan", 4 * z) for z in range(2, nz, 2)])
    rows, ham, zhm, zl, dc, gram_t = pl.pallas_call(
        functools.partial(prepare_kernel, n_chan, n_rad),
        in_specs=[any_] * 5,
        out_specs=[whole] * 6,
        out_shape=[
            jax.ShapeDtypeStruct((ncoup, ch), jnp.int32),
            pltpu.VMEM(ham_blocks.shape, BF16),
            pltpu.VMEM((4 * k, lanes), BF16),
            pltpu.VMEM((2 * k, lanes), BF16),
            pltpu.VMEM((1, lanes), F32),
            pltpu.VMEM((k, 3 * k), F32),
        ],
        scratch_shapes=[
            pltpu.VMEM(trial_block.shape, F32),
            pltpu.VMEM(precond_diag.shape, F32),
            pltpu.VMEM((ncoup, ch), jnp.int32),
            pltpu.VMEM((stored_at.shape[0] // 128, 128), jnp.int32),
            pltpu.SemaphoreType.DMA((5,)),
        ],
        compiler_params=pltpu.CompilerParams(vmem_limit_bytes=VMEM_LIMIT),
        name="prepare",
    )(
        in_hbm(trial_block),
        in_hbm(precond_diag),
        in_hbm(partners.T),
        in_hbm(stored_at.reshape(-1, 128)),
        in_hbm(ham_blocks),
    )
    far_own, near0, z1, z_even, diag0, rows = barrier((far_own, near0, z1, z_even, diag0, rows))
    some, z_even, diag0 = barrier((jnp.concatenate([z1, z_even]), z_even, diag0))
    near1, far1 = near_of(some), far_of(some)
    z_odd = swap(z_even, "chan", 4)
    z_odd, far1, near1, diag0 = barrier((z_odd, far1, near1, diag0))
    early = in_cores(
        jnp.concatenate([own, z1, z_even, near0, far_own, diag0, near1, z_odd, far1])
    )
    near_odd = near_of(z_odd)
    diag_odd = jnp.concatenate([swap(diag0, "chan", 4 * z) for z in range(3, nz, 2)])
    far2 = far_of(jnp.concatenate([z_odd, near1]))
    table = pl.pallas_call(
        functools.partial(assemble_kernel, nz, share),
        in_specs=[whole] * n_rad,
        out_specs=whole,
        out_shape=pltpu.VMEM((n_chan * ch, k, splines), BF16),
        compiler_params=pltpu.CompilerParams(vmem_limit_bytes=VMEM_LIMIT),
        name="assemble",
    )(*[in_vmem(flat(x)) for x in early])
    near_odd, diag_odd, far2, table = barrier((near_odd, diag_odd, far2, table))
    last = [in_vmem(flat(x)) for x in in_cores(jnp.concatenate([near_odd, far2, diag_odd]))]

    az, sums, _ = pl.pallas_call(
        functools.partial(apply_kernel, nz, share),
        in_specs=[smem] + [whole] * (6 + n_rad),
        out_specs=[whole, whole, whole],
        out_shape=[
            pltpu.VMEM((2 * k, lanes), BF16),
            jax.ShapeDtypeStruct((k, 8 * k), F32),
            pltpu.VMEM(table.shape, BF16),
        ],
        input_output_aliases={2: 2},
        scratch_shapes=[pltpu.VMEM((k, lanes), F32)],
        compiler_params=pltpu.CompilerParams(vmem_limit_bytes=VMEM_LIMIT),
        name="apply",
    )(rows, in_vmem(ham), in_vmem(table), in_vmem(zhm), in_vmem(zl), in_vmem(dc), gram_t, *last)

    sums = gather_sums(sums)
    new_block, ritz = pl.pallas_call(
        functools.partial(finish_kernel, total),
        out_shape=[
            jax.ShapeDtypeStruct((ch, k, r), F32),
            jax.ShapeDtypeStruct((1, k), F32),
        ],
        compiler_params=pltpu.CompilerParams(vmem_limit_bytes=VMEM_LIMIT),
        name="finish",
    )(sums, in_vmem(az), in_vmem(zhm))
    return (new_block, ritz.reshape(k))


def solution(mesh):
    return jax.shard_map(
        body,
        mesh=mesh,
        in_specs=(
            P("chan", None, "rad"),
            P("chan", None, "rad", None),
            P("chan", None),
            P(),
            P("chan", "rad"),
        ),
        out_specs=(P("chan", None, "rad"), P()),
        check_vma=False,
    )
```

```python
import functools

import jax
import jax.numpy as jnp
from jax import lax
from jax.experimental import pallas as pl
from jax.experimental.pallas import tpu as pltpu
from jax.sharding import PartitionSpec as P

SCALE = 2.0 ** -8
F32 = jnp.float32
BF16 = jnp.bfloat16
NT = (((1,), (1,)), ((), ()))
TN = (((0,), (0,)), ((), ()))
NN = (((1,), (0,)), ((), ()))
VMEM_LIMIT = 4 * 1024 * 1024


def swap(x, axis, distance):
    n = lax.axis_size(axis)
    return lax.ppermute(x, axis, [(i, i ^ distance) for i in range(n)])


def plane_swap(x, order):
    n_chan, n_rad = lax.axis_size("chan"), lax.axis_size("rad")
    pairs = []
    for c in range(n_chan):
        for r in range(n_rad):
            pairs.append((c * n_rad + r, (c ^ order[r % 2]) * n_rad + r))
    return lax.ppermute(x, ("chan", "rad"), pairs)


def table_piece(z, part, nz):
    some, odd = nz // 2, nz // 2 - 1
    is_odd = (z & 1 == 1) & (z > 1)
    i = jnp.where(is_odd, (z - 3) >> 1, jnp.where(z == 1, 0, z >> 1))
    base = 2 * some + odd + 4

    def pick(own, of_some, of_odd):
        return jnp.where(z == 0, own, jnp.where(is_odd, of_odd + i, of_some + i))

    here = pick(0, 1, 2 * some + 4)
    near = pick(some + 1, some + 4, base + some)
    far = pick(some + 2, base, base + some + odd)
    both = pick(some + 3, base + some + 2 * odd, base + 2 * some + 2 * odd)
    return jnp.where(part == 0, here, jnp.where(part == 1, near, jnp.where(part == 2, far, both)))


def early_pieces(nz):
    some, odd = [1] + list(range(2, nz, 2)), list(range(3, nz, 2))
    order = [(0, 0)] + [(z, 0) for z in some] + [(0, 1), (0, 2), (0, 3)] + [(z, 1) for z in some]
    return order + [(z, 0) for z in odd] + [(z, 2) for z in some]


def late_pieces(nz):
    some, odd = [1] + list(range(2, nz, 2)), list(range(3, nz, 2))
    return [(z, 1) for z in odd] + [(z, 2) for z in odd] + [(z, 3) for z in some + odd]


def merge(refs, table_ref, order, start, share, unroll):
    n_rad = len(refs)
    r = 128 // n_rad
    me = lax.axis_index("rad")

    def rows(n, carry):
        for i, (z, part) in enumerate(order):
            other = order.index((z, (0, 2, 1, 3)[part]))
            tiles = [ref[(other if s % 2 else i) * share + n] for s, ref in enumerate(refs)]
            by_core = []
            for c in range(n_rad):
                x = tiles[0]
                for s in range(1, n_rad):
                    x = jnp.where((me ^ s) == c, tiles[s], x)
                by_core.append(x)
            for g in range(n_rad):
                row = jnp.concatenate([x[:, g * r : (g + 1) * r] for x in by_core], axis=1)
                table_ref[((start + i) * n_rad + g) * share + n] = row
        return carry

    lax.fori_loop(0, share, rows, 0, unroll=min(unroll, share))


def in_vmem(x):
    return pltpu.with_memory_space_constraint(x, pltpu.VMEM)


def in_hbm(x):
    return pltpu.with_memory_space_constraint(x, pltpu.HBM)


def split3(x):
    hi = x.astype(BF16)
    rest = x - hi.astype(F32)
    mid = rest.astype(BF16)
    return hi, mid, (rest - mid.astype(F32)).astype(BF16)


def dot32(x, y, dims=NN):
    return lax.dot_general(x, y, dims, precision=lax.Precision.HIGHEST, preferred_element_type=F32)


def block_sum(g, rows, cols):
    g = sum(g[i : i + rows] for i in range(0, g.shape[0], rows))
    return sum(g[:, i : i + cols] for i in range(0, g.shape[1], cols))


def prepare_kernel(
    n_chan, n_rad, t_hbm, d_hbm, partners_hbm, stored_hbm, ham_hbm,
    rows_ref, ham_ref, zhm_ref, zl_ref, dc_ref, gram_ref, t_ref, d_ref, partners_ref, stored_ref, sems,
):
    moves = (
        (t_hbm, t_ref), (d_hbm, d_ref), (partners_hbm, partners_ref), (stored_hbm, stored_ref), (ham_hbm, ham_ref)
    )
    copies = [pltpu.make_async_copy(x, y, sems.at[i]) for i, (x, y) in enumerate(moves)]
    for copy in copies:
        copy.start()
    for copy in copies[:4]:
        copy.wait()
    ch, k, r = t_ref.shape
    group = 128 // r
    for i in range(ch // group):
        lanes = pl.ds(i * 128, 128)
        t = jnp.concatenate([t_ref[i * group + g] for g in range(group)], axis=1)
        d = jnp.concatenate([d_ref[pl.ds(i * group + g, 1), :] for g in range(group)], axis=1)
        dc_ref[:, lanes] = d
        hi, mid, lo = split3(jnp.concatenate([t / d, t], axis=0))
        zhm_ref[:, lanes] = jnp.concatenate([hi, mid], axis=0)
        zl_ref[:, lanes] = lo
    z = jnp.concatenate([zhm_ref[...], zl_ref[...]], axis=0)
    g = block_sum(lax.dot_general(z, z, NT, preferred_element_type=F32), 2 * k, 2 * k)
    gram_ref[...] = jnp.concatenate([g[k:, :], g[:k, :k]], axis=1)

    share, nz = ch // n_rad, n_chan // 4
    q = stored_ref[...]
    owner, local = lax.div(q, ch), lax.rem(q, ch)
    apart = (owner ^ lax.axis_index("chan")) & 3
    turned = ((apart & 1) << 1) | (apart >> 1)
    part = jnp.where((lax.axis_index("rad") & 1) == 1, turned, apart)
    piece = table_piece((owner ^ lax.axis_index("chan")) >> 2, part, nz)
    place = (piece * ch + local).astype(F32)
    lane = lax.broadcasted_iota(jnp.int32, (ch, 128), 1)
    columns = []
    partners = partners_ref[...].astype(F32).T.astype(jnp.int32)
    for j in range(partners.shape[1]):
        wanted = jnp.broadcast_to(partners[:, j : j + 1], (ch, 128)) - lane
        found = jnp.zeros((ch, 128), F32)
        for c in range(place.shape[0]):
            found = found + jnp.where(wanted == 128 * c, place[c : c + 1], 0.0)
        columns.append(jnp.sum(found, axis=1, keepdims=True))
    rows_ref[...] = jnp.concatenate(columns, axis=1).T.astype(jnp.int32)
    copies[4].wait()


def assemble_kernel(nz, share, *refs):
    merge(refs[:-1], refs[-1], early_pieces(nz), 0, share, 8)


def apply_kernel(nz, share, rows_ref, ham_ref, _, zhm_ref, zl_ref, dc_ref, gt_ref, *rest):
    last, (az_ref, sums_ref, table_ref, a0_ref) = rest[:-4], rest[-4:]
    merge(last, table_ref, late_pieces(nz), len(early_pieces(nz)), share, 32)
    ch, ncoup, r, splines = ham_ref.shape
    k = zl_ref.shape[0] // 2
    group = 256 // r

    def work(g, carry):
        left, right = [], []
        for i in range(group):
            p = g * group + i
            left.append(
                jnp.concatenate([table_ref[rows_ref[j, p]] for j in range(ncoup)], axis=1)
            )
            right.append(jnp.concatenate([ham_ref[p, j] for j in range(ncoup)], axis=1))
        product = lax.dot_general(
            jnp.concatenate(left, axis=0),
            jnp.concatenate(right, axis=0),
            NT,
            preferred_element_type=F32,
        )
        own = [product[i * k : (i + 1) * k, i * r : (i + 1) * r] for i in range(group)]
        a0_ref[:, pl.ds(pl.multiple_of(g * 256, 256), 256)] = jnp.concatenate(own, axis=1) * SCALE
        return carry

    lax.fori_loop(0, ch // group, work, 0, unroll=min(8, ch // group))

    lanes = ch * r
    block = min(lanes, 1024)

    def gram_block(i, gram):
        at = pl.ds(pl.multiple_of(i * block, block), block)
        a0 = a0_ref[:, at]
        a1_terms = split3(a0 / dc_ref[:, at])
        az_ref[:, at] = jnp.concatenate(a1_terms[:2], axis=0)
        right = jnp.concatenate(a1_terms + split3(a0), axis=0)
        left = jnp.concatenate([zhm_ref[:, at], zl_ref[:, at], right[: 3 * k]], axis=0)
        return gram + lax.dot_general(left, right, NT, preferred_element_type=F32)

    gram = lax.fori_loop(
        0, lanes // block, gram_block, jnp.zeros((9 * k, 6 * k), F32), unroll=True
    )
    ta1 = block_sum(gram[: 6 * k, : 3 * k], 2 * k, k)
    ta0 = block_sum(gram[: 6 * k, 3 * k :], 2 * k, k)
    aa = block_sum(gram[6 * k :, : 3 * k], k, k)
    gt = gt_ref[...]
    parts = [ta1[k:], gt[:, : 2 * k], ta0[k:], ta1[:k], gt[:, 2 * k :], aa, jnp.zeros((k, k), F32)]
    sums_ref[...] = jnp.concatenate(parts, axis=1)


def spread(x, i):
    return jnp.broadcast_to(x[:, i : i + 1], (x.shape[0], 128))


def finish_kernel(total, sums_ref, az_ref, zhm_ref, out_ref, ritz_ref):
    ch, k, r = out_ref.shape
    s = jnp.sum(sums_ref[...], axis=0)
    row = lax.broadcasted_iota(jnp.int32, (k, 128), 0)
    cols = [spread(s, 2 * k + i) for i in range(k)]
    x = s
    for i in range(k):
        scale = 1.0 / cols[i][i : i + 1]
        pivot = x[i : i + 1] * scale
        x = jnp.where(row == i, pivot, x - cols[i] * pivot)
        for j in range(i + 1, k):
            part = cols[j][i : i + 1] * scale
            cols[j] = jnp.where(row == i, part, cols[j] - cols[i] * part)
    coef = x[:, 3 * k : 4 * k]
    eye = lax.broadcasted_iota(jnp.int32, (k, k), 0) == lax.broadcasted_iota(jnp.int32, (k, k), 1)
    ritz_ref[...] = jnp.sum(jnp.where(eye, coef, 0.0), axis=0, keepdims=True) * (1.0 / SCALE)
    s1, b1 = s[:, :k], s[:, k : 2 * k]
    s2, b2, aa = s[:, 4 * k : 5 * k], s[:, 5 * k : 6 * k], s[:, 6 * k : 7 * k]
    known = jnp.concatenate([x[:, :k], s1, s2], axis=0)
    known = known - dot32(jnp.concatenate([x[:, k : 2 * k], b1, b2], axis=0), coef)
    mix, corr, weighted = known[:k], known[k : 2 * k], known[2 * k :]
    gram = aa - dot32(
        jnp.concatenate([s2, coef, corr], axis=0), jnp.concatenate([coef, weighted, mix], axis=0), TN
    )
    cols = [spread(gram, i) for i in range(k)]
    pad = jnp.zeros((k, 128 - 3 * k), F32)
    x = jnp.concatenate([eye.astype(F32), -coef.T, -mix.T, pad], axis=1)
    for i in range(k):
        pivot = cols[i][i : i + 1]
        scale = 1.0 / pivot
        below = jnp.where(row > i, cols[i] * scale, 0.0)
        pivot_row = x[i : i + 1]
        x = jnp.where(row == i, pivot_row * (lax.rsqrt(pivot) * (total ** 0.5)), x - below * pivot_row)
        for j in range(i + 1, k):
            cols[j] = cols[j] - below * cols[j][i : i + 1]
    hi, mid, _ = split3(x[:, : 3 * k])
    lhs = jnp.concatenate([hi, hi, mid], axis=1)
    block = min(ch * r, 1024)

    def result(b, carry):
        at = pl.ds(pl.multiple_of(b * block, block), block)
        x_hi = jnp.concatenate([az_ref[:k, at], zhm_ref[: 2 * k, at]], axis=0)
        x_mid = jnp.concatenate([az_ref[k:, at], zhm_ref[2 * k :, at]], axis=0)
        new = lax.dot_general(
            lhs, jnp.concatenate([x_hi, x_mid, x_hi], axis=0), NN, preferred_element_type=F32
        )
        for i in range(block // r):
            out_ref[b * (block // r) + i] = new[:, i * r : (i + 1) * r]
        return carry

    lax.fori_loop(0, ch * r // block, result, 0, unroll=True)


def gather_sums(x):
    n_chan, n_rad = lax.axis_size("chan"), lax.axis_size("rad")
    step = 1
    while step < n_rad:
        x = x + swap(x, "rad", step)
        step *= 2
    every = jnp.broadcast_to(x, (n_chan,) + x.shape)
    return lax.all_to_all(every, "chan", split_axis=0, concat_axis=0, tiled=True)


def body(trial_block, ham_blocks, partners, stored_at, precond_diag):
    n_chan, n_rad = lax.axis_size("chan"), lax.axis_size("rad")
    ch, k, r = trial_block.shape
    ncoup, splines = ham_blocks.shape[1], ham_blocks.shape[3]
    lanes = ch * r
    total = float(n_chan * n_rad * lanes)
    share, nz = ch // n_rad, n_chan // 4

    barrier = lax.optimization_barrier
    smem = pl.BlockSpec(memory_space=pltpu.SMEM)
    any_ = pl.BlockSpec(memory_space=pl.ANY)
    whole = pl.BlockSpec(memory_space=pltpu.VMEM)

    def near_of(x):
        return plane_swap(x, (1, 2))

    def far_of(x):
        return plane_swap(x, (2, 1))

    def flat(x):
        return x.reshape((-1,) + x.shape[2:])

    def in_cores(x):
        return [x] + [swap(x, "rad", c) for c in range(1, n_rad)]

    own = jnp.concatenate(jnp.split(trial_block.astype(BF16), n_rad), axis=2)[None]
    near0, far_own, diag0 = near_of(own), far_of(own), swap(own, "chan", 3)
    z1 = swap(own, "chan", 4)
    z_even = jnp.concatenate([swap(own, "chan", 4 * z) for z in range(2, nz, 2)])
    rows, ham, zhm, zl, dc, gram_t = pl.pallas_call(
        functools.partial(prepare_kernel, n_chan, n_rad),
        in_specs=[any_] * 5,
        out_specs=[whole] * 6,
        out_shape=[
            jax.ShapeDtypeStruct((ncoup, ch), jnp.int32),
            pltpu.VMEM(ham_blocks.shape, BF16),
            pltpu.VMEM((4 * k, lanes), BF16),
            pltpu.VMEM((2 * k, lanes), BF16),
            pltpu.VMEM((1, lanes), F32),
            pltpu.VMEM((k, 3 * k), F32),
        ],
        scratch_shapes=[
            pltpu.VMEM(trial_block.shape, F32),
            pltpu.VMEM(precond_diag.shape, F32),
            pltpu.VMEM((ncoup, ch), jnp.int32),
            pltpu.VMEM((stored_at.shape[0] // 128, 128), jnp.int32),
            pltpu.SemaphoreType.DMA((5,)),
        ],
        compiler_params=pltpu.CompilerParams(vmem_limit_bytes=VMEM_LIMIT),
        name="prepare",
    )(
        in_hbm(trial_block),
        in_hbm(precond_diag),
        in_hbm(partners.T),
        in_hbm(stored_at.reshape(-1, 128)),
        in_hbm(ham_blocks),
    )
    far_own, near0, z1, z_even, diag0, rows = barrier((far_own, near0, z1, z_even, diag0, rows))
    some, z_even, diag0 = barrier((jnp.concatenate([z1, z_even]), z_even, diag0))
    near1, far1 = near_of(some), far_of(some)
    z_odd = swap(z_even, "chan", 4)
    z_odd, far1, near1, diag0 = barrier((z_odd, far1, near1, diag0))
    early = in_cores(
        jnp.concatenate([own, z1, z_even, near0, far_own, diag0, near1, z_odd, far1])
    )
    near_odd = near_of(z_odd)
    diag_odd = jnp.concatenate([swap(diag0, "chan", 4 * z) for z in range(3, nz, 2)])
    far2 = far_of(jnp.concatenate([z_odd, near1]))
    table = pl.pallas_call(
        functools.partial(assemble_kernel, nz, share),
        in_specs=[whole] * n_rad,
        out_specs=whole,
        out_shape=pltpu.VMEM((n_chan * ch, k, splines), BF16),
        compiler_params=pltpu.CompilerParams(vmem_limit_bytes=VMEM_LIMIT),
        name="assemble",
    )(*[in_vmem(flat(x)) for x in early])
    near_odd, diag_odd, far2, table = barrier((near_odd, diag_odd, far2, table))
    last = [in_vmem(flat(x)) for x in in_cores(jnp.concatenate([near_odd, far2, diag_odd]))]

    az, sums, _ = pl.pallas_call(
        functools.partial(apply_kernel, nz, share),
        in_specs=[smem] + [whole] * (6 + n_rad),
        out_specs=[whole, whole, whole],
        out_shape=[
            pltpu.VMEM((2 * k, lanes), BF16),
            jax.ShapeDtypeStruct((k, 8 * k), F32),
            pltpu.VMEM(table.shape, BF16),
        ],
        input_output_aliases={2: 2},
        scratch_shapes=[pltpu.VMEM((k, lanes), F32)],
        compiler_params=pltpu.CompilerParams(vmem_limit_bytes=VMEM_LIMIT),
        name="apply",
    )(rows, in_vmem(ham), in_vmem(table), in_vmem(zhm), in_vmem(zl), in_vmem(dc), gram_t, *last)

    sums = gather_sums(sums)
    new_block, ritz = pl.pallas_call(
        functools.partial(finish_kernel, total),
        out_shape=[
            jax.ShapeDtypeStruct((ch, k, r), F32),
            jax.ShapeDtypeStruct((1, k), F32),
        ],
        compiler_params=pltpu.CompilerParams(vmem_limit_bytes=VMEM_LIMIT),
        name="finish",
    )(sums, in_vmem(az), in_vmem(zhm))
    return (new_block, ritz.reshape(k))


def solution(mesh):
    return jax.shard_map(
        body,
        mesh=mesh,
        in_specs=(
            P("chan", None, "rad"),
            P("chan", None, "rad", None),
            P("chan", None),
            P(),
            P("chan", "rad"),
        ),
        out_specs=(P("chan", None, "rad"), P()),
        check_vma=False,
    )
```

```python
import functools

import jax
import jax.numpy as jnp
from jax import lax
from jax.experimental import pallas as pl
from jax.experimental.pallas import tpu as pltpu
from jax.sharding import PartitionSpec as P

SCALE = 2.0 ** -8
F32 = jnp.float32
BF16 = jnp.bfloat16
NT = (((1,), (1,)), ((), ()))
TN = (((0,), (0,)), ((), ()))
NN = (((1,), (0,)), ((), ()))
VMEM_LIMIT = 4 * 1024 * 1024


def swap(x, axis, distance):
    n = lax.axis_size(axis)
    return lax.ppermute(x, axis, [(i, i ^ distance) for i in range(n)])


def plane_swap(x, order):
    n_chan, n_rad = lax.axis_size("chan"), lax.axis_size("rad")
    pairs = []
    for c in range(n_chan):
        for r in range(n_rad):
            pairs.append((c * n_rad + r, (c ^ order[r % 2]) * n_rad + r))
    return lax.ppermute(x, ("chan", "rad"), pairs)


def table_piece(z, part, nz):
    some, odd = nz // 2, nz // 2 - 1
    is_odd = (z & 1 == 1) & (z > 1)
    i = jnp.where(is_odd, (z - 3) >> 1, jnp.where(z == 1, 0, z >> 1))
    base = 2 * some + odd + 4

    def pick(own, of_some, of_odd):
        return jnp.where(z == 0, own, jnp.where(is_odd, of_odd + i, of_some + i))

    here = pick(0, 1, 2 * some + 4)
    near = pick(some + 1, some + 4, base + some)
    far = pick(some + 2, base, base + some + odd)
    both = pick(some + 3, base + some + 2 * odd, base + 2 * some + 2 * odd)
    return jnp.where(part == 0, here, jnp.where(part == 1, near, jnp.where(part == 2, far, both)))


def early_pieces(nz):
    some, odd = [1] + list(range(2, nz, 2)), list(range(3, nz, 2))
    order = [(0, 0)] + [(z, 0) for z in some] + [(0, 1), (0, 2), (0, 3)] + [(z, 1) for z in some]
    return order + [(z, 0) for z in odd] + [(z, 2) for z in some]


def late_pieces(nz):
    some, odd = [1] + list(range(2, nz, 2)), list(range(3, nz, 2))
    return [(z, 1) for z in odd] + [(z, 2) for z in odd] + [(z, 3) for z in some + odd]


def merge(refs, table_ref, order, start, share, unroll):
    n_rad = len(refs)
    r = 128 // n_rad
    me = lax.axis_index("rad")

    def rows(n, carry):
        for i, (z, part) in enumerate(order):
            other = order.index((z, (0, 2, 1, 3)[part]))
            tiles = [ref[(other if s % 2 else i) * share + n] for s, ref in enumerate(refs)]
            by_core = []
            for c in range(n_rad):
                x = tiles[0]
                for s in range(1, n_rad):
                    x = jnp.where((me ^ s) == c, tiles[s], x)
                by_core.append(x)
            for g in range(n_rad):
                row = jnp.concatenate([x[:, g * r : (g + 1) * r] for x in by_core], axis=1)
                table_ref[((start + i) * n_rad + g) * share + n] = row
        return carry

    lax.fori_loop(0, share, rows, 0, unroll=min(unroll, share))


def in_vmem(x):
    return pltpu.with_memory_space_constraint(x, pltpu.VMEM)


def in_hbm(x):
    return pltpu.with_memory_space_constraint(x, pltpu.HBM)


def split3(x):
    hi = x.astype(BF16)
    rest = x - hi.astype(F32)
    mid = rest.astype(BF16)
    return hi, mid, (rest - mid.astype(F32)).astype(BF16)


def dot32(x, y, dims=NN):
    return lax.dot_general(x, y, dims, precision=lax.Precision.HIGHEST, preferred_element_type=F32)


def block_sum(g, rows, cols):
    g = sum(g[i : i + rows] for i in range(0, g.shape[0], rows))
    return sum(g[:, i : i + cols] for i in range(0, g.shape[1], cols))


def prepare_kernel(
    n_chan, n_rad, t_hbm, d_hbm, partners_hbm, stored_hbm, ham_hbm,
    rows_ref, ham_ref, zhm_ref, zl_ref, dc_ref, gram_ref, t_ref, d_ref, partners_ref, stored_ref, sems,
):
    moves = (
        (t_hbm, t_ref), (d_hbm, d_ref), (partners_hbm, partners_ref), (stored_hbm, stored_ref), (ham_hbm, ham_ref)
    )
    copies = [pltpu.make_async_copy(x, y, sems.at[i]) for i, (x, y) in enumerate(moves)]
    for copy in copies:
        copy.start()
    for copy in copies[:4]:
        copy.wait()
    ch, k, r = t_ref.shape
    group = 128 // r
    for i in range(ch // group):
        lanes = pl.ds(i * 128, 128)
        t = jnp.concatenate([t_ref[i * group + g] for g in range(group)], axis=1)
        d = jnp.concatenate([d_ref[pl.ds(i * group + g, 1), :] for g in range(group)], axis=1)
        dc_ref[:, lanes] = d
        hi, mid, lo = split3(jnp.concatenate([t / d, t], axis=0))
        zhm_ref[:, lanes] = jnp.concatenate([hi, mid], axis=0)
        zl_ref[:, lanes] = lo
    z = jnp.concatenate([zhm_ref[...], zl_ref[...]], axis=0)
    g = block_sum(lax.dot_general(z, z, NT, preferred_element_type=F32), 2 * k, 2 * k)
    gram_ref[...] = jnp.concatenate([g[k:, :], g[:k, :k]], axis=1)

    share, nz = ch // n_rad, n_chan // 4
    q = stored_ref[...]
    owner, local = lax.div(q, ch), lax.rem(q, ch)
    apart = (owner ^ lax.axis_index("chan")) & 3
    turned = ((apart & 1) << 1) | (apart >> 1)
    part = jnp.where((lax.axis_index("rad") & 1) == 1, turned, apart)
    piece = table_piece((owner ^ lax.axis_index("chan")) >> 2, part, nz)
    place = (piece * ch + local).astype(F32)
    lane = lax.broadcasted_iota(jnp.int32, (ch, 128), 1)
    columns = []
    partners = partners_ref[...].astype(F32).T.astype(jnp.int32)
    for j in range(partners.shape[1]):
        wanted = jnp.broadcast_to(partners[:, j : j + 1], (ch, 128)) - lane
        found = jnp.zeros((ch, 128), F32)
        for c in range(place.shape[0]):
            found = found + jnp.where(wanted == 128 * c, place[c : c + 1], 0.0)
        columns.append(jnp.sum(found, axis=1, keepdims=True))
    rows_ref[...] = jnp.concatenate(columns, axis=1).T.astype(jnp.int32)
    copies[4].wait()


def assemble_kernel(nz, share, *refs):
    merge(refs[:-1], refs[-1], early_pieces(nz), 0, share, 8)


def apply_kernel(nz, share, rows_ref, ham_ref, _, zhm_ref, zl_ref, dc_ref, gt_ref, *rest):
    last, (az_ref, sums_ref, table_ref, a0_ref) = rest[:-4], rest[-4:]
    merge(last, table_ref, late_pieces(nz), len(early_pieces(nz)), share, 32)
    ch, ncoup, r, splines = ham_ref.shape
    k = zl_ref.shape[0] // 2
    group = 256 // r

    def work(g, carry):
        left, right = [], []
        for i in range(group):
            p = g * group + i
            left.append(
                jnp.concatenate([table_ref[rows_ref[j, p]] for j in range(ncoup)], axis=1)
            )
            right.append(jnp.concatenate([ham_ref[p, j] for j in range(ncoup)], axis=1))
        product = lax.dot_general(
            jnp.concatenate(left, axis=0),
            jnp.concatenate(right, axis=0),
            NT,
            preferred_element_type=F32,
        )
        own = [product[i * k : (i + 1) * k, i * r : (i + 1) * r] for i in range(group)]
        a0_ref[:, pl.ds(pl.multiple_of(g * 256, 256), 256)] = jnp.concatenate(own, axis=1) * SCALE
        return carry

    lax.fori_loop(0, ch // group, work, 0, unroll=True)

    lanes = ch * r
    block = min(lanes, 1024)

    def gram_block(i, gram):
        at = pl.ds(pl.multiple_of(i * block, block), block)
        a0 = a0_ref[:, at]
        a1_terms = split3(a0 / dc_ref[:, at])
        az_ref[:, at] = jnp.concatenate(a1_terms[:2], axis=0)
        right = jnp.concatenate(a1_terms + split3(a0), axis=0)
        left = jnp.concatenate([zhm_ref[:, at], zl_ref[:, at], right[: 3 * k]], axis=0)
        return gram + lax.dot_general(left, right, NT, preferred_element_type=F32)

    gram = lax.fori_loop(
        0, lanes // block, gram_block, jnp.zeros((9 * k, 6 * k), F32), unroll=True
    )
    ta1 = block_sum(gram[: 6 * k, : 3 * k], 2 * k, k)
    ta0 = block_sum(gram[: 6 * k, 3 * k :], 2 * k, k)
    aa = block_sum(gram[6 * k :, : 3 * k], k, k)
    gt = gt_ref[...]
    parts = [ta1[k:], gt[:, : 2 * k], ta0[k:], ta1[:k], gt[:, 2 * k :], aa, jnp.zeros((k, k), F32)]
    sums_ref[...] = jnp.concatenate(parts, axis=1)


def spread(x, i):
    return jnp.broadcast_to(x[:, i : i + 1], (x.shape[0], 128))


def finish_kernel(total, sums_ref, az_ref, zhm_ref, out_ref, ritz_ref):
    ch, k, r = out_ref.shape
    s = jnp.sum(sums_ref[...], axis=0)
    row = lax.broadcasted_iota(jnp.int32, (k, 128), 0)
    cols = [spread(s, 2 * k + i) for i in range(k)]
    x = s
    for i in range(k):
        scale = 1.0 / cols[i][i : i + 1]
        pivot = x[i : i + 1] * scale
        x = jnp.where(row == i, pivot, x - cols[i] * pivot)
        for j in range(i + 1, k):
            part = cols[j][i : i + 1] * scale
            cols[j] = jnp.where(row == i, part, cols[j] - cols[i] * part)
    coef = x[:, 3 * k : 4 * k]
    eye = lax.broadcasted_iota(jnp.int32, (k, k), 0) == lax.broadcasted_iota(jnp.int32, (k, k), 1)
    ritz_ref[...] = jnp.sum(jnp.where(eye, coef, 0.0), axis=0, keepdims=True) * (1.0 / SCALE)
    s1, b1 = s[:, :k], s[:, k : 2 * k]
    s2, b2, aa = s[:, 4 * k : 5 * k], s[:, 5 * k : 6 * k], s[:, 6 * k : 7 * k]
    known = jnp.concatenate([x[:, :k], s1, s2], axis=0)
    known = known - dot32(jnp.concatenate([x[:, k : 2 * k], b1, b2], axis=0), coef)
    mix, corr, weighted = known[:k], known[k : 2 * k], known[2 * k :]
    left = split3(jnp.concatenate([s2, coef, corr], axis=0))
    right = split3(jnp.concatenate([coef, weighted, mix], axis=0))
    pairs = ((0, 0), (0, 1), (1, 0), (1, 1), (0, 2), (2, 0))
    gram = aa - lax.dot_general(
        jnp.concatenate([left[i] for i, _ in pairs], axis=0),
        jnp.concatenate([right[j] for _, j in pairs], axis=0),
        TN,
        preferred_element_type=F32,
    )
    cols = [spread(gram, i) for i in range(k)]
    pad = jnp.zeros((k, 128 - 3 * k), F32)
    x = jnp.concatenate([eye.astype(F32), -coef.T, -mix.T, pad], axis=1)
    for i in range(k):
        pivot = cols[i][i : i + 1]
        scale = 1.0 / pivot
        below = jnp.where(row > i, cols[i] * scale, 0.0)
        pivot_row = x[i : i + 1]
        x = jnp.where(row == i, pivot_row * (lax.rsqrt(pivot) * (total ** 0.5)), x - below * pivot_row)
        for j in range(i + 1, k):
            cols[j] = cols[j] - below * cols[j][i : i + 1]
    hi, mid, _ = split3(x[:, : 3 * k])
    lhs = jnp.concatenate([hi, hi, mid], axis=1)
    block = min(ch * r, 1024)

    def result(b, carry):
        at = pl.ds(pl.multiple_of(b * block, block), block)
        x_hi = jnp.concatenate([az_ref[:k, at], zhm_ref[: 2 * k, at]], axis=0)
        x_mid = jnp.concatenate([az_ref[k:, at], zhm_ref[2 * k :, at]], axis=0)
        new = lax.dot_general(
            lhs, jnp.concatenate([x_hi, x_mid, x_hi], axis=0), NN, preferred_element_type=F32
        )
        for i in range(block // r):
            out_ref[b * (block // r) + i] = new[:, i * r : (i + 1) * r]
        return carry

    lax.fori_loop(0, ch * r // block, result, 0, unroll=True)


def gather_sums(x):
    n_chan, n_rad = lax.axis_size("chan"), lax.axis_size("rad")
    step = 1
    while step < n_rad:
        x = x + swap(x, "rad", step)
        step *= 2
    every = jnp.broadcast_to(x, (n_chan,) + x.shape)
    return lax.all_to_all(every, "chan", split_axis=0, concat_axis=0, tiled=True)


def body(trial_block, ham_blocks, partners, stored_at, precond_diag):
    n_chan, n_rad = lax.axis_size("chan"), lax.axis_size("rad")
    ch, k, r = trial_block.shape
    ncoup, splines = ham_blocks.shape[1], ham_blocks.shape[3]
    lanes = ch * r
    total = float(n_chan * n_rad * lanes)
    share, nz = ch // n_rad, n_chan // 4

    barrier = lax.optimization_barrier
    smem = pl.BlockSpec(memory_space=pltpu.SMEM)
    any_ = pl.BlockSpec(memory_space=pl.ANY)
    whole = pl.BlockSpec(memory_space=pltpu.VMEM)

    def near_of(x):
        return plane_swap(x, (1, 2))

    def far_of(x):
        return plane_swap(x, (2, 1))

    def flat(x):
        return x.reshape((-1,) + x.shape[2:])

    def in_cores(x):
        return [x] + [swap(x, "rad", c) for c in range(1, n_rad)]

    own = jnp.concatenate(jnp.split(trial_block.astype(BF16), n_rad), axis=2)[None]
    near0, far_own, diag0 = near_of(own), far_of(own), swap(own, "chan", 3)
    z1 = swap(own, "chan", 4)
    z_even = jnp.concatenate([swap(own, "chan", 4 * z) for z in range(2, nz, 2)])
    rows, ham, zhm, zl, dc, gram_t = pl.pallas_call(
        functools.partial(prepare_kernel, n_chan, n_rad),
        in_specs=[any_] * 5,
        out_specs=[whole] * 6,
        out_shape=[
            jax.ShapeDtypeStruct((ncoup, ch), jnp.int32),
            pltpu.VMEM(ham_blocks.shape, BF16),
            pltpu.VMEM((4 * k, lanes), BF16),
            pltpu.VMEM((2 * k, lanes), BF16),
            pltpu.VMEM((1, lanes), F32),
            pltpu.VMEM((k, 3 * k), F32),
        ],
        scratch_shapes=[
            pltpu.VMEM(trial_block.shape, F32),
            pltpu.VMEM(precond_diag.shape, F32),
            pltpu.VMEM((ncoup, ch), jnp.int32),
            pltpu.VMEM((stored_at.shape[0] // 128, 128), jnp.int32),
            pltpu.SemaphoreType.DMA((5,)),
        ],
        compiler_params=pltpu.CompilerParams(vmem_limit_bytes=VMEM_LIMIT),
        name="prepare",
    )(
        in_hbm(trial_block),
        in_hbm(precond_diag),
        in_hbm(partners.T),
        in_hbm(stored_at.reshape(-1, 128)),
        in_hbm(ham_blocks),
    )
    far_own, near0, z1, z_even, diag0, rows = barrier((far_own, near0, z1, z_even, diag0, rows))
    some, z_even, diag0 = barrier((jnp.concatenate([z1, z_even]), z_even, diag0))
    near1, far1 = near_of(some), far_of(some)
    z_odd = swap(z_even, "chan", 4)
    z_odd, far1, near1, diag0 = barrier((z_odd, far1, near1, diag0))
    early = in_cores(
        jnp.concatenate([own, z1, z_even, near0, far_own, diag0, near1, z_odd, far1])
    )
    near_odd = near_of(z_odd)
    diag_odd = jnp.concatenate([swap(diag0, "chan", 4 * z) for z in range(3, nz, 2)])
    far2 = far_of(jnp.concatenate([z_odd, near1]))
    table = pl.pallas_call(
        functools.partial(assemble_kernel, nz, share),
        in_specs=[whole] * n_rad,
        out_specs=whole,
        out_shape=pltpu.VMEM((n_chan * ch, k, splines), BF16),
        compiler_params=pltpu.CompilerParams(vmem_limit_bytes=VMEM_LIMIT),
        name="assemble",
    )(*[in_vmem(flat(x)) for x in early])
    near_odd, diag_odd, far2, table = barrier((near_odd, diag_odd, far2, table))
    last = [in_vmem(flat(x)) for x in in_cores(jnp.concatenate([near_odd, far2, diag_odd]))]

    az, sums, _ = pl.pallas_call(
        functools.partial(apply_kernel, nz, share),
        in_specs=[smem] + [whole] * (6 + n_rad),
        out_specs=[whole, whole, whole],
        out_shape=[
            pltpu.VMEM((2 * k, lanes), BF16),
            jax.ShapeDtypeStruct((k, 8 * k), F32),
            pltpu.VMEM(table.shape, BF16),
        ],
        input_output_aliases={2: 2},
        scratch_shapes=[pltpu.VMEM((k, lanes), F32)],
        compiler_params=pltpu.CompilerParams(vmem_limit_bytes=VMEM_LIMIT),
        name="apply",
    )(rows, in_vmem(ham), in_vmem(table), in_vmem(zhm), in_vmem(zl), in_vmem(dc), gram_t, *last)

    sums = gather_sums(sums)
    new_block, ritz = pl.pallas_call(
        functools.partial(finish_kernel, total),
        out_shape=[
            jax.ShapeDtypeStruct((ch, k, r), F32),
            jax.ShapeDtypeStruct((1, k), F32),
        ],
        compiler_params=pltpu.CompilerParams(vmem_limit_bytes=VMEM_LIMIT),
        name="finish",
    )(sums, in_vmem(az), in_vmem(zhm))
    return (new_block, ritz.reshape(k))


def solution(mesh):
    return jax.shard_map(
        body,
        mesh=mesh,
        in_specs=(
            P("chan", None, "rad"),
            P("chan", None, "rad", None),
            P("chan", None),
            P(),
            P("chan", "rad"),
        ),
        out_specs=(P("chan", None, "rad"), P()),
        check_vma=False,
    )
```

```python
import functools

import jax
import jax.numpy as jnp
from jax import lax
from jax.experimental import pallas as pl
from jax.experimental.pallas import tpu as pltpu
from jax.sharding import PartitionSpec as P

SCALE = 2.0 ** -8
F32 = jnp.float32
BF16 = jnp.bfloat16
NT = (((1,), (1,)), ((), ()))
TN = (((0,), (0,)), ((), ()))
NN = (((1,), (0,)), ((), ()))
VMEM_LIMIT = 4 * 1024 * 1024


def swap(x, axis, distance):
    n = lax.axis_size(axis)
    return lax.ppermute(x, axis, [(i, i ^ distance) for i in range(n)])


def plane_swap(x, order):
    n_chan, n_rad = lax.axis_size("chan"), lax.axis_size("rad")
    pairs = []
    for c in range(n_chan):
        for r in range(n_rad):
            pairs.append((c * n_rad + r, (c ^ order[r % 2]) * n_rad + r))
    return lax.ppermute(x, ("chan", "rad"), pairs)


def table_piece(z, part, nz):
    some, odd = nz // 2, nz // 2 - 1
    is_odd = (z & 1 == 1) & (z > 1)
    i = jnp.where(is_odd, (z - 3) >> 1, jnp.where(z == 1, 0, z >> 1))
    base = 2 * some + odd + 4

    def pick(own, of_some, of_odd):
        return jnp.where(z == 0, own, jnp.where(is_odd, of_odd + i, of_some + i))

    here = pick(0, 1, 2 * some + 4)
    near = pick(some + 1, some + 4, base + some)
    far = pick(some + 2, base, base + some + odd)
    both = pick(some + 3, base + some + 2 * odd, base + 2 * some + 2 * odd)
    return jnp.where(part == 0, here, jnp.where(part == 1, near, jnp.where(part == 2, far, both)))


def early_pieces(nz):
    some, odd = [1] + list(range(2, nz, 2)), list(range(3, nz, 2))
    order = [(0, 0)] + [(z, 0) for z in some] + [(0, 1), (0, 2), (0, 3)] + [(z, 1) for z in some]
    return order + [(z, 0) for z in odd] + [(z, 2) for z in some]


def late_pieces(nz):
    some, odd = [1] + list(range(2, nz, 2)), list(range(3, nz, 2))
    return [(z, 1) for z in odd] + [(z, 2) for z in odd] + [(z, 3) for z in some + odd]


def merge(refs, table_ref, order, start, share, unroll):
    n_rad = len(refs)
    r = 128 // n_rad
    me = lax.axis_index("rad")

    def rows(n, carry):
        for i, (z, part) in enumerate(order):
            other = order.index((z, (0, 2, 1, 3)[part]))
            tiles = [ref[(other if s % 2 else i) * share + n] for s, ref in enumerate(refs)]
            by_core = []
            for c in range(n_rad):
                x = tiles[0]
                for s in range(1, n_rad):
                    x = jnp.where((me ^ s) == c, tiles[s], x)
                by_core.append(x)
            for g in range(n_rad):
                row = jnp.concatenate([x[:, g * r : (g + 1) * r] for x in by_core], axis=1)
                table_ref[((start + i) * n_rad + g) * share + n] = row
        return carry

    lax.fori_loop(0, share, rows, 0, unroll=min(unroll, share))


def in_vmem(x):
    return pltpu.with_memory_space_constraint(x, pltpu.VMEM)


def in_hbm(x):
    return pltpu.with_memory_space_constraint(x, pltpu.HBM)


def split3(x):
    hi = x.astype(BF16)
    rest = x - hi.astype(F32)
    mid = rest.astype(BF16)
    return hi, mid, (rest - mid.astype(F32)).astype(BF16)


def dot32(x, y, dims=NN):
    return lax.dot_general(x, y, dims, precision=lax.Precision.HIGHEST, preferred_element_type=F32)


def block_sum(g, rows, cols):
    g = sum(g[i : i + rows] for i in range(0, g.shape[0], rows))
    return sum(g[:, i : i + cols] for i in range(0, g.shape[1], cols))


def prepare_kernel(
    n_chan, n_rad, t_hbm, d_hbm, partners_hbm, stored_hbm, ham_hbm,
    rows_ref, ham_ref, zhm_ref, zl_ref, dc_ref, gram_ref, t_ref, d_ref, partners_ref, stored_ref, sems,
):
    moves = (
        (t_hbm, t_ref), (d_hbm, d_ref), (partners_hbm, partners_ref), (stored_hbm, stored_ref), (ham_hbm, ham_ref)
    )
    copies = [pltpu.make_async_copy(x, y, sems.at[i]) for i, (x, y) in enumerate(moves)]
    for copy in copies:
        copy.start()
    for copy in copies[:4]:
        copy.wait()
    ch, k, r = t_ref.shape
    group = 128 // r
    for i in range(ch // group):
        lanes = pl.ds(i * 128, 128)
        t = jnp.concatenate([t_ref[i * group + g] for g in range(group)], axis=1)
        d = jnp.concatenate([d_ref[pl.ds(i * group + g, 1), :] for g in range(group)], axis=1)
        dc_ref[:, lanes] = d
        hi, mid, lo = split3(jnp.concatenate([t / d, t], axis=0))
        zhm_ref[:, lanes] = jnp.concatenate([hi, mid], axis=0)
        zl_ref[:, lanes] = lo
    z = jnp.concatenate([zhm_ref[...], zl_ref[...]], axis=0)
    g = block_sum(lax.dot_general(z, z, NT, preferred_element_type=F32), 2 * k, 2 * k)
    gram_ref[...] = jnp.concatenate([g[k:, :], g[:k, :k]], axis=1)

    share, nz = ch // n_rad, n_chan // 4
    q = stored_ref[...]
    owner, local = lax.div(q, ch), lax.rem(q, ch)
    apart = (owner ^ lax.axis_index("chan")) & 3
    turned = ((apart & 1) << 1) | (apart >> 1)
    part = jnp.where((lax.axis_index("rad") & 1) == 1, turned, apart)
    piece = table_piece((owner ^ lax.axis_index("chan")) >> 2, part, nz)
    place = (piece * ch + local).astype(F32)
    lane = lax.broadcasted_iota(jnp.int32, (ch, 128), 1)
    columns = []
    partners = partners_ref[...].astype(F32).T.astype(jnp.int32)
    for j in range(partners.shape[1]):
        wanted = jnp.broadcast_to(partners[:, j : j + 1], (ch, 128)) - lane
        found = jnp.zeros((ch, 128), F32)
        for c in range(place.shape[0]):
            found = found + jnp.where(wanted == 128 * c, place[c : c + 1], 0.0)
        columns.append(jnp.sum(found, axis=1, keepdims=True))
    rows_ref[...] = jnp.concatenate(columns, axis=1).T.astype(jnp.int32)
    copies[4].wait()


def assemble_kernel(nz, share, *refs):
    merge(refs[:-1], refs[-1], early_pieces(nz), 0, share, 8)


def apply_kernel(nz, share, rows_ref, ham_ref, _, zhm_ref, zl_ref, dc_ref, gt_ref, *rest):
    last, (az_ref, sums_ref, table_ref, a0_ref) = rest[:-4], rest[-4:]
    merge(last, table_ref, late_pieces(nz), len(early_pieces(nz)), share, 32)
    ch, ncoup, r, splines = ham_ref.shape
    k = zl_ref.shape[0] // 2
    group = 256 // r

    def work(g, carry):
        left, right = [], []
        for i in range(group):
            p = g * group + i
            left.append(
                jnp.concatenate([table_ref[rows_ref[j, p]] for j in range(ncoup)], axis=1)
            )
            right.append(jnp.concatenate([ham_ref[p, j] for j in range(ncoup)], axis=1))
        product = lax.dot_general(
            jnp.concatenate(left, axis=0),
            jnp.concatenate(right, axis=0),
            NT,
            preferred_element_type=F32,
        )
        own = [product[i * k : (i + 1) * k, i * r : (i + 1) * r] for i in range(group)]
        a0_ref[:, pl.ds(pl.multiple_of(g * 256, 256), 256)] = jnp.concatenate(own, axis=1) * SCALE
        return carry

    lax.fori_loop(0, ch // group, work, 0, unroll=True)

    lanes = ch * r
    block = min(lanes, 1024)

    def gram_block(i, gram):
        at = pl.ds(pl.multiple_of(i * block, block), block)
        a0 = a0_ref[:, at]
        a1_terms = split3(a0 / dc_ref[:, at])
        az_ref[:, at] = jnp.concatenate(a1_terms[:2], axis=0)
        right = jnp.concatenate(a1_terms + split3(a0), axis=0)
        left = jnp.concatenate([zhm_ref[:, at], zl_ref[:, at], right[: 3 * k]], axis=0)
        return gram + lax.dot_general(left, right, NT, preferred_element_type=F32)

    gram = lax.fori_loop(
        0, lanes // block, gram_block, jnp.zeros((9 * k, 6 * k), F32), unroll=True
    )
    ta1 = block_sum(gram[: 6 * k, : 3 * k], 2 * k, k)
    ta0 = block_sum(gram[: 6 * k, 3 * k :], 2 * k, k)
    aa = block_sum(gram[6 * k :, : 3 * k], k, k)
    gt = gt_ref[...]
    parts = [ta1[k:], gt[:, : 2 * k], ta0[k:], ta1[:k], gt[:, 2 * k :], aa, jnp.zeros((k, k), F32)]
    sums_ref[...] = jnp.concatenate(parts, axis=1)


def spread(x, i):
    return jnp.broadcast_to(x[:, i : i + 1], (x.shape[0], 128))


def finish_kernel(total, sums_ref, az_ref, zhm_ref, out_ref, ritz_ref):
    ch, k, r = out_ref.shape
    s = jnp.sum(sums_ref[...], axis=0)
    row = lax.broadcasted_iota(jnp.int32, (k, 128), 0)
    cols = [spread(s, 2 * k + i) for i in range(k)]
    x = s
    for i in range(k):
        scale = 1.0 / cols[i][i : i + 1]
        pivot = x[i : i + 1] * scale
        x = jnp.where(row == i, pivot, x - cols[i] * pivot)
        for j in range(i + 1, k):
            part = cols[j][i : i + 1] * scale
            cols[j] = jnp.where(row == i, part, cols[j] - cols[i] * part)
    coef = x[:, 3 * k : 4 * k]
    eye = lax.broadcasted_iota(jnp.int32, (k, k), 0) == lax.broadcasted_iota(jnp.int32, (k, k), 1)
    ritz_ref[...] = jnp.sum(jnp.where(eye, coef, 0.0), axis=0, keepdims=True) * (1.0 / SCALE)
    s1, b1 = s[:, :k], s[:, k : 2 * k]
    s2, b2, aa = s[:, 4 * k : 5 * k], s[:, 5 * k : 6 * k], s[:, 6 * k : 7 * k]
    known = jnp.concatenate([x[:, :k], s1, s2], axis=0)
    known = known - dot32(jnp.concatenate([x[:, k : 2 * k], b1, b2], axis=0), coef)
    mix, corr, weighted = known[:k], known[k : 2 * k], known[2 * k :]
    left = split3(jnp.concatenate([s2, coef, corr], axis=0))
    right = split3(jnp.concatenate([coef, weighted, mix], axis=0))
    pairs = ((0, 0), (0, 1), (1, 0), (1, 1), (0, 2), (2, 0))
    gram = aa - lax.dot_general(
        jnp.concatenate([left[i] for i, _ in pairs], axis=0),
        jnp.concatenate([right[j] for _, j in pairs], axis=0),
        TN,
        preferred_element_type=F32,
    )
    cols = [spread(gram, i) for i in range(k)]
    pad = jnp.zeros((k, 128 - 3 * k), F32)
    x = jnp.concatenate([eye.astype(F32), -coef.T, -mix.T, pad], axis=1)
    for i in range(k):
        pivot = cols[i][i : i + 1]
        scale = 1.0 / pivot
        below = jnp.where(row > i, cols[i] * scale, 0.0)
        pivot_row = x[i : i + 1]
        x = jnp.where(row == i, pivot_row * (lax.rsqrt(pivot) * (total ** 0.5)), x - below * pivot_row)
        for j in range(i + 1, k):
            cols[j] = cols[j] - below * cols[j][i : i + 1]
    hi, mid, _ = split3(x[:, : 3 * k])
    lhs = jnp.concatenate([hi, hi, mid], axis=1)
    block = min(ch * r, 1024)

    def result(b, carry):
        at = pl.ds(pl.multiple_of(b * block, block), block)
        x_hi = jnp.concatenate([az_ref[:k, at], zhm_ref[: 2 * k, at]], axis=0)
        x_mid = jnp.concatenate([az_ref[k:, at], zhm_ref[2 * k :, at]], axis=0)
        new = lax.dot_general(
            lhs, jnp.concatenate([x_hi, x_mid, x_hi], axis=0), NN, preferred_element_type=F32
        )
        for i in range(block // r):
            out_ref[b * (block // r) + i] = new[:, i * r : (i + 1) * r]
        return carry

    lax.fori_loop(0, ch * r // block, result, 0, unroll=True)


def gather_sums(x):
    n_chan, n_rad = lax.axis_size("chan"), lax.axis_size("rad")
    step = 1
    while step < n_rad:
        x = x + swap(x, "rad", step)
        step *= 2
    every = jnp.broadcast_to(x, (n_chan,) + x.shape)
    return lax.all_to_all(every, "chan", split_axis=0, concat_axis=0, tiled=True)


def body(trial_block, ham_blocks, partners, stored_at, precond_diag):
    n_chan, n_rad = lax.axis_size("chan"), lax.axis_size("rad")
    ch, k, r = trial_block.shape
    ncoup, splines = ham_blocks.shape[1], ham_blocks.shape[3]
    lanes = ch * r
    total = float(n_chan * n_rad * lanes)
    share, nz = ch // n_rad, n_chan // 4

    barrier = lax.optimization_barrier
    smem = pl.BlockSpec(memory_space=pltpu.SMEM)
    any_ = pl.BlockSpec(memory_space=pl.ANY)
    whole = pl.BlockSpec(memory_space=pltpu.VMEM)

    def near_of(x):
        return plane_swap(x, (1, 2))

    def far_of(x):
        return plane_swap(x, (2, 1))

    def flat(x):
        return x.reshape((-1,) + x.shape[2:])

    def in_cores(x):
        return [x] + [swap(x, "rad", c) for c in range(1, n_rad)]

    own = jnp.concatenate(jnp.split(trial_block.astype(BF16), n_rad), axis=2)[None]
    near0, far_own, diag0 = near_of(own), far_of(own), swap(own, "chan", 3)
    z1 = swap(own, "chan", 4)
    z_even = jnp.concatenate([swap(own, "chan", 4 * z) for z in range(2, nz, 2)])
    rows, ham, zhm, zl, dc, gram_t = pl.pallas_call(
        functools.partial(prepare_kernel, n_chan, n_rad),
        in_specs=[any_] * 5,
        out_specs=[whole] * 6,
        out_shape=[
            jax.ShapeDtypeStruct((ncoup, ch), jnp.int32),
            pltpu.VMEM(ham_blocks.shape, BF16),
            pltpu.VMEM((4 * k, lanes), BF16),
            pltpu.VMEM((2 * k, lanes), BF16),
            pltpu.VMEM((1, lanes), F32),
            pltpu.VMEM((k, 3 * k), F32),
        ],
        scratch_shapes=[
            pltpu.VMEM(trial_block.shape, F32),
            pltpu.VMEM(precond_diag.shape, F32),
            pltpu.VMEM((ncoup, ch), jnp.int32),
            pltpu.VMEM((stored_at.shape[0] // 128, 128), jnp.int32),
            pltpu.SemaphoreType.DMA((5,)),
        ],
        compiler_params=pltpu.CompilerParams(vmem_limit_bytes=VMEM_LIMIT),
        name="prepare",
    )(
        in_hbm(trial_block),
        in_hbm(precond_diag),
        in_hbm(partners.T),
        in_hbm(stored_at.reshape(-1, 128)),
        in_hbm(ham_blocks),
    )
    far_own, near0, z1, diag0, z_even, rows = barrier((far_own, near0, z1, diag0, z_even, rows))
    some, z_even, diag0 = barrier((jnp.concatenate([z1, z_even]), z_even, diag0))
    near1, far1 = near_of(some), far_of(some)
    z_odd = swap(z_even, "chan", 4)
    z_odd, far1, near1, diag0 = barrier((z_odd, far1, near1, diag0))
    early = in_cores(
        jnp.concatenate([own, z1, z_even, near0, far_own, diag0, near1, z_odd, far1])
    )
    near_odd = near_of(z_odd)
    diag_odd = jnp.concatenate([swap(diag0, "chan", 4 * z) for z in range(3, nz, 2)])
    far2 = far_of(jnp.concatenate([z_odd, near1]))
    table = pl.pallas_call(
        functools.partial(assemble_kernel, nz, share),
        in_specs=[whole] * n_rad,
        out_specs=whole,
        out_shape=pltpu.VMEM((n_chan * ch, k, splines), BF16),
        compiler_params=pltpu.CompilerParams(vmem_limit_bytes=VMEM_LIMIT),
        name="assemble",
    )(*[in_vmem(flat(x)) for x in early])
    near_odd, diag_odd, far2, table = barrier((near_odd, diag_odd, far2, table))
    last = [in_vmem(flat(x)) for x in in_cores(jnp.concatenate([near_odd, far2, diag_odd]))]

    az, sums, _ = pl.pallas_call(
        functools.partial(apply_kernel, nz, share),
        in_specs=[smem] + [whole] * (6 + n_rad),
        out_specs=[whole, whole, whole],
        out_shape=[
            pltpu.VMEM((2 * k, lanes), BF16),
            jax.ShapeDtypeStruct((k, 8 * k), F32),
            pltpu.VMEM(table.shape, BF16),
        ],
        input_output_aliases={2: 2},
        scratch_shapes=[pltpu.VMEM((k, lanes), F32)],
        compiler_params=pltpu.CompilerParams(vmem_limit_bytes=VMEM_LIMIT),
        name="apply",
    )(rows, in_vmem(ham), in_vmem(table), in_vmem(zhm), in_vmem(zl), in_vmem(dc), gram_t, *last)

    sums = gather_sums(sums)
    new_block, ritz = pl.pallas_call(
        functools.partial(finish_kernel, total),
        out_shape=[
            jax.ShapeDtypeStruct((ch, k, r), F32),
            jax.ShapeDtypeStruct((1, k), F32),
        ],
        compiler_params=pltpu.CompilerParams(vmem_limit_bytes=VMEM_LIMIT),
        name="finish",
    )(sums, in_vmem(az), in_vmem(zhm))
    return (new_block, ritz.reshape(k))


def solution(mesh):
    return jax.shard_map(
        body,
        mesh=mesh,
        in_specs=(
            P("chan", None, "rad"),
            P("chan", None, "rad", None),
            P("chan", None),
            P(),
            P("chan", "rad"),
        ),
        out_specs=(P("chan", None, "rad"), P()),
        check_vma=False,
    )
```
